32 devices in a mesh: dp: 2 (over z_hi), seq: 8 (over y, x, core), tensor: 2 (over z_lo).
Axes of the slice: x: 2, y: 2, z: 4 (z_hi: 2, z_lo: 2; z = z_hi * 2 + z_lo), core: 2. Of those that a mesh axis runs over, the one named last changes fastest.
Arguments:
- hidden_in: bfloat16 [4096, 2048], P(('dp', 'seq')), may hold values from -6 to 6
- doc_lengths: int32 [2, 2], P('dp'), may hold values from 1 to 2047, as said below
- attention_gain: float32 [2048], replicated, may hold values from 0.1 to 1.9
- query_weight: bfloat16 [2048, 2048], P(('dp', 'seq'), 'tensor'), may hold values from -0.125 to 0.125
- key_projection: bfloat16 [2048, 512], P(('dp', 'seq'), 'tensor'), may hold values from -0.125 to 0.125
- value_projection: bfloat16 [2048, 512], P(('dp', 'seq'), 'tensor'), may hold values from -0.125 to 0.125
- output_weight: bfloat16 [2048, 2048], P('tensor', ('dp', 'seq')), may hold values from -0.5 to 0.5
- query_down: bfloat16 [2048, 8], replicated, may hold values from -0.125 to 0.125
- query_up: bfloat16 [8, 2048], P(None, 'tensor'), may hold values from -2 to 2
- key_down: bfloat16 [2048, 8], replicated, may hold values from -0.125 to 0.125
- key_adapter_up: bfloat16 [8, 512], P(None, 'tensor'), may hold values from -2 to 2
- value_down: bfloat16 [2048, 8], replicated, may hold values from -0.125 to 0.125
- value_adapter_up: bfloat16 [8, 512], P(None, 'tensor'), may hold values from -2 to 2
- output_down: bfloat16 [2048, 8], P('tensor'), may hold values from -0.5 to 0.5
- output_up: bfloat16 [8, 2048], replicated, may hold values from -2 to 2
- query_feature_maps: bfloat16 [32, 64, 64], P('tensor'), may hold values from -0.75 to 0.75
- key_feature_maps: bfloat16 [32, 64, 64], P('tensor'), may hold values from -0.75 to 0.75
- feedforward_gain: float32 [2048], replicated, may hold values from 0.1 to 1.9
- gate_weight: bfloat16 [2048, 8192], P(('dp', 'seq'), 'tensor'), may hold values from -0.125 to 0.125
- up_weight: bfloat16 [2048, 8192], P(('dp', 'seq'), 'tensor'), may hold values from -0.125 to 0.125
- down_weight: bfloat16 [8192, 2048], P('tensor', ('dp', 'seq')), may hold values from -0.0625 to 0.0625
- block_cotangent: bfloat16 [4096, 2048], P(('dp', 'seq')), may hold values from -6 to 6
Outputs:
- block_output: bfloat16 [4096, 2048], P(('dp', 'seq'))
- input_grad: bfloat16 [4096, 2048], P(('dp', 'seq'))
- attention_gain_grad: float32 [2048], replicated
- query_weight_grad: float32 [2048, 2048], P(('dp', 'seq'), 'tensor')
- key_weight_grad: float32 [2048, 512], P(('dp', 'seq'), 'tensor')
- value_weight_grad: float32 [2048, 512], P(('dp', 'seq'), 'tensor')
- output_weight_grad: float32 [2048, 2048], P('tensor', ('dp', 'seq'))
- query_down_grad: float32 [2048, 8], replicated
- query_up_grad: float32 [8, 2048], P(None, 'tensor')
- key_down_grad: float32 [2048, 8], replicated
- key_up_grad: float32 [8, 512], P(None, 'tensor')
- value_down_grad: float32 [2048, 8], replicated
- value_up_grad: float32 [8, 512], P(None, 'tensor')
- output_down_grad: float32 [2048, 8], P('tensor')
- output_up_grad: float32 [8, 2048], replicated
- query_features_grad: float32 [32, 64, 64], P('tensor')
- key_features_grad: float32 [32, 64, 64], P('tensor')
- feedforward_gain_grad: float32 [2048], replicated
- gate_weight_grad: float32 [2048, 8192], P(('dp', 'seq'), 'tensor')
- up_weight_grad: float32 [2048, 8192], P(('dp', 'seq'), 'tensor')
- down_weight_grad: float32 [8192, 2048], P('tensor', ('dp', 'seq'))
The draws below stay inside these ranges and needn't reach their ends.
Inputs may be any that keep to these rules, and one draw needn't show every extreme that they name: `doc_lengths`: row g lists the lengths of group g's 2 documents in order; they sum to 2048, and one of them, the first or the second, is shorter than 256.
All inputs are finite; a program needn't handle non-finite values.
Results may differ from the reference program's by a relative error of at most 0.02.
The reference program's roundings to bfloat16 on the way count: a program that leaves them out, or rounds other values in their place, can miss the bound.
Values may be sent and summed in bfloat16 or wider, within the bound.
A program may use at most 320 MiB of HBM per device.

```python
import jax
import jax.numpy as jnp
import numpy as np
from jax import lax

MODEL_WIDTH = 2048
QUERY_HEADS = 32
KEY_VALUE_HEADS = 8
HEAD_SIZE = 64
FF = 8192
FEATURE_HALF = 64
ADAPTER_RANK = 8
SOFTMAX_KEYS = 64
TOK_DEV = 256
NDOC = 2
GROUPS = 2
GROUP_TOKENS = 2048
TOKENS = 4096


def draw_doc_lengths(key, part):
    short_piece = jax.random.randint(jax.random.fold_in(key, 21), (GROUPS,), 1, TOK_DEV, dtype=jnp.int32)
    picked = jax.random.randint(jax.random.fold_in(key, 22), (), 0, GROUPS, dtype=jnp.int32)
    group_index = jnp.arange(GROUPS, dtype=jnp.int32)
    short_piece = jnp.where(group_index == picked, 1, short_piece).astype(jnp.int32)
    long_piece = (GROUP_TOKENS - short_piece).astype(jnp.int32)
    flipped = jax.random.randint(jax.random.fold_in(key, 23), (GROUPS,), 0, 2, dtype=jnp.int32)
    first_doc = jnp.where(flipped == 1, short_piece, long_piece)
    second_doc = jnp.where(flipped == 1, long_piece, short_piece)
    return jnp.stack([first_doc, second_doc], axis=1).astype(jnp.int32)


def block_levels(rng, dims, shards, smallest, top_value):
    def one(dim, parts):
        draws = jax.random.uniform(jax.random.fold_in(jax.random.fold_in(rng, 6), dim), (parts,), jnp.float32, smallest / len(shards), top_value / len(shards))
        return jnp.repeat(jnp.exp(draws), dims[dim] // parts).reshape((-1,) + (1,) * (len(dims) - dim - 1))

    loudness = one(*shards[0])
    for cut in shards[1:]:
        loudness = loudness * one(*cut)
    return loudness


def noise(stream_key, dims, scale, reach, shards=(), kind=jnp.bfloat16):
    values = jax.random.normal(stream_key, dims, jnp.float32) * scale
    if len(shards) > 0:
        values = block_levels(stream_key, dims, shards, -0.22, 0.18) * values
    return jnp.clip(values, min=-reach, max=reach).astype(kind)


def setup_inputs(seed: int = 0) -> dict:
    seeds = jax.random.split(jax.random.key(seed), 23)
    hidden_in = noise(seeds[0], (TOKENS, MODEL_WIDTH), 1.0, 6.0, ((0, 16),))
    doc_lengths = draw_doc_lengths(jax.random.fold_in(seeds[22], 71), 0)
    attention_gain = jnp.clip(1.0 + 0.18 * jax.random.normal(seeds[2], (MODEL_WIDTH,), jnp.float32), 0.1, 1.9)
    query_weight = noise(seeds[3], (MODEL_WIDTH, QUERY_HEADS * HEAD_SIZE), MODEL_WIDTH ** -0.5, 0.125, ((0, 16), (1, 2)))
    key_projection = noise(seeds[4], (MODEL_WIDTH, KEY_VALUE_HEADS * HEAD_SIZE), MODEL_WIDTH ** -0.5, 0.125, ((0, 16), (1, 2)))
    value_projection = noise(seeds[5], (MODEL_WIDTH, KEY_VALUE_HEADS * HEAD_SIZE), MODEL_WIDTH ** -0.5, 0.125, ((0, 16), (1, 2)))
    output_weight = noise(seeds[6], (QUERY_HEADS * HEAD_SIZE, MODEL_WIDTH), (QUERY_HEADS * HEAD_SIZE // 16) ** -0.5, 0.5, ((0, 2), (1, 16)))
    query_down = noise(seeds[7], (MODEL_WIDTH, ADAPTER_RANK), MODEL_WIDTH ** -0.5, 0.125)
    query_up = noise(seeds[8], (ADAPTER_RANK, QUERY_HEADS * HEAD_SIZE), ADAPTER_RANK ** -0.5, 2.0, ((1, 2),))
    key_down = noise(seeds[9], (MODEL_WIDTH, ADAPTER_RANK), MODEL_WIDTH ** -0.5, 0.125)
    key_adapter_up = noise(seeds[10], (ADAPTER_RANK, KEY_VALUE_HEADS * HEAD_SIZE), ADAPTER_RANK ** -0.5, 2.0, ((1, 2),))
    value_down = noise(seeds[11], (MODEL_WIDTH, ADAPTER_RANK), MODEL_WIDTH ** -0.5, 0.125)
    value_adapter_up = noise(seeds[12], (ADAPTER_RANK, KEY_VALUE_HEADS * HEAD_SIZE), ADAPTER_RANK ** -0.5, 2.0, ((1, 2),))
    output_down = noise(seeds[13], (QUERY_HEADS * HEAD_SIZE, ADAPTER_RANK), (QUERY_HEADS * HEAD_SIZE // 16) ** -0.5, 0.5, ((0, 2),))
    output_up = noise(seeds[14], (ADAPTER_RANK, MODEL_WIDTH), ADAPTER_RANK ** -0.5, 2.0)
    query_feature_maps = noise(seeds[15], (QUERY_HEADS, HEAD_SIZE, FEATURE_HALF), HEAD_SIZE ** -0.5, 0.75, ((0, 2),))
    key_feature_maps = noise(seeds[16], (QUERY_HEADS, HEAD_SIZE, FEATURE_HALF), HEAD_SIZE ** -0.5, 0.75, ((0, 2),))
    feedforward_gain = jnp.clip(1.0 + 0.18 * jax.random.normal(seeds[17], (MODEL_WIDTH,), jnp.float32), 0.1, 1.9)
    gate_weight = noise(seeds[18], (MODEL_WIDTH, FF), MODEL_WIDTH ** -0.5, 0.125, ((0, 16), (1, 2)))
    up_weight = noise(seeds[19], (MODEL_WIDTH, FF), MODEL_WIDTH ** -0.5, 0.125, ((0, 16), (1, 2)))
    down_weight = noise(seeds[20], (FF, MODEL_WIDTH), FF ** -0.5, 0.0625, ((0, 2), (1, 16)))
    block_cotangent = noise(seeds[21], (TOKENS, MODEL_WIDTH), 1.0, 6.0, ((0, 16),))
    return dict(hidden_in=hidden_in, doc_lengths=doc_lengths, attention_gain=attention_gain, query_weight=query_weight, key_projection=key_projection, value_projection=value_projection, output_weight=output_weight, query_down=query_down, query_up=query_up, key_down=key_down, key_adapter_up=key_adapter_up, value_down=value_down, value_adapter_up=value_adapter_up, output_down=output_down, output_up=output_up, query_feature_maps=query_feature_maps, key_feature_maps=key_feature_maps, feedforward_gain=feedforward_gain, gate_weight=gate_weight, up_weight=up_weight, down_weight=down_weight, block_cotangent=block_cotangent)


EPS = 1e-05
HIGHEST = lax.Precision.HIGHEST

@jax.custom_vjp
def adapter_hidden(v):
    return lax.optimization_barrier(v.astype(jnp.bfloat16)).astype(jnp.float32)

@jax.custom_vjp
def adapter_hidden_gradient(v):
    return v

def low_keep(v):
    return (adapter_hidden(v), None)

def low_pass(kept, grad):
    return (grad,)

def back_keep(v):
    return (v, None)

def back_low(kept, grad):
    return (adapter_hidden(grad),)
adapter_hidden.defvjp(low_keep, low_pass)
adapter_hidden_gradient.defvjp(back_keep, back_low)

def frequencies(head_width):
    inverse = 1.0 / 500000.0 ** (np.arange(0, head_width, 2) / head_width)
    wavelen = 2.0 * np.pi / inverse
    smooth = (8192.0 / wavelen - 1.0) / 3.0
    blended = (1.0 - smooth) * inverse / 32.0 + smooth * inverse
    return np.where(wavelen > 8192.0, inverse / 32.0, np.where(wavelen < 2048.0, inverse, blended))

def rotation(positions, head_width):
    freq_table = jnp.asarray(frequencies(head_width), jnp.float32)
    turned = positions.astype(jnp.float32)[:, None] * freq_table[None, :]
    doubled = jnp.concatenate([turned, turned], axis=-1)
    return (jnp.cos(doubled), jnp.sin(doubled))

def apply_rotary(values, cosine_table, sine_table):
    half_width = values.shape[-1] // 2
    turned = jnp.concatenate([-values[..., half_width:], values[..., :half_width]], axis=-1)
    return values * cosine_table[:, None, :] + turned * sine_table[:, None, :]

def locate(places, lengths):
    doc_ends = jnp.cumsum(lengths).astype(jnp.int32)
    passed = places[:, None] >= doc_ends[None, :]
    segment = lax.optimization_barrier(jnp.sum(passed.astype(jnp.int32), axis=1)).astype(jnp.int32)
    doc_begin = lax.optimization_barrier(jnp.sum(jnp.where(passed, lengths[None, :], 0), axis=1)).astype(jnp.int32)
    return (jnp.where(places < 0, -1, segment).astype(jnp.int32), (places - doc_begin).astype(jnp.int32))

def norm_scale(inputs):
    return lax.rsqrt(lax.optimization_barrier(jnp.mean(inputs * inputs, axis=-1, keepdims=True)) + EPS)

def matrix_multiply(left, right):
    return jnp.dot(left, right, precision=HIGHEST, preferred_element_type=jnp.float32)

def feature_map(mixed_in):
    return jnp.concatenate([jax.nn.softmax(mixed_in, axis=-1), jax.nn.softmax(-mixed_in, axis=-1)], axis=-1)

def reference(hidden_in, doc_lengths, attention_gain, query_weight, key_projection, value_projection, output_weight, query_down, query_up, key_down, key_adapter_up, value_down, value_adapter_up, output_down, output_up, query_feature_maps, key_feature_maps, feedforward_gain, gate_weight, up_weight, down_weight, block_cotangent):
    token_row_count = TOK_DEV
    block_count = TOKENS // token_row_count
    heads_per_group = QUERY_HEADS // KEY_VALUE_HEADS
    score_scale = HEAD_SIZE ** (-0.5)
    seg_parts = []
    pos_parts = []
    for group_at in range(GROUPS):
        places = jnp.arange(GROUP_TOKENS, dtype=jnp.int32)
        segment, position = locate(places, doc_lengths[group_at])
        seg_parts.append((segment + group_at * NDOC).astype(jnp.int32))
        pos_parts.append(position)
    seg_all = jnp.concatenate(seg_parts)
    pos_all = jnp.concatenate(pos_parts)
    padded = jnp.concatenate([jnp.full((SOFTMAX_KEYS,), -1, jnp.int32), seg_all])
    block_start = jnp.arange(block_count, dtype=jnp.int32) * token_row_count
    rim_seg = padded[block_start[:, None] + jnp.arange(SOFTMAX_KEYS, dtype=jnp.int32)[None, :]]
    seg_before = padded[block_start + SOFTMAX_KEYS - 1]
    row_at = jnp.arange(token_row_count)[:, None]
    key_at = jnp.arange(token_row_count + SOFTMAX_KEYS)[None, :]

    def forward(hidden, attention_gain, query_weight, key_projection, value_projection, output_weight, query_down, query_up, key_down, key_adapter_up, value_down, value_adapter_up, output_down, output_up, query_feature_maps, key_feature_maps, feedforward_gain, gate_weight, up_weight, down_weight):
        query_feature_table = query_feature_maps.reshape(KEY_VALUE_HEADS, heads_per_group, HEAD_SIZE, FEATURE_HALF)
        key_feature_table = key_feature_maps.reshape(KEY_VALUE_HEADS, heads_per_group, HEAD_SIZE, FEATURE_HALF)

        def one_block(carried, inputs):
            rim_keys, rim_values, state_kv, state_norm = carried
            rows_in, seg_rows, seg_rim, pos_rows, seg_first = inputs
            cosine_table, sine_table = rotation(pos_rows, HEAD_SIZE)
            normalized_input = adapter_hidden(rows_in * norm_scale(rows_in) * attention_gain)
            low_q = adapter_hidden(matrix_multiply(normalized_input, query_down))
            low_k = adapter_hidden(matrix_multiply(normalized_input, key_down))
            value_adapter_hidden = adapter_hidden(matrix_multiply(normalized_input, value_down))
            query_before_rotation = adapter_hidden_gradient(matrix_multiply(normalized_input, query_weight) + matrix_multiply(low_q, query_up))
            query_heads_rows = adapter_hidden(apply_rotary(query_before_rotation.reshape(token_row_count, QUERY_HEADS, HEAD_SIZE), cosine_table, sine_table)).reshape(token_row_count, KEY_VALUE_HEADS, heads_per_group, HEAD_SIZE)
            key_before_rotation = adapter_hidden_gradient(matrix_multiply(normalized_input, key_projection) + matrix_multiply(low_k, key_adapter_up))
            projected_keys = adapter_hidden(apply_rotary(key_before_rotation.reshape(token_row_count, KEY_VALUE_HEADS, HEAD_SIZE), cosine_table, sine_table))
            projected_values = adapter_hidden(adapter_hidden_gradient(matrix_multiply(normalized_input, value_projection) + matrix_multiply(value_adapter_hidden, value_adapter_up))).reshape(token_row_count, KEY_VALUE_HEADS, HEAD_SIZE)
            key_ext = jnp.concatenate([rim_keys, projected_keys], axis=0)
            value_ext = jnp.concatenate([rim_values, projected_values], axis=0)
            seg_ext = jnp.concatenate([seg_rim, seg_rows])
            phi_q = adapter_hidden(feature_map(adapter_hidden_gradient(jnp.einsum('tkgd,kgdf->tkgf', query_heads_rows, query_feature_table, precision=HIGHEST))))
            phi_k = adapter_hidden(feature_map(adapter_hidden_gradient(jnp.einsum('ekd,kgdf->ekgf', key_ext, key_feature_table, precision=HIGHEST))))
            raw_scores = adapter_hidden_gradient(jnp.einsum('tkgd,ekd->kgte', query_heads_rows, key_ext, precision=HIGHEST))
            linear = adapter_hidden_gradient(jnp.einsum('tkgf,ekgf->kgte', phi_q, phi_k, precision=HIGHEST))
            same_doc = seg_rows[:, None] == seg_ext[None, :]
            window = same_doc & (key_at > row_at) & (key_at <= row_at + SOFTMAX_KEYS)
            earlier = same_doc & (key_at <= row_at)
            window_exp = jnp.where(window, jnp.exp(jnp.where(window, score_scale * raw_scores, 0.0)), 0.0)
            linear_old = jnp.where(earlier, linear, 0.0)
            continuing = (seg_rows == seg_first).astype(jnp.float32)
            numerator = jnp.einsum('kgte,ekd->tkgd', adapter_hidden(window_exp), value_ext, precision=HIGHEST) + jnp.einsum('kgte,ekd->tkgd', linear_old, value_ext, precision=HIGHEST) + continuing[:, None, None, None] * jnp.einsum('tkgf,kgfd->tkgd', phi_q, state_kv, precision=HIGHEST)
            denominator = lax.optimization_barrier(jnp.sum(window_exp + linear_old, axis=-1)).transpose(2, 0, 1) + continuing[:, None, None] * jnp.einsum('tkgf,kgf->tkg', phi_q, state_norm, precision=HIGHEST)
            attended = adapter_hidden(adapter_hidden_gradient(numerator) / denominator[..., None]).reshape(token_row_count, QUERY_HEADS * HEAD_SIZE)
            seg_last = seg_rows[token_row_count - 1]
            carry_mask = ((jnp.arange(token_row_count + SOFTMAX_KEYS) < token_row_count) & (seg_ext == seg_last)).astype(jnp.float32)
            masked_phi = phi_k * carry_mask[:, None, None, None]
            resets = (seg_last != seg_first).astype(jnp.float32)
            new_kv = (1.0 - resets) * state_kv + jnp.einsum('ekgf,ekd->kgfd', masked_phi, value_ext, precision=HIGHEST)
            new_norm = (1.0 - resets) * state_norm + lax.optimization_barrier(jnp.sum(masked_phi, axis=0))
            low_mid = adapter_hidden(matrix_multiply(attended, output_down))
            residual = rows_in + adapter_hidden_gradient(matrix_multiply(attended, output_weight) + matrix_multiply(low_mid, output_up))
            normed_ff = adapter_hidden(residual * norm_scale(residual) * feedforward_gain)
            gate_act = adapter_hidden_gradient(matrix_multiply(normed_ff, gate_weight))
            up_act = adapter_hidden_gradient(matrix_multiply(normed_ff, up_weight))
            hidden_units = adapter_hidden(jax.nn.silu(gate_act) * up_act)
            out_rows = adapter_hidden(residual + matrix_multiply(hidden_units, down_weight))
            next_carry = (projected_keys[token_row_count - SOFTMAX_KEYS:], projected_values[token_row_count - SOFTMAX_KEYS:], new_kv, new_norm)
            return (next_carry, out_rows)
        block_step = jax.checkpoint(one_block)
        initial_carry = (jnp.zeros((SOFTMAX_KEYS, KEY_VALUE_HEADS, HEAD_SIZE), jnp.float32), jnp.zeros((SOFTMAX_KEYS, KEY_VALUE_HEADS, HEAD_SIZE), jnp.float32), jnp.zeros((KEY_VALUE_HEADS, heads_per_group, 2 * FEATURE_HALF, HEAD_SIZE), jnp.float32), jnp.zeros((KEY_VALUE_HEADS, heads_per_group, 2 * FEATURE_HALF), jnp.float32))
        block_inputs = (hidden.reshape(block_count, token_row_count, MODEL_WIDTH), seg_all.reshape(block_count, token_row_count), rim_seg, pos_all.reshape(block_count, token_row_count), seg_before)
        final_carry, out_blocks = lax.scan(block_step, initial_carry, block_inputs)
        return out_blocks.reshape(TOKENS, MODEL_WIDTH)
    floats = tuple((argument.astype(jnp.float32) for argument in (hidden_in, attention_gain, query_weight, key_projection, value_projection, output_weight, query_down, query_up, key_down, key_adapter_up, value_down, value_adapter_up, output_down, output_up, query_feature_maps, key_feature_maps, feedforward_gain, gate_weight, up_weight, down_weight)))
    output, pullback = jax.vjp(forward, *floats)
    gradients = pullback(block_cotangent.astype(jnp.float32))
    return (output.astype(jnp.bfloat16), gradients[0].astype(jnp.bfloat16), gradients[1], gradients[2], gradients[3], gradients[4], gradients[5], gradients[6], gradients[7], gradients[8], gradients[9], gradients[10], gradients[11], gradients[12], gradients[13], gradients[14], gradients[15], gradients[16], gradients[17], gradients[18], gradients[19])
```

```python
import functools

import jax
import jax.numpy as jnp
import numpy as np
from jax import lax
from jax.experimental import pallas as pl
from jax.experimental.pallas import tpu as pltpu
from jax.sharding import Mesh
from jax.sharding import PartitionSpec as P

HEAD_SIZE = 64
FEATURE_HALF = 64
SOFTMAX_KEYS = 64
CORES = 2


EPS = 1e-05
FLOAT = jnp.float32
BFLOAT = jnp.bfloat16


def swap(value, axis, mask=1):
    count = lax.axis_size(axis)
    return lax.ppermute(value, axis, [(source, source ^ mask) for source in range(count)])


def bit(axis, mask=1):
    return (lax.axis_index(axis) // mask) % 2


def ordered(which, mine, other, dim):
    return jnp.where(
        which == 0,
        jnp.concatenate([mine, other], axis=dim),
        jnp.concatenate([other, mine], axis=dim),
    )


def take(value, index, dim):
    return lax.dynamic_index_in_dim(value, index, dim, keepdims=True)


def cube_dims():
    chips = lax.axis_size("chip")
    masks = []
    mask = chips // 2
    while mask >= 1:
        masks.append(("chip", mask))
        mask //= 2
    return [("dp", 1)] + masks


def cube_orders():
    count = len(cube_dims())
    inner = list(range(1, count))
    return ([0] + inner, [0] + inner[::-1])


def gather_blocks(block, order):
    dims = cube_dims()
    value = block.reshape((1,) * len(dims) + block.shape)
    for dim in order:
        axis, mask = dims[dim]
        value = ordered(bit(axis, mask), value, swap(value, axis, mask), dim)
    return value.reshape((-1,) + block.shape)


def scatter_blocks(value, order):
    dims = cube_dims()
    block = value.shape[1:]
    value = value.reshape((2,) * len(dims) + block)
    for dim in order:
        axis, mask = dims[dim]
        which = bit(axis, mask)
        send = take(value, 1 - which, dim).astype(BFLOAT)
        value = take(value, which, dim).astype(FLOAT) + swap(send, axis, mask).astype(FLOAT)
    return value.reshape(block)


def token_orders():
    masks = [dim for dim in cube_dims() if dim[0] == "chip"]
    return (masks[::-1], masks)


def gather_tokens(rows, order):
    for axis, mask in order:
        rows = jnp.concatenate([rows, swap(rows, axis, mask)], axis=0)
    return rows, swap(rows, "core")


def scatter_tokens(rows, sibling_rows, order):
    rows = rows.astype(FLOAT) + swap(sibling_rows, "core").astype(FLOAT)
    for axis, mask in order[::-1]:
        half = rows.shape[0] // 2
        send = rows[half:].astype(BFLOAT)
        rows = rows[:half] + swap(send, axis, mask).astype(FLOAT)
    return rows


def pair_sum(value, axis, mask=1):
    sent = value.astype(BFLOAT)
    return sent.astype(FLOAT) + swap(sent, axis, mask).astype(FLOAT)


def frequencies(head_width):
    inverse = 1.0 / 500000.0 ** (np.arange(0, head_width, 2) / head_width)
    wavelen = 2.0 * np.pi / inverse
    smooth = (8192.0 / wavelen - 1.0) / 3.0
    blended = (1.0 - smooth) * inverse / 32.0 + smooth * inverse
    return np.where(wavelen > 8192.0, inverse / 32.0, np.where(wavelen < 2048.0, inverse, blended))


def rotation(positions, head_width):
    freq_table = jnp.asarray(frequencies(head_width), FLOAT)
    turned = positions.astype(FLOAT)[:, None] * freq_table[None, :]
    cosine, sine = jnp.cos(turned), jnp.sin(turned)
    return (
        jnp.concatenate([cosine, cosine], axis=-1),
        jnp.concatenate([-sine, sine], axis=-1),
    )


def turn(values):
    width = values.shape[1]
    half = HEAD_SIZE // 2
    first = (lax.broadcasted_iota(jnp.int32, (1, width), 1) % HEAD_SIZE) < half
    return jnp.where(first, jnp.roll(values, -half, axis=1), jnp.roll(values, half, axis=1))


def spread(table, width):
    return jnp.tile(table, (1, width // table.shape[1]))


def apply_rotary(values, cosine_table, sine_table):
    width = values.shape[1]
    return values * spread(cosine_table, width) + turn(values) * spread(sine_table, width)


def rotate_back(grad_in, cosine_table, sine_table):
    width = grad_in.shape[1]
    return grad_in * spread(cosine_table, width) - turn(grad_in) * spread(sine_table, width)


def locate(places, lengths):
    doc_ends = jnp.cumsum(lengths)
    passed = places[:, None] >= doc_ends[None, :]
    segment = jnp.sum(passed.astype(jnp.int32), axis=1)
    doc_begin = jnp.sum(jnp.where(passed, lengths[None, :], 0), axis=1)
    return (jnp.where(places < 0, -1, segment), places - doc_begin)


def norm_scale(inputs):
    return lax.rsqrt(jnp.mean(inputs * inputs, axis=-1, keepdims=True) + EPS)


def norm_back(inputs, gain_vec, grad_normed):
    scale_vec = norm_scale(inputs)
    weighted = grad_normed * gain_vec
    grad_inputs = scale_vec * weighted - inputs * scale_vec * scale_vec * scale_vec * jnp.mean(
        weighted * inputs, axis=-1, keepdims=True
    )
    return (grad_inputs, jnp.sum(grad_normed * inputs * scale_vec, axis=0))


def product(left, right):
    return jnp.dot(left, right, preferred_element_type=FLOAT)


def product_t(left, right):
    return lax.dot_general(left, right, (((1,), (1,)), ((), ())), preferred_element_type=FLOAT)


def t_product(left, right):
    return lax.dot_general(left, right, (((0,), (0,)), ((), ())), preferred_element_type=FLOAT)


def dot(left, right):
    return lax.dot_general(left, right, (((1,), (0,)), ((), ())), preferred_element_type=FLOAT)


def lanes(shape):
    return lax.broadcasted_iota(jnp.int32, shape, 1)


def half_sums(rows):
    first = lax.broadcasted_iota(jnp.int32, (128, 128), 0) < FEATURE_HALF
    ones = jnp.where(first == (lanes((128, 128)) < FEATURE_HALF), 1.0, 0.0).astype(BFLOAT)
    return dot(rows, ones)


def two_softmax(mixed):
    low = lanes(mixed.shape) < FEATURE_HALF
    top = jnp.max(jnp.where(low, mixed, -jnp.inf), axis=1, keepdims=True)
    top_other = jnp.max(jnp.where(low, -jnp.inf, mixed), axis=1, keepdims=True)
    raised = jnp.exp(mixed - jnp.where(low, top, top_other))
    return (raised / half_sums(raised.astype(BFLOAT))).astype(BFLOAT)


def phi_kernel(group, q_ref, k_ref, vm_ref, fq_ref, fk_ref, phi_q_ref, phi_k_ref, state_ref):
    keys = k_ref[0]
    masked = vm_ref[0]
    for head in range(group):
        rows = q_ref[:, head * HEAD_SIZE : (head + 1) * HEAD_SIZE]
        phi_q_ref[head] = two_softmax(dot(rows, fq_ref[head]))
        phi_k = two_softmax(dot(keys, fk_ref[head]))
        phi_k_ref[head] = phi_k
        state_ref[head] = t_product(masked, phi_k).astype(BFLOAT)


def tile_masks(seg_q, seg_k, at):
    width = at + 256
    same = seg_q == seg_k[:, :width]
    row = lax.broadcasted_iota(jnp.int32, (128, 256), 0)
    col = lanes((128, 256))
    earlier = col <= row + SOFTMAX_KEYS
    window = (col > row + SOFTMAX_KEYS) & (col <= row + 128) & same[:, at:]
    return same[:, :at], window, earlier & same[:, at:]


def tile_weights(rows, phi_rows, k_ref, phi_k, at, masks):
    far, window, earlier = masks
    scale = HEAD_SIZE ** (-0.5)
    raw = product_t(rows, k_ref[0, at : at + 256])
    window_exp = jnp.where(window, jnp.exp(jnp.where(window, scale * raw, 0.0)), 0.0)
    linear = product_t(phi_rows, phi_k[: at + 256])
    near = jnp.where(earlier, linear[:, at:], window_exp)
    if at == 0:
        return window_exp, near.astype(BFLOAT)
    return window_exp, jnp.concatenate(
        [jnp.where(far, linear[:, :at], 0.0), near], axis=1
    ).astype(BFLOAT)


def intra_kernel(group, q_ref, k_ref, v_ref, phi_q_ref, phi_k_ref, seg_q_ref, seg_k_ref, num_ref):
    for at in range(0, q_ref.shape[0], 128):
        masks = tile_masks(seg_q_ref[at : at + 128], seg_k_ref[...], at)
        for head in range(group):
            rows = q_ref[at : at + 128, head * HEAD_SIZE : (head + 1) * HEAD_SIZE]
            weights = tile_weights(
                rows, phi_q_ref[head, at : at + 128], k_ref, phi_k_ref.at[head], at, masks
            )[1]
            num_ref[head, at : at + 128] = dot(weights, v_ref[0, : at + 256])


def finish_kernel(group, num_ref, phi_q_ref, state_ref, cont_ref, att_ref, den_ref):
    cont = cont_ref[...]
    den = jnp.zeros(den_ref.shape[1:], FLOAT)
    for head in range(group):
        total = num_ref[head] + cont * product_t(phi_q_ref[head], state_ref[head])
        below = total[:, HEAD_SIZE : HEAD_SIZE + 1]
        att_ref[:, head * HEAD_SIZE : (head + 1) * HEAD_SIZE] = (
            total[:, :HEAD_SIZE] / below
        ).astype(BFLOAT)
        den = jnp.where(lanes(den.shape) == head, below, den)
    den_ref[0] = den


def grad_numer_kernel(group, da_ref, att_ref, den_ref, phi_q_ref, cont_ref, dn_ref, ds_ref):
    cont = cont_ref[...]
    for head in range(group):
        cols = slice(head * HEAD_SIZE, (head + 1) * HEAD_SIZE)
        numer = da_ref[:, cols] / den_ref[0][:, head : head + 1]
        denom = -jnp.sum(numer * att_ref[:, cols].astype(FLOAT), axis=1, keepdims=True)
        high = denom.astype(BFLOAT).astype(FLOAT)
        wide = jnp.concatenate([numer, jnp.zeros_like(numer)], axis=1)
        lane = lanes(wide.shape)
        wide = jnp.where(lane == HEAD_SIZE, high, wide)
        wide = jnp.where(lane == HEAD_SIZE + 1, denom - high, wide)
        dn_ref[head] = wide.astype(BFLOAT)
        state = t_product((wide * cont).astype(BFLOAT), phi_q_ref[head])
        row = lax.broadcasted_iota(jnp.int32, state.shape, 0)
        both = state[HEAD_SIZE : HEAD_SIZE + 1] + state[HEAD_SIZE + 1 : HEAD_SIZE + 2]
        state = jnp.where(row == HEAD_SIZE, both, jnp.where(row > HEAD_SIZE, 0.0, state))
        ds_ref[head] = state.astype(BFLOAT)


def intra_back_kernel(
    group, q_ref, k_ref, v_ref, phi_q_ref, phi_k_ref, dn_ref, seg_q_ref, seg_k_ref,
    dq_ref, dk_ref, dv_ref, dphi_q_ref, dphi_k_ref,
):
    scale = HEAD_SIZE ** (-0.5)
    dk_ref[...] = jnp.zeros(dk_ref.shape, FLOAT)
    dv_ref[...] = jnp.zeros(dv_ref.shape, FLOAT)
    dphi_k_ref[...] = jnp.zeros(dphi_k_ref.shape, FLOAT)
    for at in range(0, q_ref.shape[0], 128):
        masks = tile_masks(seg_q_ref[at : at + 128], seg_k_ref[...], at)
        tile = slice(at, at + 128)
        width = at + 256
        for head in range(group):
            cols = slice(head * HEAD_SIZE, (head + 1) * HEAD_SIZE)
            rows = q_ref[tile, cols]
            phi_rows = phi_q_ref[head, tile]
            numer = dn_ref[head, tile]
            window_exp, weights = tile_weights(
                rows, phi_rows, k_ref, phi_k_ref.at[head], at, masks
            )
            grad = product_t(numer, v_ref[0, :width])
            near = grad[:, at:]
            grad_raw = (scale * near * window_exp).astype(BFLOAT)
            grad_linear = jnp.where(masks[2], near, 0.0)
            if at > 0:
                grad_linear = jnp.concatenate(
                    [jnp.where(masks[0], grad[:, :at], 0.0), grad_linear], axis=1
                )
            grad_linear = grad_linear.astype(BFLOAT)
            dv_ref[0, :width] += t_product(weights, numer)
            dphi_q_ref[head, tile] = dot(grad_linear, phi_k_ref[head, :width])
            dphi_k_ref[head, :width] += t_product(grad_linear, phi_rows)
            dq_ref[tile, cols] = dot(grad_raw, k_ref[0, at:width])
            dk_ref[0, at:width] += t_product(grad_raw, rows)


def softmax_back(phi, grad):
    wide = phi.astype(FLOAT)
    terms = grad * wide
    high = terms.astype(BFLOAT)
    low = (terms - high.astype(FLOAT)).astype(BFLOAT)
    mean = (half_sums(high) + half_sums(low)) / half_sums(phi)
    return (wide * (grad - mean)).astype(BFLOAT)


def features_back_kernel(
    group, q_ref, k_ref, v_ref, phi_q_ref, phi_k_ref, dn_ref, fq_ref, fk_ref, state_ref, ds_ref,
    cont_ref, carry_ref, dq_in, dk_in, dv_in, dphi_q_ref, dphi_k_ref,
    dq_ref, dk_ref, dv_ref, gq_ref, gk_ref,
):
    cont = cont_ref[...]
    carry = carry_ref[...]
    keys = k_ref[0]
    dk = dk_in[0]
    dv = dv_in[0]
    for head in range(group):
        cols = slice(head * HEAD_SIZE, (head + 1) * HEAD_SIZE)
        grad_state = ds_ref[head]
        phi_k = phi_k_ref[head]
        grad_q = dphi_q_ref[head] + cont * dot(dn_ref[head], state_ref[head])
        grad_k = dphi_k_ref[head] + carry * dot(v_ref[0], grad_state)
        dv = dv + carry * product_t(phi_k, grad_state)
        mixed_q = softmax_back(phi_q_ref[head], grad_q)
        mixed_k = softmax_back(phi_k, grad_k)
        dq_ref[:, cols] = dq_in[:, cols] + product_t(mixed_q, fq_ref[head])
        dk = dk + product_t(mixed_k, fk_ref[head])
        gq_ref[head] = t_product(q_ref[:, cols], mixed_q)
        gk_ref[head] = t_product(keys, mixed_k)
    dk_ref[0] = dk
    dv_ref[0] = dv


def feed_kernel(x_ref, c_ref, gate_ref, up_ref, down_ref, hid_ref, dg_ref, du_ref, out_ref, back_ref):
    rows = x_ref[...]
    gate = dot(rows, gate_ref[...])
    up = dot(rows, up_ref[...])
    grad = product_t(c_ref[...], down_ref[...])
    sigmoid = 1.0 / (1.0 + jnp.exp(-gate))
    silu = gate * sigmoid
    hidden = (silu * up).astype(BFLOAT)
    grad_gate = (grad * up * (sigmoid + silu * (1.0 - sigmoid))).astype(BFLOAT)
    grad_up = (grad * silu).astype(BFLOAT)
    hid_ref[...] = hidden
    dg_ref[...] = grad_gate
    du_ref[...] = grad_up
    back_ref[...] = (product_t(grad_gate, gate_ref[...]) + product_t(grad_up, up_ref[...])).astype(BFLOAT)
    out_ref[...] = dot(hidden, down_ref[...]).astype(BFLOAT)


def feed(rows, cotangent, gate, up, down):
    count, model = rows.shape
    units = gate.shape[1]
    tile = min(256, count)

    def tiled(width):
        return pl.BlockSpec((tile, width), lambda at: (at, 0))

    def whole(shape):
        return pl.BlockSpec(shape, lambda at: (0, 0))

    return pl.pallas_call(
        feed_kernel,
        grid=(count // tile,),
        in_specs=[tiled(model), tiled(model), whole(gate.shape), whole(up.shape), whole(down.shape)],
        out_specs=[tiled(units)] * 3 + [tiled(model)] * 2,
        out_shape=[jax.ShapeDtypeStruct((count, units), BFLOAT)] * 3
        + [jax.ShapeDtypeStruct((count, model), BFLOAT)] * 2,
        compiler_params=pltpu.CompilerParams(vmem_limit_bytes=56 * 1024 * 1024),
        cost_estimate=pl.CostEstimate(
            flops=12 * count * model * units,
            bytes_accessed=8 * count * model + 6 * model * units,
            transcendentals=count * units,
        ),
    )(rows, cotangent, gate, up, down)


def tie(first, second):
    return lax.optimization_barrier((first, second))


def heads_call(kernel, kv_heads, group, args, outs, flops):
    def spec(shape, kind):
        if kind == "cols":
            return pl.BlockSpec((shape[0], shape[1] // kv_heads), lambda at: (0, at))
        if kind == "all":
            return pl.BlockSpec(shape, lambda at: (0,) * len(shape))
        return pl.BlockSpec((shape[0] // kv_heads,) + shape[1:], lambda at: (at, 0, 0))

    moved = sum(np.prod(value.shape) * 2 for value, _ in args) + sum(np.prod(s) * 3 for s, _, _ in outs)
    return pl.pallas_call(
        functools.partial(kernel, group),
        grid=(kv_heads,),
        in_specs=[spec(value.shape, kind) for value, kind in args],
        out_specs=[spec(shape, kind) for shape, _, kind in outs],
        out_shape=[jax.ShapeDtypeStruct(shape, dtype) for shape, dtype, _ in outs],
        compiler_params=pltpu.CompilerParams(vmem_limit_bytes=48 * 1024 * 1024),
        cost_estimate=pl.CostEstimate(flops=int(flops), bytes_accessed=int(moved), transcendentals=0),
    )(*[value for value, _ in args])


def carried(value, coefs):
    count = lax.axis_size("chip")
    me = lax.axis_index("chip")
    sent = value[:, : HEAD_SIZE + 16]
    total = jnp.zeros(sent.shape, FLOAT)
    for step in range(1, count):
        total = total + coefs[me ^ step] * swap(sent, "chip", step).astype(FLOAT)
    return jnp.pad(total.astype(BFLOAT), ((0, 0), (0, value.shape[1] - sent.shape[1]), (0, 0)))


def carry_coefs(lengths, tokens):
    count = lax.axis_size("chip")
    me = lax.axis_index("chip")
    starts = jnp.arange(count, dtype=jnp.int32) * tokens
    open_chip = locate(starts - 1, lengths)[0] == locate(starts + tokens - 1, lengths)[0]
    source = jnp.arange(count)[:, None]
    between = jnp.arange(count)[None, :]
    after = (between > source) & (between < me)
    before = (between < source) & (between > me)
    forward = jnp.all(open_chip[None, :] | ~after, axis=1) & (source[:, 0] < me)
    backward = jnp.all(open_chip[None, :] | ~before, axis=1) & (source[:, 0] > me)
    return forward.astype(FLOAT), backward.astype(FLOAT)


def on_device(
    hidden_in,
    doc_lengths,
    attention_gain,
    query_weight,
    key_projection,
    value_projection,
    output_weight,
    query_down,
    query_up,
    key_down,
    key_adapter_up,
    value_down,
    value_adapter_up,
    output_down,
    output_up,
    query_feature_maps,
    key_feature_maps,
    feedforward_gain,
    gate_weight,
    up_weight,
    down_weight,
    block_cotangent,
):
    own_rows, model = hidden_in.shape
    tokens = own_rows * CORES
    core = lax.axis_index("core")
    chip = lax.axis_index("chip")
    chips = lax.axis_size("chip")
    heads = query_feature_maps.shape[0] // CORES
    kv_heads = key_projection.shape[1] // HEAD_SIZE // CORES
    group = heads // kv_heads
    q_width = heads * HEAD_SIZE
    kv_width = kv_heads * HEAD_SIZE
    rank = query_down.shape[1]
    ff_axes = ("chip", "core")

    def own_cols(value, width, which):
        return lax.dynamic_slice_in_dim(value, which * width, width, 1)

    def own_heads(value, count, which):
        return lax.dynamic_slice_in_dim(value, which * count, count, 0)

    def qkv_cols(which):
        return jnp.concatenate(
            [
                own_cols(query_weight, q_width, which),
                own_cols(key_projection, kv_width, which),
                own_cols(value_projection, kv_width, which),
            ],
            axis=1,
        )

    qkv_block = ordered(core, qkv_cols(core), swap(qkv_cols(1 - core), "core"), 0)
    out_mine = own_heads(output_weight, q_width, core)[None]
    out_block = ordered(core, out_mine, swap(own_heads(output_weight, q_width, 1 - core)[None], "core"), 0)
    orders = cube_orders()
    qkv_width = q_width + 2 * kv_width

    def gather_two(block, dim):
        parts = jnp.split(block, 2, axis=dim)
        return [gather_blocks(part, order) for part, order in zip(parts, orders)]

    qkv_parts = gather_two(qkv_block, 1)
    full_qkv = jnp.concatenate([part.reshape(model, qkv_width // 2) for part in qkv_parts], axis=1)
    out_parts = gather_two(out_block, 1)
    full_out = jnp.concatenate(
        [part.transpose(2, 0, 1, 3).reshape(q_width // 2, model) for part in out_parts], axis=0
    )

    t_orders = token_orders()

    def gather_rows(rows):
        return [gather_tokens(part, order) for part, order in zip(jnp.split(rows, 2, axis=0), t_orders)]

    dp_at = lax.axis_index("dp")

    def ff_weight(weight, split_dim):
        both = ordered(dp_at, weight[None], swap(weight, "dp")[None], 0)
        mine = lax.all_to_all(both, ff_axes, split_dim + 1, 2 - split_dim, tiled=True)
        return mine

    full_gate = ff_weight(gate_weight, 1).reshape(model, -1)
    full_up = ff_weight(up_weight, 1).reshape(model, -1)
    down_both = ff_weight(down_weight, 0)
    full_down = jnp.concatenate([down_both[0], down_both[1]], axis=1)
    cotangents = gather_rows(block_cotangent)

    first_row = chip * tokens
    lengths = doc_lengths[0]
    seg_rows, pos_rows = locate(first_row + jnp.arange(tokens, dtype=jnp.int32), lengths)
    seg_rim = locate(first_row - SOFTMAX_KEYS + jnp.arange(SOFTMAX_KEYS, dtype=jnp.int32), lengths)[
        0
    ]
    seg_first = locate(jnp.reshape(first_row - 1, (1,)), lengths)[0][0]
    gap = 128 - SOFTMAX_KEYS
    seg_ext = jnp.concatenate([jnp.full((gap,), -2, jnp.int32), seg_rim, seg_rows])
    seg_last = seg_rows[tokens - 1]
    continuing = (seg_rows == seg_first).astype(FLOAT)[:, None]
    carry = ((jnp.arange(tokens + 128) < tokens + gap) & (seg_ext == seg_last)).astype(FLOAT)[:, None]
    seg_column, seg_line = seg_rows[:, None], seg_ext[None, :]
    forward_coefs, backward_coefs = carry_coefs(lengths, tokens)
    cosine_table, sine_table = rotation(pos_rows, HEAD_SIZE)
    query_table = own_heads(query_feature_maps, heads, core)
    key_table = own_heads(key_feature_maps, heads, core)
    query_table = jnp.concatenate([query_table, -query_table], axis=2)
    key_table = jnp.concatenate([key_table, -key_table], axis=2)
    downs = jnp.concatenate([query_down, key_down, value_down], axis=1)
    own_query_up = own_cols(query_up, q_width, core)
    own_key_up = own_cols(key_adapter_up, kv_width, core)
    own_value_up = own_cols(value_adapter_up, kv_width, core)
    own_output_down = own_heads(output_down, q_width, core)
    pad = 128 - 3 * rank
    ups = jnp.concatenate(
        [
            jnp.pad(own_query_up, ((0, 0), (0, 2 * kv_width))),
            jnp.pad(own_key_up, ((0, 0), (q_width, kv_width))),
            jnp.pad(own_value_up, ((0, 0), (q_width + kv_width, 0))),
        ],
        axis=0,
    )

    hidden_chip = ordered(core, hidden_in, swap(hidden_in, "core"), 0)
    hidden32 = hidden_chip.astype(FLOAT)
    normed = (hidden32 * norm_scale(hidden32) * attention_gain).astype(BFLOAT)
    low_rank = product(normed, downs).astype(BFLOAT)
    pre = product(normed, full_qkv) + product(low_rank, ups)
    queries = apply_rotary(pre[:, :q_width], cosine_table, sine_table).astype(BFLOAT)
    keys = apply_rotary(pre[:, q_width : q_width + kv_width], cosine_table, sine_table).astype(BFLOAT)
    values = pre[:, q_width + kv_width :].astype(BFLOAT)
    rim = lax.ppermute(
        jnp.concatenate([keys[tokens - SOFTMAX_KEYS :], values[tokens - SOFTMAX_KEYS :]], axis=1),
        "chip",
        [(source, source + 1) for source in range(chips - 1)],
    )
    kv_ext = jnp.concatenate(
        [jnp.zeros((gap, 2 * kv_width), BFLOAT), rim, jnp.concatenate([keys, values], axis=1)], axis=0
    )
    kv_ext = kv_ext.reshape(tokens + 128, 2, kv_heads, HEAD_SIZE).transpose(1, 2, 0, 3)
    key_ext = kv_ext[0]
    tail = jnp.where(jnp.arange(128 - HEAD_SIZE) < 2, 1.0, 0.0).astype(BFLOAT)
    value_ext = jnp.concatenate(
        [kv_ext[1], jnp.broadcast_to(tail, (kv_heads, tokens + 128, 128 - HEAD_SIZE))], axis=2
    )
    masked_values = value_ext * carry.astype(BFLOAT)
    extent = tokens + 128
    call = functools.partial(heads_call, kv_heads=kv_heads, group=group)
    phi_q, phi_k, state_part = call(
        phi_kernel,
        args=[
            (queries, "cols"),
            (key_ext, "heads"),
            (masked_values, "heads"),
            (query_table, "heads"),
            (key_table, "heads"),
        ],
        outs=[
            ((heads, tokens, 128), BFLOAT, "heads"),
            ((heads, extent, 128), BFLOAT, "heads"),
            ((heads, 128, 128), BFLOAT, "heads"),
        ],
        flops=4e9,
    )
    numer_part = call(
        intra_kernel,
        args=[
            (queries, "cols"),
            (key_ext, "heads"),
            (value_ext, "heads"),
            (phi_q, "heads"),
            (phi_k, "heads"),
            (seg_column, "all"),
            (seg_line, "all"),
        ],
        outs=[((heads, tokens, 128), FLOAT, "heads")],
        flops=8e9,
    )[0]
    state = carried(state_part, forward_coefs)
    attended, denominator = call(
        finish_kernel,
        args=[(numer_part, "heads"), (phi_q, "heads"), (state, "heads"), (continuing, "all")],
        outs=[((tokens, q_width), BFLOAT, "cols"), ((kv_heads, tokens, 128), FLOAT, "heads")],
        flops=1e9,
    )

    out_and_down = jnp.concatenate(
        [full_out, own_output_down, jnp.zeros((q_width, 128 - rank), BFLOAT)], axis=1
    )

    def over_heads(part):
        halves = part.reshape(CORES, own_rows, -1)
        mine = take(halves, core, 0)[0].astype(FLOAT) + swap(
            take(halves, 1 - core, 0)[0].astype(BFLOAT), "core"
        ).astype(FLOAT)
        return pair_sum(mine, "tensor")

    branch = over_heads(product(attended, out_and_down).astype(BFLOAT))
    low_mid = branch[:, model : model + rank].astype(BFLOAT)
    hidden_own = hidden_in.astype(FLOAT)
    residual = hidden_own + branch[:, :model] + product(low_mid, output_up)
    normed_ff = (residual * norm_scale(residual) * feedforward_gain).astype(BFLOAT)

    parts = []
    for gathered, cotangent, order in zip(gather_rows(normed_ff), cotangents, t_orders):
        there = feed(gathered[1], cotangent[1], full_gate, full_up, full_down)
        here = feed(gathered[0], cotangent[0], full_gate, full_up, full_down)
        parts.append((here, gathered[0], cotangent[0]))
        parts.append((there, gathered[1], cotangent[1]))

    def halves_sum(which):
        pieces = [
            scatter_tokens(parts[2 * at][0][which], parts[2 * at + 1][0][which], t_orders[at])
            for at in range(2)
        ]
        return pair_sum(jnp.concatenate(pieces, axis=0), "tensor")

    grad_normed_ff = halves_sum(4)

    def rows_sum(pick):
        return sum(t_product(*pick(part)) for part in parts)

    gate_grad = rows_sum(lambda part: (part[1], part[0][1]))
    up_grad = rows_sum(lambda part: (part[1], part[0][2]))
    down_grad = rows_sum(lambda part: (part[0][0], part[2]))
    block_output = (residual + halves_sum(3)).astype(BFLOAT)

    def dp_half(grad, dim):
        half = grad.shape[dim] // 2
        send = lax.dynamic_slice_in_dim(grad, (1 - dp_at) * half, half, dim).astype(BFLOAT)
        keep = lax.dynamic_slice_in_dim(grad, dp_at * half, half, dim).astype(FLOAT)
        return (keep + swap(send, "dp").astype(FLOAT)).astype(BFLOAT)

    down_shard = lax.all_to_all(dp_half(down_grad, 1), ff_axes, 1, 0, tiled=True).astype(FLOAT)
    gate_shard = lax.all_to_all(dp_half(gate_grad, 0), ff_axes, 0, 1, tiled=True).astype(FLOAT)
    up_shard = lax.all_to_all(dp_half(up_grad, 0), ff_axes, 0, 1, tiled=True).astype(FLOAT)

    grad_res_part, feedforward_gain_grad = norm_back(residual, feedforward_gain, grad_normed_ff)
    grad_residual = block_cotangent.astype(FLOAT) + grad_res_part
    grad_branch_own = grad_residual.astype(BFLOAT)
    output_up_grad = t_product(low_mid, grad_branch_own)
    grad_branch = ordered(core, grad_branch_own, swap(grad_branch_own, "core"), 0)
    grad_mid = product_t(grad_branch, output_up).astype(BFLOAT)
    grad_attended = product_t(grad_branch, full_out) + product_t(grad_mid, own_output_down)
    output_down_grad = t_product(grad_mid, attended)
    out_grad = t_product(attended, grad_branch).astype(BFLOAT)
    grad_numer, grad_state_part = call(
        grad_numer_kernel,
        args=[
            (grad_attended, "cols"),
            (attended, "cols"),
            (denominator, "heads"),
            (phi_q, "heads"),
            (continuing, "all"),
        ],
        outs=[((heads, tokens, 128), BFLOAT, "heads"), ((heads, 128, 128), BFLOAT, "heads")],
        flops=2e9,
    )
    intra = call(
        intra_back_kernel,
        args=[
            (queries, "cols"),
            (key_ext, "heads"),
            (value_ext, "heads"),
            (phi_q, "heads"),
            (phi_k, "heads"),
            (grad_numer, "heads"),
            (seg_column, "all"),
            (seg_line, "all"),
        ],
        outs=[
            ((tokens, q_width), FLOAT, "cols"),
            ((kv_heads, extent, HEAD_SIZE), FLOAT, "heads"),
            ((kv_heads, extent, 128), FLOAT, "heads"),
            ((heads, tokens, 128), FLOAT, "heads"),
            ((heads, extent, 128), FLOAT, "heads"),
        ],
        flops=16e9,
    )
    grad_state = carried(grad_state_part, backward_coefs)
    grad_queries, grad_keys, grad_values, query_tables, key_tables = call(
        features_back_kernel,
        args=[
            (queries, "cols"),
            (key_ext, "heads"),
            (value_ext, "heads"),
            (phi_q, "heads"),
            (phi_k, "heads"),
            (grad_numer, "heads"),
            (query_table, "heads"),
            (key_table, "heads"),
            (state, "heads"),
            (grad_state, "heads"),
            (continuing, "all"),
            (carry, "all"),
            (intra[0], "cols"),
            (intra[1], "heads"),
            (intra[2], "heads"),
            (intra[3], "heads"),
            (intra[4], "heads"),
        ],
        outs=[
            ((tokens, q_width), FLOAT, "cols"),
            ((kv_heads, extent, HEAD_SIZE), FLOAT, "heads"),
            ((kv_heads, extent, 128), FLOAT, "heads"),
            ((heads, HEAD_SIZE, 128), FLOAT, "heads"),
            ((heads, HEAD_SIZE, 128), FLOAT, "heads"),
        ],
        flops=6e9,
    )
    query_table_grad = query_tables[:, :, :FEATURE_HALF] - query_tables[:, :, FEATURE_HALF:]
    key_table_grad = key_tables[:, :, :FEATURE_HALF] - key_tables[:, :, FEATURE_HALF:]
    grad_kv_ext = jnp.concatenate(
        [grad_keys[head, gap:] for head in range(kv_heads)]
        + [grad_values[head, gap:, :HEAD_SIZE] for head in range(kv_heads)],
        axis=1,
    )
    rim_grad = lax.ppermute(
        grad_kv_ext[:SOFTMAX_KEYS],
        "chip",
        [(source + 1, source) for source in range(chips - 1)],
    )
    grad_kv = grad_kv_ext[SOFTMAX_KEYS:] + jnp.pad(rim_grad, ((tokens - SOFTMAX_KEYS, 0), (0, 0)))
    grad_pre = jnp.concatenate(
        [
            rotate_back(grad_queries, cosine_table, sine_table),
            rotate_back(grad_kv[:, :kv_width], cosine_table, sine_table),
            grad_kv[:, kv_width:],
        ],
        axis=1,
    ).astype(BFLOAT)
    qkv_grad = t_product(normed, grad_pre).astype(BFLOAT)
    back_weights = jnp.concatenate(
        [full_qkv, ups, jnp.zeros((pad, qkv_width), BFLOAT)], axis=0
    )
    back = over_heads(product_t(grad_pre, back_weights).astype(BFLOAT))
    grad_low = back[:, model : model + 3 * rank].astype(BFLOAT)
    grad_normed = back[:, :model] + product_t(grad_low, downs)
    normed_own = (hidden_own * norm_scale(hidden_own) * attention_gain).astype(BFLOAT)
    downs_grad = t_product(grad_low, normed_own)
    grad_in_part, attention_gain_grad = norm_back(hidden_own, attention_gain, grad_normed)
    input_grad = (grad_residual + grad_in_part).astype(BFLOAT)
    ups_grad = t_product(low_rank, grad_pre)
    value_up_grad = t_product(low_rank[:, 2 * rank :], grad_pre[:, q_width + kv_width :])

    def scatter_two(parts):
        return [scatter_blocks(part, order[::-1]) for part, order in zip(parts, orders)]

    blocks = 2 ** len(cube_dims())
    qkv_blocks = qkv_grad.reshape(blocks, CORES, model // blocks // CORES, qkv_width)
    qkv_sums = jnp.concatenate(scatter_two(jnp.split(qkv_blocks, 2, axis=3)), axis=2)
    qkv_keep = take(qkv_sums, core, 0)[0]
    qkv_other = swap(take(qkv_sums, 1 - core, 0)[0].astype(BFLOAT), "core").astype(FLOAT)
    query_shard = ordered(core, qkv_keep[:, :q_width], qkv_other[:, :q_width], 1)
    key_shard = ordered(
        core,
        qkv_keep[:, q_width : q_width + kv_width],
        qkv_other[:, q_width : q_width + kv_width],
        1,
    )
    value_shard = ordered(
        core, qkv_keep[:, q_width + kv_width :], qkv_other[:, q_width + kv_width :], 1
    )
    out_blocks = out_grad.reshape(q_width, blocks, CORES, model // blocks // CORES).transpose(
        1, 2, 0, 3
    )
    out_sums = jnp.concatenate(scatter_two(jnp.split(out_blocks, 2, axis=2)), axis=1)
    out_keep = take(out_sums, core, 0)[0]
    out_other = swap(take(out_sums, 1 - core, 0)[0].astype(BFLOAT), "core").astype(FLOAT)
    output_shard = ordered(core, out_keep, out_other, 0)

    shared = jnp.concatenate(
        [attention_gain_grad[None], feedforward_gain_grad[None], downs_grad, output_up_grad], axis=0
    )
    headed = jnp.concatenate(
        [
            query_table_grad.reshape(-1, model),
            key_table_grad.reshape(-1, model),
            jnp.concatenate([output_down_grad, ups_grad[:rank, :q_width]], axis=0).reshape(-1, model),
            jnp.concatenate(
                [
                    ups_grad[rank : 2 * rank, q_width : q_width + kv_width],
                    value_up_grad,
                ],
                axis=0,
            ).reshape(-1, model),
        ],
        axis=0,
    )
    shared_rows = shared.shape[0]
    shared = shared + swap(shared, "core")
    small = jnp.concatenate([shared, headed], axis=0)
    for axis, mask in cube_dims()[::-1]:
        small = small + swap(small, axis, mask)
    shared = small[:shared_rows]
    headed = small[shared_rows:]
    both = ordered(core, headed[None], swap(headed, "core")[None], 0)
    table_rows = heads * HEAD_SIZE * FEATURE_HALF // model
    query_features = both[:, :table_rows].reshape(CORES * heads, HEAD_SIZE, FEATURE_HALF)
    key_features = both[:, table_rows : 2 * table_rows].reshape(
        CORES * heads, HEAD_SIZE, FEATURE_HALF
    )
    wide_rows = rank * q_width // model
    at = 2 * table_rows
    down_total = both[:, at : at + wide_rows].reshape(CORES, rank, q_width)
    query_up_total = both[:, at + wide_rows : at + 2 * wide_rows].reshape(CORES, rank, q_width)
    narrow = both[:, at + 2 * wide_rows :].reshape(CORES, 2, rank, kv_width)

    def joined(value):
        return jnp.concatenate([value[0], value[1]], axis=1)

    downs_total = shared[2 : 2 + 3 * rank].T
    return (
        block_output,
        input_grad,
        shared[0],
        query_shard,
        key_shard,
        value_shard,
        output_shard,
        downs_total[:, :rank],
        joined(query_up_total),
        downs_total[:, rank : 2 * rank],
        joined(narrow[:, 0]),
        downs_total[:, 2 * rank :],
        joined(narrow[:, 1]),
        joined(down_total).T,
        shared[2 + 3 * rank :],
        query_features,
        key_features,
        shared[1],
        gate_shard,
        up_shard,
        down_shard,
    )


def solution(mesh):
    dp, seq, tensor = (mesh.shape[name] for name in ("dp", "seq", "tensor"))
    split = Mesh(
        mesh.devices.reshape(dp, seq // CORES, CORES, tensor), ("dp", "chip", "core", "tensor")
    )
    tok = ("dp", "chip", "core")
    in_specs = (
        P(tok, None),
        P("dp", None),
        P(),
        P(tok, "tensor"),
        P(tok, "tensor"),
        P(tok, "tensor"),
        P("tensor", tok),
        P(),
        P(None, "tensor"),
        P(),
        P(None, "tensor"),
        P(),
        P(None, "tensor"),
        P("tensor", None),
        P(),
        P("tensor", None, None),
        P("tensor", None, None),
        P(),
        P(tok, "tensor"),
        P(tok, "tensor"),
        P("tensor", tok),
        P(tok, None),
    )
    out_specs = (
        P(tok, None),
        P(tok, None),
        P(),
        P(tok, "tensor"),
        P(tok, "tensor"),
        P(tok, "tensor"),
        P("tensor", tok),
        P(),
        P(None, "tensor"),
        P(),
        P(None, "tensor"),
        P(),
        P(None, "tensor"),
        P("tensor", None),
        P(),
        P("tensor", None, None),
        P("tensor", None, None),
        P(),
        P(tok, "tensor"),
        P(tok, "tensor"),
        P("tensor", tok),
    )
    return jax.shard_map(
        on_device, mesh=split, in_specs=in_specs, out_specs=out_specs, check_vma=False
    )
```

```python
import functools

import jax
import jax.numpy as jnp
import numpy as np
from jax import lax
from jax.experimental import pallas as pl
from jax.experimental.pallas import tpu as pltpu
from jax.sharding import Mesh
from jax.sharding import PartitionSpec as P

HEAD_SIZE = 64
FEATURE_HALF = 64
SOFTMAX_KEYS = 64
CORES = 2


EPS = 1e-05
FLOAT = jnp.float32
BFLOAT = jnp.bfloat16


def ordered(which, mine, other, dim):
    return jnp.where(
        which == 0,
        jnp.concatenate([mine, other], axis=dim),
        jnp.concatenate([other, mine], axis=dim),
    )


def frequencies(head_width):
    inverse = 1.0 / 500000.0 ** (np.arange(0, head_width, 2) / head_width)
    wavelen = 2.0 * np.pi / inverse
    smooth = (8192.0 / wavelen - 1.0) / 3.0
    blended = (1.0 - smooth) * inverse / 32.0 + smooth * inverse
    return np.where(wavelen > 8192.0, inverse / 32.0, np.where(wavelen < 2048.0, inverse, blended))


def rotation(positions, head_width):
    freq_table = jnp.asarray(frequencies(head_width), FLOAT)
    turned = positions.astype(FLOAT)[:, None] * freq_table[None, :]
    cosine, sine = jnp.cos(turned), jnp.sin(turned)
    return (
        jnp.concatenate([cosine, cosine], axis=-1),
        jnp.concatenate([-sine, sine], axis=-1),
    )


def spread(table, width):
    return jnp.tile(table, (1, width // table.shape[1]))


def locate(places, lengths):
    doc_ends = jnp.cumsum(lengths)
    passed = places[:, None] >= doc_ends[None, :]
    segment = jnp.sum(passed.astype(jnp.int32), axis=1)
    doc_begin = jnp.sum(jnp.where(passed, lengths[None, :], 0), axis=1)
    return (jnp.where(places < 0, -1, segment), places - doc_begin)


def product(left, right):
    return jnp.dot(left, right, preferred_element_type=FLOAT)


def product_t(left, right):
    return lax.dot_general(left, right, (((1,), (1,)), ((), ())), preferred_element_type=FLOAT)


def t_product(left, right):
    return lax.dot_general(left, right, (((0,), (0,)), ((), ())), preferred_element_type=FLOAT)


def dot(left, right):
    return lax.dot_general(left, right, (((1,), (0,)), ((), ())), preferred_element_type=FLOAT)


def lanes(shape):
    return lax.broadcasted_iota(jnp.int32, shape, 1)


def half_sums(rows):
    first = lax.broadcasted_iota(jnp.int32, (128, 128), 0) < FEATURE_HALF
    ones = jnp.where(first == (lanes((128, 128)) < FEATURE_HALF), 1.0, 0.0).astype(BFLOAT)
    return dot(rows, ones)


def two_softmax(mixed):
    low = lanes(mixed.shape) < FEATURE_HALF
    top = jnp.max(jnp.where(low, mixed, -jnp.inf), axis=1, keepdims=True)
    top_other = jnp.max(jnp.where(low, -jnp.inf, mixed), axis=1, keepdims=True)
    raised = jnp.exp(mixed - jnp.where(low, top, top_other))
    return (raised / half_sums(raised.astype(BFLOAT))).astype(BFLOAT)


def phi_kernel(group, q_ref, k_ref, vm_ref, fq_ref, fk_ref, phi_q_ref, phi_k_ref, state_ref):
    keys = k_ref[0]
    masked = vm_ref[0]
    for head in range(group):
        rows = q_ref[:, head * HEAD_SIZE : (head + 1) * HEAD_SIZE]
        phi_q_ref[head] = two_softmax(dot(rows, fq_ref[head]))
        phi_k = two_softmax(dot(keys, fk_ref[head]))
        phi_k_ref[head] = phi_k
        state_ref[head] = t_product(masked, phi_k).astype(BFLOAT)


def tile_masks(seg_q, seg_k, at):
    width = at + 256
    same = seg_q == seg_k[:, :width]
    row = lax.broadcasted_iota(jnp.int32, (128, 256), 0)
    col = lanes((128, 256))
    earlier = col <= row + SOFTMAX_KEYS
    window = (col > row + SOFTMAX_KEYS) & (col <= row + 128) & same[:, at:]
    return same[:, :at], window, earlier & same[:, at:]


def tile_weights(rows, phi_rows, k_ref, phi_k, at, masks):
    far, window, earlier = masks
    scale = HEAD_SIZE ** (-0.5)
    raw = product_t(rows, k_ref[0, at : at + 256])
    window_exp = jnp.where(window, jnp.exp(jnp.where(window, scale * raw, 0.0)), 0.0)
    linear = product_t(phi_rows, phi_k[: at + 256])
    near = jnp.where(earlier, linear[:, at:], window_exp)
    if at == 0:
        return window_exp, near.astype(BFLOAT)
    return window_exp, jnp.concatenate(
        [jnp.where(far, linear[:, :at], 0.0), near], axis=1
    ).astype(BFLOAT)


def intra_kernel(group, q_ref, k_ref, v_ref, phi_q_ref, phi_k_ref, seg_q_ref, seg_k_ref, num_ref):
    for at in range(0, q_ref.shape[0], 128):
        masks = tile_masks(seg_q_ref[at : at + 128], seg_k_ref[...], at)
        for head in range(group):
            rows = q_ref[at : at + 128, head * HEAD_SIZE : (head + 1) * HEAD_SIZE]
            weights = tile_weights(
                rows, phi_q_ref[head, at : at + 128], k_ref, phi_k_ref.at[head], at, masks
            )[1]
            num_ref[head, at : at + 128] = dot(weights, v_ref[0, : at + 256])


def finish_kernel(group, num_ref, phi_q_ref, state_ref, cont_ref, att_ref, den_ref):
    cont = cont_ref[...]
    den = jnp.zeros(den_ref.shape[1:], FLOAT)
    for head in range(group):
        total = num_ref[head] + cont * product_t(phi_q_ref[head], state_ref[head])
        below = total[:, HEAD_SIZE : HEAD_SIZE + 1]
        att_ref[:, head * HEAD_SIZE : (head + 1) * HEAD_SIZE] = (
            total[:, :HEAD_SIZE] / below
        ).astype(BFLOAT)
        den = jnp.where(lanes(den.shape) == head, below, den)
    den_ref[0] = den


def grad_numer_kernel(group, da_ref, att_ref, den_ref, phi_q_ref, cont_ref, dn_ref, ds_ref):
    cont = cont_ref[...]
    for head in range(group):
        cols = slice(head * HEAD_SIZE, (head + 1) * HEAD_SIZE)
        numer = da_ref[:, cols] / den_ref[0][:, head : head + 1]
        denom = -jnp.sum(numer * att_ref[:, cols].astype(FLOAT), axis=1, keepdims=True)
        high = denom.astype(BFLOAT).astype(FLOAT)
        wide = jnp.concatenate([numer, jnp.zeros_like(numer)], axis=1)
        lane = lanes(wide.shape)
        wide = jnp.where(lane == HEAD_SIZE, high, wide)
        wide = jnp.where(lane == HEAD_SIZE + 1, denom - high, wide)
        dn_ref[head] = wide.astype(BFLOAT)
        state = t_product((wide * cont).astype(BFLOAT), phi_q_ref[head])
        row = lax.broadcasted_iota(jnp.int32, state.shape, 0)
        both = state[HEAD_SIZE : HEAD_SIZE + 1] + state[HEAD_SIZE + 1 : HEAD_SIZE + 2]
        state = jnp.where(row == HEAD_SIZE, both, jnp.where(row > HEAD_SIZE, 0.0, state))
        ds_ref[head] = state.astype(BFLOAT)


def intra_back_kernel(
    group, q_ref, k_ref, v_ref, phi_q_ref, phi_k_ref, dn_ref, seg_q_ref, seg_k_ref,
    dq_ref, dk_ref, dv_ref, dphi_q_ref, dphi_k_ref,
):
    scale = HEAD_SIZE ** (-0.5)
    dk_ref[...] = jnp.zeros(dk_ref.shape, FLOAT)
    dv_ref[...] = jnp.zeros(dv_ref.shape, FLOAT)
    dphi_k_ref[...] = jnp.zeros(dphi_k_ref.shape, FLOAT)
    for at in range(0, q_ref.shape[0], 128):
        masks = tile_masks(seg_q_ref[at : at + 128], seg_k_ref[...], at)
        tile = slice(at, at + 128)
        width = at + 256
        for head in range(group):
            cols = slice(head * HEAD_SIZE, (head + 1) * HEAD_SIZE)
            rows = q_ref[tile, cols]
            phi_rows = phi_q_ref[head, tile]
            numer = dn_ref[head, tile]
            window_exp, weights = tile_weights(
                rows, phi_rows, k_ref, phi_k_ref.at[head], at, masks
            )
            grad = product_t(numer, v_ref[0, :width])
            near = grad[:, at:]
            grad_raw = (scale * near * window_exp).astype(BFLOAT)
            grad_linear = jnp.where(masks[2], near, 0.0)
            if at > 0:
                grad_linear = jnp.concatenate(
                    [jnp.where(masks[0], grad[:, :at], 0.0), grad_linear], axis=1
                )
            grad_linear = grad_linear.astype(BFLOAT)
            dv_ref[0, :width] += t_product(weights, numer)
            dphi_q_ref[head, tile] = dot(grad_linear, phi_k_ref[head, :width])
            dphi_k_ref[head, :width] += t_product(grad_linear, phi_rows)
            dq_ref[tile, cols] = dot(grad_raw, k_ref[0, at:width])
            dk_ref[0, at:width] += t_product(grad_raw, rows)


def softmax_back(phi, grad):
    wide = phi.astype(FLOAT)
    terms = grad * wide
    high = terms.astype(BFLOAT)
    low = (terms - high.astype(FLOAT)).astype(BFLOAT)
    mean = (half_sums(high) + half_sums(low)) / half_sums(phi)
    return (wide * (grad - mean)).astype(BFLOAT)


def features_back_kernel(
    group, q_ref, k_ref, v_ref, phi_q_ref, phi_k_ref, dn_ref, fq_ref, fk_ref, state_ref, ds_ref,
    cont_ref, carry_ref, dq_in, dk_in, dv_in, dphi_q_ref, dphi_k_ref,
    dq_ref, dk_ref, dv_ref, gq_ref, gk_ref,
):
    cont = cont_ref[...]
    carry = carry_ref[...]
    keys = k_ref[0]
    dk = dk_in[0]
    dv = dv_in[0]
    for head in range(group):
        cols = slice(head * HEAD_SIZE, (head + 1) * HEAD_SIZE)
        grad_state = ds_ref[head]
        phi_k = phi_k_ref[head]
        grad_q = dphi_q_ref[head] + cont * dot(dn_ref[head], state_ref[head])
        grad_k = dphi_k_ref[head] + carry * dot(v_ref[0], grad_state)
        dv = dv + carry * product_t(phi_k, grad_state)
        mixed_q = softmax_back(phi_q_ref[head], grad_q)
        mixed_k = softmax_back(phi_k, grad_k)
        dq_ref[:, cols] = dq_in[:, cols] + product_t(mixed_q, fq_ref[head])
        dk = dk + product_t(mixed_k, fk_ref[head])
        gq_ref[head] = t_product(q_ref[:, cols], mixed_q)
        gk_ref[head] = t_product(keys, mixed_k)
    dk_ref[0] = dk
    dv_ref[0] = dv


def remote(source, target, send_sem, recv_sem, **where):
    return pltpu.make_async_remote_copy(
        src_ref=source,
        dst_ref=target,
        send_sem=send_sem,
        recv_sem=recv_sem,
        device_id=where,
        device_id_type=pl.DeviceIdType.MESH,
    )


def greet(peers):
    barrier = pltpu.get_barrier_semaphore()
    for where in peers:
        pl.semaphore_signal(barrier, inc=1, device_id=where, device_id_type=pl.DeviceIdType.MESH)
    pl.semaphore_wait(barrier, len(peers))


def feed_kernel(
    chips, x_ref, c_ref, ff_ref,
    grad_ref, out_ref, ffg_ref, got_ref,
    x_buf, c_buf, gg_ref, gu_ref, gd_ref, keep, sib_out, sib_in, part, stage, wide,
    load_sems, stage_sems, sib_send, sib_recv, part_send, part_recv, cross_sems, ffg_sems, free_sem,
):
    core, chip, tensor = (lax.axis_index(name) for name in ("core", "chip", "tensor"))
    rows = keep.shape[2]
    count, model = x_buf.shape[1:]
    units = ff_ref.shape[2]
    gate_ref, up_ref, down_ref = (ff_ref.at[which] for which in range(3))
    sibling = {"core": 1 - core}
    greet(
        [sibling, {"tensor": 1 - tensor}]
        + [{"chip": lax.rem(chip + step, chips)} for step in range(1, chips)]
    )

    def place(step):
        return lax.rem(step + 1, chips)

    def loads(step):
        slot = lax.rem(step, 2)
        return [
            pltpu.make_async_copy(ref.at[place(step)], buf.at[slot], load_sems.at[at, slot])
            for at, (ref, buf) in enumerate(((x_ref, x_buf), (c_ref, c_buf)))
        ]

    def to_sibling(step):
        slot = lax.rem(step, 2)
        return remote(
            sib_out.at[slot], sib_in.at[slot], sib_send.at[slot], sib_recv.at[slot], **sibling
        )

    def stage_copy(step):
        slot = lax.rem(step, 2)
        return pltpu.make_async_copy(stage.at[slot], out_ref.at[place(step)], stage_sems.at[slot])

    def to_chip(step):
        return remote(
            part.at[step],
            got_ref.at[step],
            part_send.at[step],
            part_recv.at[step],
            chip=lax.rem(chip + step + 1, chips),
        )

    def total(step, which):
        slot = lax.rem(step, 2)
        return keep[slot, which].astype(FLOAT) + sib_in[slot, which].astype(FLOAT)

    for copy in loads(0):
        copy.start()
    gg_ref[...] = jnp.zeros(gg_ref.shape, FLOAT)
    gu_ref[...] = jnp.zeros(gu_ref.shape, FLOAT)
    gd_ref[...] = jnp.zeros(gd_ref.shape, FLOAT)

    def body(step, nothing):
        slot = lax.rem(step, 2)
        for copy in loads(step):
            copy.wait()

        @pl.when(step < chips - 1)
        def _():
            for copy in loads(step + 1):
                copy.start()

        tokens = x_buf[slot]
        cotangent = c_buf[slot]
        gate = dot(tokens, gate_ref[...])
        up = dot(tokens, up_ref[...])
        grad = dot(cotangent, down_ref[...])
        sigmoid = 1.0 / (1.0 + jnp.exp(-gate))
        silu = gate * sigmoid
        hidden = (silu * up).astype(BFLOAT)
        grad_gate = (grad * up * (sigmoid + silu * (1.0 - sigmoid))).astype(BFLOAT)
        grad_up = (grad * silu).astype(BFLOAT)

        @pl.when(step >= 2)
        def _():
            to_sibling(step).wait_send()
            pl.semaphore_wait(free_sem, 1)

        def back(part_of):
            return (
                product_t(grad_gate[part_of], gate_ref[...])
                + product_t(grad_up[part_of], up_ref[...])
            ).astype(BFLOAT)

        def out(part_of):
            return product_t(hidden[part_of], down_ref[...]).astype(BFLOAT)

        mine, theirs = slice(0, rows), slice(rows, 2 * rows)
        sib_out[slot, 0] = back(theirs)
        sib_out[slot, 1] = out(theirs)
        to_sibling(step).start()
        keep[slot, 0] = back(mine)
        keep[slot, 1] = out(mine)

        @pl.when(step > 0)
        def _():
            before = step - 1
            to_sibling(before).wait_recv()
            part[before] = total(before, 0).astype(BFLOAT)
            to_chip(before).start()

            @pl.when(step > 2)
            def _():
                stage_copy(before).wait()

            stage[lax.rem(before, 2)] = total(before, 1).astype(BFLOAT)
            stage_copy(before).start()
            pl.semaphore_signal(free_sem, inc=1, device_id=sibling, device_id_type=pl.DeviceIdType.MESH)

        gg_ref[...] += t_product(tokens, grad_gate)
        gu_ref[...] += t_product(tokens, grad_up)
        gd_ref[...] += t_product(cotangent, hidden)
        return nothing

    lax.fori_loop(0, chips, body, 0)
    last = chips - 1
    to_sibling(last).wait_recv()
    grad_ref[...] = total(last, 0)
    if chips > 2:
        stage_copy(last).wait()
    stage[last % 2] = total(last, 1).astype(BFLOAT)
    stage_copy(last).start()
    per = model // units
    ffg_copies = []
    for which, ref in enumerate((gg_ref, gu_ref, gd_ref)):
        for at in range(model // count):
            place_at = which * (model // count) + at
            buf = (x_buf, c_buf)[place_at // (2 * per)]
            spot = buf.at[(place_at // per) % 2, :, pl.ds((place_at % per) * units, units)]
            piece = pl.ds(at * count, count)
            spot[...] = ref[piece].astype(BFLOAT)
            copy = pltpu.make_async_copy(spot, ffg_ref.at[which, piece], ffg_sems.at[place_at])
            copy.start()
            ffg_copies.append(copy)

    def finish(step, nothing):
        to_chip(step).wait_recv()
        load = pltpu.make_async_copy(got_ref.at[step], wide.at[0], load_sems.at[0, 0])
        load.start()
        load.wait()
        grad_ref[...] += wide[0].astype(FLOAT)
        return nothing

    lax.fori_loop(0, chips - 1, finish, 0)
    wide[0] = grad_ref[...].astype(BFLOAT)
    across = remote(wide.at[0], wide.at[1], cross_sems.at[0], cross_sems.at[1], tensor=1 - tensor)
    across.start()

    def drain(step, nothing):
        to_chip(step).wait_send()
        return nothing

    lax.fori_loop(0, chips - 1, drain, 0)
    for copy in ffg_copies:
        copy.wait()
    for step in range(max(0, chips - 2), chips):
        to_sibling(step).wait_send()
        stage_copy(step).wait()
    pl.semaphore_wait(free_sem, min(1, chips - 1))
    across.wait()
    grad_ref[...] = wide[0].astype(FLOAT) + wide[1].astype(FLOAT)


def feed(tokens, cotangent, weights):
    chips, count, model = tokens.shape
    rows = count // CORES
    units = weights.shape[2]
    near = pl.BlockSpec(memory_space=pltpu.VMEM)
    far = pl.BlockSpec(memory_space=pl.ANY)
    return pl.pallas_call(
        functools.partial(feed_kernel, chips),
        in_specs=[far, far, near],
        out_specs=[near, far, far, far],
        out_shape=[
            jax.ShapeDtypeStruct((rows, model), FLOAT),
            jax.ShapeDtypeStruct((chips, rows, model), BFLOAT),
            jax.ShapeDtypeStruct(weights.shape, BFLOAT),
            jax.ShapeDtypeStruct((chips - 1, rows, model), BFLOAT),
        ],
        scratch_shapes=[
            pltpu.VMEM((2, count, model), BFLOAT),
            pltpu.VMEM((2, count, model), BFLOAT),
            pltpu.VMEM((model, units), FLOAT),
            pltpu.VMEM((model, units), FLOAT),
            pltpu.VMEM((model, units), FLOAT),
            pltpu.VMEM((2, 2, rows, model), BFLOAT),
            pltpu.VMEM((2, 2, rows, model), BFLOAT),
            pltpu.VMEM((2, 2, rows, model), BFLOAT),
            pltpu.VMEM((chips - 1, rows, model), BFLOAT),
            pltpu.VMEM((2, rows, model), BFLOAT),
            pltpu.VMEM((2, rows, model), BFLOAT),
            pltpu.SemaphoreType.DMA((2, 2)),
            dma_row(2),
            dma_row(2),
            dma_row(2),
            dma_row(chips - 1),
            dma_row(chips - 1),
            dma_row(2),
            dma_row(3 * model // count),
            pltpu.SemaphoreType.REGULAR,
        ],
        compiler_params=pltpu.CompilerParams(
            vmem_limit_bytes=62 * 1024 * 1024, collective_id=1, has_side_effects=True
        ),
        cost_estimate=pl.CostEstimate(
            flops=18 * chips * count * model * units,
            bytes_accessed=8 * chips * count * model,
            transcendentals=0,
        ),
    )(tokens, cotangent, weights)


def dma_row(count):
    return pltpu.SemaphoreType.DMA((count,))


def front_kernel(
    chips, kv_heads, group,
    hid_ref, again_ref, fgain_ref, downs_ref, ups_ref, cos_ref, sin_ref, fq_ref, fk_ref,
    seg_q_ref, seg_k_ref, cont_ref, carry_ref, coef_ref, odown_ref, oup_ref,
    wqkv_ref, wo_ref, gate_ref, up_ref, down_ref, cot_ref,
    qkv_ref, wof_ref, normed_ref, low_ref, mid_ref, res_ref, q_ref, k_ref, v_ref,
    phi_q_ref, phi_k_ref, att_ref, den_ref, state_ref,
    ff_ref, call_ref, xall_ref,
    hid_sib, vm, rim_out, rim_in, st_out, st_in, num, br_out, br_in, tz_out, tz_in, xn,
    hid_sem, q1_send, q1_recv, q2_send, q2_recv, o1_send, o1_recv, o2_send, o2_recv,
    ff_send, ff_recv, local_sems, c_send, c_recv, cf_send, cf_recv, x_send, x_recv, xf_send, xf_recv,
    rim_sem, st_send, st_recv, br_sem, tz_sem,
):
    dp, chip, core, tensor = (lax.axis_index(name) for name in ("dp", "chip", "core", "tensor"))
    own = hid_ref.shape[0]
    tokens = CORES * own
    model = hid_ref.shape[1]
    shard = wqkv_ref.shape[1]
    q_width = q_ref.shape[1]
    pairs = CORES * chips
    units = ff_ref.shape[2]
    other = 1 - core
    there = 1 - dp
    sibling = {"core": other}
    at_chip = [lax.rem(chip + step, chips) for step in range(1, chips)]
    behind = [lax.rem(chip + chips - step, chips) for step in range(1, chips)]
    greet(
        [sibling, {"tensor": 1 - tensor}]
        + [{"dp": there, "core": core}, {"dp": there, "core": other}]
        + [{"chip": to, "core": which} for to in at_chip for which in (core, other)]
        + [{"dp": there, "chip": to, "core": which} for to in at_chip for which in (core, other)]
    )

    def first(source, target, send, recv):
        rows = pl.ds(((dp * chips + chip) * CORES + core) * shard, shard)
        return [
            remote(source.at[other], target.at[rows], send.at[0], recv.at[0], core=other),
            remote(source.at[core], target.at[rows], send.at[1], recv.at[1], dp=there),
            remote(source.at[other], target.at[rows], send.at[2], recv.at[2], dp=there, core=other),
        ]

    def local(source, target, at):
        rows = pl.ds(((dp * chips + chip) * CORES + core) * shard, shard)
        return pltpu.make_async_copy(source.at[core], target.at[rows], local_sems.at[at])

    def second(target, send, recv, side):
        group_at = dp if side == 0 else there
        rows = pl.ds((group_at * chips + chip) * CORES * shard, CORES * shard)
        return [
            remote(target.at[rows], target.at[rows], send.at[side, at], recv.at[side, at], chip=to)
            for at, to in enumerate(at_chip)
        ]

    q_first = first(wqkv_ref, qkv_ref, q1_send, q1_recv)
    o_first = first(wo_ref, wof_ref, o1_send, o1_recv)
    q_local, o_local = local(wqkv_ref, qkv_ref, 0), local(wo_ref, wof_ref, 1)
    q_second = [second(qkv_ref, q2_send, q2_recv, side) for side in range(2)]
    o_second = [second(wof_ref, o2_send, o2_recv, side) for side in range(2)]
    hid_copy = remote(hid_ref, hid_sib, hid_sem.at[0], hid_sem.at[1], **sibling)
    q_local.start()
    hid_copy.start()
    for copy in q_first:
        copy.start()

    ff_rows = pl.ds(((dp * chips + chip) * CORES + core) * shard, shard)
    ff_sources = (gate_ref, up_ref, down_ref)

    def ff_copy(which, step, side):
        to = lax.rem(chip * CORES + core + step, pairs)
        return remote(
            ff_sources[which].at[:, pl.ds(pl.multiple_of(to * units, units), units)],
            ff_ref.at[which, ff_rows],
            ff_send.at[which],
            ff_recv.at[which],
            dp=dp if side == 0 else there,
            chip=to // CORES,
            core=lax.rem(to, CORES),
        )

    def ff_local(which):
        return pltpu.make_async_copy(
            ff_sources[which].at[:, pl.ds(pl.multiple_of((chip * CORES + core) * units, units), units)],
            ff_ref.at[which, ff_rows],
            local_sems.at[2 + which],
        )

    def ff_start(which, side):
        def one(step, nothing):
            ff_copy(which, step, side).start()
            return nothing

        lax.fori_loop(1 - side, pairs, one, 0)

    def row_copies(source, target, send, recv):
        return [
            remote(source, target.at[step + 1, pl.ds(0, own)], send.at[step], recv.at[step], chip=to)
            for step, to in enumerate(behind)
        ]

    def forward_copy(source, target, send, recv, step):
        return remote(source, target.at[step, pl.ds(own, own)], send.at[step], recv.at[step], **sibling)

    c_copies = row_copies(cot_ref, call_ref, c_send, c_recv)
    x_copies = row_copies(xn, xall_ref, x_send, x_recv)
    c_forward = [
        forward_copy(cot_ref if step == 0 else call_ref.at[step, pl.ds(0, own)], call_ref, cf_send, cf_recv, step)
        for step in range(chips)
    ]
    x_forward = [
        forward_copy(xn if step == 0 else xall_ref.at[step, pl.ds(0, own)], xall_ref, xf_send, xf_recv, step)
        for step in range(chips)
    ]
    c_local = pltpu.make_async_copy(cot_ref, call_ref.at[0, pl.ds(0, own)], local_sems.at[5])
    x_local = pltpu.make_async_copy(xn, xall_ref.at[0, pl.ds(0, own)], local_sems.at[6])

    def normalized(rows, gain):
        return (rows * lax.rsqrt(jnp.mean(rows * rows, axis=1, keepdims=True) + EPS) * gain).astype(BFLOAT)

    hidden = hid_ref[...].astype(FLOAT)
    normed_ref[pl.ds(pl.multiple_of(core * own, own), own)] = normalized(hidden, again_ref[...])
    q_first[0].wait_recv()
    q_local.wait()
    for copy in q_second[0]:
        copy.start()
    hid_copy.wait()
    normed_ref[pl.ds(pl.multiple_of(other * own, own), own)] = normalized(
        hid_sib[...].astype(FLOAT), again_ref[...]
    )
    low_ref[...] = dot(normed_ref[...], downs_ref[...]).astype(BFLOAT)
    q_first[1].wait_recv()
    q_first[2].wait_recv()
    for copy in q_second[1]:
        copy.start()
    o_local.start()
    for copy in o_first:
        copy.start()
    for which in range(3):
        ff_local(which).start()
    c_local.start()
    ff_start(0, 1)
    o_first[0].wait_recv()
    o_local.wait()
    for copy in o_second[0]:
        copy.start()
    for side in range(2):
        for copy in q_second[side]:
            copy.wait_recv()
    o_first[1].wait_recv()
    o_first[2].wait_recv()
    for copy in o_second[1]:
        copy.start()
    ff_start(1, 1)
    ff_start(0, 0)

    pre = dot(normed_ref[...], qkv_ref[...]) + dot(low_ref[...], ups_ref[...])
    half = HEAD_SIZE // 2
    first_half = lax.rem(lanes((tokens, 128)), HEAD_SIZE) < half

    def rotated(block):
        turned = jnp.where(first_half, pltpu.roll(block, 128 - half, 1), pltpu.roll(block, half, 1))
        return (block * cos_ref[...] + turned * sin_ref[...]).astype(BFLOAT)

    for at in range(0, q_width, 128):
        q_ref[:, at : at + 128] = rotated(pre[:, at : at + 128])
    keys = rotated(pre[:, q_width : q_width + 128])
    values = pre[:, q_width + 128 :].astype(BFLOAT)
    rim_out[:, :128] = keys[tokens - SOFTMAX_KEYS :]
    rim_out[:, 128:] = values[tokens - SOFTMAX_KEYS :]
    rim_copy = remote(rim_out, rim_in, rim_sem.at[0], rim_sem.at[1], chip=lax.rem(chip + 1, chips))

    @pl.when(chip < chips - 1)
    def _():
        rim_copy.start()

    def tailed(rows):
        tail = jnp.where(lanes((rows.shape[0], 128 - HEAD_SIZE)) < 2, 1.0, 0.0).astype(BFLOAT)
        return jnp.concatenate([rows, tail], axis=1)

    gap = 128 - SOFTMAX_KEYS
    for head in range(kv_heads):
        cols = slice(head * HEAD_SIZE, (head + 1) * HEAD_SIZE)
        k_ref[head, 128:] = keys[:, cols]
        v_ref[head, 128:] = tailed(values[:, cols])
        k_ref[head, :gap] = jnp.zeros((gap, HEAD_SIZE), BFLOAT)
        v_ref[head, :gap] = tailed(jnp.zeros((gap, HEAD_SIZE), BFLOAT))

    @pl.when(chip == 0)
    def _():
        rim_in[...] = jnp.zeros(rim_in.shape, BFLOAT)

    @pl.when(chip > 0)
    def _():
        rim_copy.wait_recv()

    carry = carry_ref[...]
    for head in range(kv_heads):
        cols = slice(head * HEAD_SIZE, (head + 1) * HEAD_SIZE)
        k_ref[head, gap:128] = rim_in[:, cols]
        v_ref[head, gap:128] = tailed(rim_in[:, 128 + head * HEAD_SIZE : 128 + (head + 1) * HEAD_SIZE])
        vm[head] = (v_ref[head].astype(FLOAT) * carry).astype(BFLOAT)

    def views(at):
        heads = pl.ds(at * group, group)
        one = pl.ds(at, 1)
        wide = pl.ds(at * group * HEAD_SIZE, group * HEAD_SIZE)
        return heads, one, wide

    for at in range(kv_heads):
        heads, one, wide = views(at)
        phi_kernel(
            group, q_ref.at[:, wide], k_ref.at[one], vm.at[one], fq_ref.at[heads], fk_ref.at[heads],
            phi_q_ref.at[heads], phi_k_ref.at[heads], st_out.at[heads],
        )
    kept = HEAD_SIZE + 16
    st_copies = [
        remote(st_out.at[:, pl.ds(0, kept)], st_in.at[at], st_send.at[at], st_recv.at[at], chip=to)
        for at, to in enumerate(at_chip)
    ]
    for copy in st_copies:
        copy.start()
    ff_start(2, 1)
    ff_start(1, 0)
    for at in range(kv_heads):
        heads, one, wide = views(at)
        intra_kernel(
            group, q_ref.at[:, wide], k_ref.at[one], v_ref.at[one], phi_q_ref.at[heads],
            phi_k_ref.at[heads], seg_q_ref, seg_k_ref, num.at[heads],
        )
    total = jnp.zeros(st_in.shape[1:], FLOAT)
    for at, copy in enumerate(st_copies):
        copy.wait_recv()
        total = total + coef_ref[at] * st_in[at].astype(FLOAT)
    state_ref[:, :kept] = total.astype(BFLOAT)
    state_ref[:, kept:] = jnp.zeros((state_ref.shape[0], 128 - kept, 128), BFLOAT)
    for at in range(kv_heads):
        heads, one, wide = views(at)
        finish_kernel(
            group, num.at[heads], phi_q_ref.at[heads], state_ref.at[heads], cont_ref,
            att_ref.at[:, wide], den_ref.at[one],
        )

    for side in range(2):
        for copy in o_second[side]:
            copy.wait_recv()

    def branch(which, target):
        rows = att_ref[pl.ds(pl.multiple_of(which * own, own), own)]
        return product_t(rows, wof_ref[...]), dot(rows, odown_ref[...])

    wide_part, low_part = branch(other, None)
    br_out[:, :model] = wide_part.astype(BFLOAT)
    br_out[:, model:] = low_part.astype(BFLOAT)
    br_copy = remote(br_out, br_in, br_sem.at[0], br_sem.at[1], **sibling)
    br_copy.start()
    wide_part, low_part = branch(core, None)
    br_copy.wait_recv()
    tz_out[:, :model] = (wide_part + br_in[:, :model].astype(FLOAT)).astype(BFLOAT)
    tz_out[:, model:] = (low_part + br_in[:, model:].astype(FLOAT)).astype(BFLOAT)
    tz_copy = remote(tz_out, tz_in, tz_sem.at[0], tz_sem.at[1], tensor=1 - tensor)
    tz_copy.start()
    ff_start(2, 0)
    c_forward[0].start()
    for copy in c_copies:
        copy.start()
    tz_copy.wait_recv()
    mid = (tz_out[:, model:].astype(FLOAT) + tz_in[:, model:].astype(FLOAT)).astype(BFLOAT)
    mid_ref[...] = mid
    residual = (
        hid_ref[...].astype(FLOAT)
        + (tz_out[:, :model].astype(FLOAT) + tz_in[:, :model].astype(FLOAT))
        + dot(mid, oup_ref[...])
    )
    res_ref[...] = residual
    xn[...] = normalized(residual, fgain_ref[...])
    x_local.start()
    x_forward[0].start()
    for copy in x_copies:
        copy.start()
    for step in range(1, chips):
        c_copies[step - 1].wait_recv()
        c_forward[step].start()
    for step in range(1, chips):
        x_copies[step - 1].wait_recv()
        x_forward[step].start()

    hid_done = [br_copy, tz_copy] + q_first + o_first + q_second[0] + q_second[1]
    for copy in hid_done + o_second[0] + o_second[1] + st_copies + c_copies + x_copies:
        copy.wait_send()

    @pl.when(chip < chips - 1)
    def _():
        rim_copy.wait_send()

    for copy in c_forward + x_forward:
        copy.wait()
    c_local.wait()
    x_local.wait()
    moved = (2 * pairs - 1) * shard
    for which in range(3):
        ff_local(which).wait()
        every = ff_ref.at[which, pl.ds(0, moved)]
        remote(every, every, ff_send.at[which], ff_recv.at[which], **sibling).wait()


def front(
    chips, kv_heads, group, tokens, near_args, far_args
):
    own, model = near_args[0].shape
    heads = kv_heads * group
    q_width = heads * HEAD_SIZE
    qkv_width = q_width + 2 * kv_heads * HEAD_SIZE
    extent = tokens + 128
    units = far_args[2].shape[1] // (chips * CORES)
    near = pl.BlockSpec(memory_space=pltpu.VMEM)
    far = pl.BlockSpec(memory_space=pl.ANY)
    kept = HEAD_SIZE + 16
    near_outs = [
        ((model, qkv_width), BFLOAT),
        ((model, q_width), BFLOAT),
        ((tokens, model), BFLOAT),
        ((tokens, 128), BFLOAT),
        ((own, 128), BFLOAT),
        ((own, model), FLOAT),
        ((tokens, q_width), BFLOAT),
        ((kv_heads, extent, HEAD_SIZE), BFLOAT),
        ((kv_heads, extent, 128), BFLOAT),
        ((heads, tokens, 128), BFLOAT),
        ((heads, extent, 128), BFLOAT),
        ((tokens, q_width), BFLOAT),
        ((kv_heads, tokens, 128), FLOAT),
        ((heads, 128, 128), BFLOAT),
    ]
    far_outs = [
        ((3, model, units), BFLOAT),
        ((chips, tokens, model), BFLOAT),
        ((chips, tokens, model), BFLOAT),
    ]
    pair = dma_row(2)
    return pl.pallas_call(
        functools.partial(front_kernel, chips, kv_heads, group),
        in_specs=[near] * len(near_args) + [far] * len(far_args),
        out_specs=[near] * len(near_outs) + [far] * len(far_outs),
        out_shape=[jax.ShapeDtypeStruct(*out) for out in near_outs + far_outs],
        scratch_shapes=[
            pltpu.VMEM((own, model), BFLOAT),
            pltpu.VMEM((kv_heads, extent, 128), BFLOAT),
            pltpu.VMEM((SOFTMAX_KEYS, 256), BFLOAT),
            pltpu.VMEM((SOFTMAX_KEYS, 256), BFLOAT),
            pltpu.VMEM((heads, 128, 128), BFLOAT),
            pltpu.VMEM((chips - 1, heads, kept, 128), BFLOAT),
            pltpu.VMEM((heads, tokens, 128), FLOAT),
            pltpu.VMEM((own, model + 128), BFLOAT),
            pltpu.VMEM((own, model + 128), BFLOAT),
            pltpu.VMEM((own, model + 128), BFLOAT),
            pltpu.VMEM((own, model + 128), BFLOAT),
            pltpu.VMEM((own, model), BFLOAT),
            pair,
            dma_row(3),
            dma_row(3),
            pltpu.SemaphoreType.DMA((2, chips - 1)),
            pltpu.SemaphoreType.DMA((2, chips - 1)),
            dma_row(3),
            dma_row(3),
            pltpu.SemaphoreType.DMA((2, chips - 1)),
            pltpu.SemaphoreType.DMA((2, chips - 1)),
            dma_row(3),
            dma_row(3),
            dma_row(7),
            dma_row(chips - 1),
            dma_row(chips - 1),
            dma_row(chips),
            dma_row(chips),
            dma_row(chips - 1),
            dma_row(chips - 1),
            dma_row(chips),
            dma_row(chips),
            pair,
            dma_row(chips - 1),
            dma_row(chips - 1),
            pair,
            pair,
        ],
        compiler_params=pltpu.CompilerParams(
            vmem_limit_bytes=60 * 1024 * 1024, collective_id=2, has_side_effects=True
        ),
        cost_estimate=pl.CostEstimate(
            flops=int(1e10), bytes_accessed=int(1e8), transcendentals=0
        ),
    )(*near_args, *far_args)


def rear_kernel(
    chips, kv_heads, group, rank,
    gnf_ref, res_ref, cot_ref, hid_ref, again_ref, fgain_ref, wof_ref, odown_ref, oup_ref, mid_ref,
    att_ref, den_ref, q_ref, k_ref, v_ref, phi_q_ref, phi_k_ref, fq_ref, fk_ref, state_ref,
    seg_q_ref, seg_k_ref, cont_ref, carry_ref, coef_ref, cos_ref, sin_ref,
    normed_ref, low_ref, qkv_ref, ups_ref, downs_ref,
    out_ref, ffg_ref,
    block_ref, igrad_ref, qkv_own, qkv_sib, o_own, o_sib,
    tab_own, early_own, ups_own, late_own, tab_sib, early_sib, ups_sib, late_sib,
    ffin_ref, oin_ref,
    db, dq, dn, ds_out, ds_in, gstate, dk, dv, dphi_q, dphi_k, gq, gk, dres,
    rim_out, rim_in, gp, br_out, br_in, tz_in,
    qg, q_in, q_dp_out, q_dp_in, q_core, og, o_in, o_dp_out, o_dp_in, o_core,
    tab_slots, early_slots, ups_slots, late_slots,
    tab_dp, early_dp, ups_dp, late_dp,
    db_sem, ds_send, ds_recv, rim_sem, br_sem, tz_sem, oz_sem, o_load, os_send, os_recv,
    q_send, q_recv, q_dp_sem, q_core_sem, o_send, o_recv, o_dp_sem, o_core_sem,
    small_send, small_recv, small_dp, small_core,
    ff_send, ff_recv, local_sems,
):
    dp, chip, core, tensor = (lax.axis_index(name) for name in ("dp", "chip", "core", "tensor"))
    own, model = gnf_ref.shape
    tokens = CORES * own
    q_width = q_ref.shape[1]
    pairs = CORES * chips
    shard = model // (2 * pairs)
    units = ffg_ref.shape[2]
    other = 1 - core
    there = 1 - dp
    sibling = {"core": other}
    at_chip = [lax.rem(chip + step, chips) for step in range(1, chips)]
    greet(
        [sibling, {"tensor": 1 - tensor}]
        + [{"dp": there, "core": core}, {"dp": there, "core": other}]
        + [{"chip": to, "core": which} for to in at_chip for which in (core, other)]
        + [{"dp": there, "chip": to, "core": which} for to in at_chip for which in (core, other)]
    )
    mine = pl.ds(pl.multiple_of(core * own, own), own)
    theirs = pl.ds(pl.multiple_of(other * own, own), own)

    def ff_start(which, side):
        def one(step, nothing):
            to = lax.rem(chip * CORES + core + step, pairs)
            group_to = dp if side == 0 else there
            remote(
                ffg_ref.at[which, pl.ds((group_to * pairs + to) * shard, shard)],
                ffin_ref.at[which, dp, :, pl.ds(pl.multiple_of((chip * CORES + core) * units, units), units)],
                ff_send.at[which, side],
                ff_recv.at[which, side],
                dp=group_to,
                chip=to // CORES,
                core=lax.rem(to, CORES),
            ).start()
            return nothing

        lax.fori_loop(1 - side, pairs, one, 0)

    def ff_local(which):
        at = chip * CORES + core
        return pltpu.make_async_copy(
            ffg_ref.at[which, pl.ds((dp * pairs + at) * shard, shard)],
            ffin_ref.at[which, dp, :, pl.ds(pl.multiple_of(at * units, units), units)],
            local_sems.at[which],
        )

    os_copies = [
        remote(out_ref.at[at + 1], oin_ref.at[at], os_send.at[at], os_recv.at[at], chip=to)
        for at, to in enumerate(at_chip)
    ]

    def norm_back_rows(inputs, gain, grad):
        scale = lax.rsqrt(jnp.mean(inputs * inputs, axis=1, keepdims=True) + EPS)
        weighted = grad * gain
        back = scale * weighted - inputs * (
            scale * scale * scale * jnp.mean(weighted * inputs, axis=1, keepdims=True)
        )
        return back, jnp.sum(grad * inputs * scale, axis=0, keepdims=True)

    slots = (tab_slots, early_slots, ups_slots, late_slots)
    dp_bufs = (tab_dp, early_dp, ups_dp, late_dp)
    owns = (tab_own, early_own, ups_own, late_own)
    sibs = (tab_sib, early_sib, ups_sib, late_sib)

    def small_copies(which):
        return [
            remote(
                slots[which].at[chip], slots[which].at[chip],
                small_send.at[which, at], small_recv.at[which, at], chip=to,
            )
            for at, to in enumerate(at_chip)
        ]

    def small_start(which, value):
        slots[which][chip] = value.astype(BFLOAT)
        for copy in small_copies(which):
            copy.start()

    def small_across(which):
        return remote(
            dp_bufs[which].at[0], dp_bufs[which].at[1],
            small_dp.at[which, 0], small_dp.at[which, 1], dp=there,
        )

    def small_over(which):
        return remote(owns[which], sibs[which], small_core.at[which, 0], small_core.at[which, 1], **sibling)

    def small_middle(which):
        for copy in small_copies(which):
            copy.wait()
        total = slots[which][0].astype(FLOAT)
        for at in range(1, chips):
            total = total + slots[which][at].astype(FLOAT)
        dp_bufs[which][0] = total.astype(BFLOAT)
        small_across(which).start()

    def small_end(which):
        small_across(which).wait()
        owns[which][...] = dp_bufs[which][0].astype(FLOAT) + dp_bufs[which][1].astype(FLOAT)
        small_over(which).start()

    def grad_copies(source, target, send, recv):
        return [
            remote(
                source.at[pl.ds(((dp if side == 0 else there) * chips + to) * CORES * shard, CORES * shard)],
                target.at[at, side],
                send.at[side, at],
                recv.at[side, at],
                chip=to,
            )
            for at, to in enumerate(at_chip)
            for side in range(2)
        ]

    q_copies = grad_copies(qg, q_in, q_send, q_recv)
    o_copies = grad_copies(og, o_in, o_send, o_recv)
    q_across = remote(q_dp_out, q_dp_in, q_dp_sem.at[0], q_dp_sem.at[1], dp=there)
    o_across = remote(o_dp_out, o_dp_in, o_dp_sem.at[0], o_dp_sem.at[1], dp=there)
    q_over = remote(q_core, qkv_sib, q_core_sem.at[0], q_core_sem.at[1], **sibling)
    o_over = remote(o_core, o_sib, o_core_sem.at[0], o_core_sem.at[1], **sibling)

    def chip_sum(source, target, side):
        group_at = dp if side == 0 else there
        total = source[pl.ds((group_at * chips + chip) * CORES * shard, CORES * shard)].astype(FLOAT)
        for at in range(chips - 1):
            total = total + target[at, side].astype(FLOAT)
        return total

    def grads_middle(copies, source, target, dp_out, across):
        for copy in copies:
            copy.wait_recv()
        dp_out[...] = chip_sum(source, target, 1).astype(BFLOAT)
        across.start()

    def grads_end(source, target, dp_in, across, result, core_out, over):
        across.wait()
        total = chip_sum(source, target, 0) + dp_in[...].astype(FLOAT)
        upper, lower = total[shard:], total[:shard]
        result[...] = jnp.where(core == 0, lower, upper)
        core_out[...] = jnp.where(core == 0, upper, lower).astype(BFLOAT)
        over.start()

    back_rows, gain_row = norm_back_rows(res_ref[...], fgain_ref[...], gnf_ref[...])
    grad_residual = cot_ref[...].astype(FLOAT) + back_rows
    dres[...] = grad_residual
    db[mine] = grad_residual.astype(BFLOAT)
    db_copy = remote(db.at[mine], db.at[mine], db_sem.at[0], db_sem.at[1], **sibling)
    db_copy.start()
    ff_start(0, 1)
    for copy in os_copies:
        copy.start()
    for which in range(3):
        ff_local(which).start()
    up_rows = t_product(mid_ref[...], db[mine])[:rank]
    filler = jnp.zeros((16 - 1 - rank, model), FLOAT)
    small_start(1, jnp.concatenate([up_rows, gain_row, filler], axis=0))
    db_copy.wait_recv()
    dmid = product_t(db[...], oup_ref[...]).astype(BFLOAT)
    dq[...] = dot(db[...], wof_ref[...]) + product_t(dmid, odown_ref[...])

    def views(at):
        return (
            pl.ds(at * group, group),
            pl.ds(at, 1),
            pl.ds(at * group * HEAD_SIZE, group * HEAD_SIZE),
        )

    for at in range(kv_heads):
        heads, one, wide = views(at)
        grad_numer_kernel(
            group, dq.at[:, wide], att_ref.at[:, wide], den_ref.at[one], phi_q_ref.at[heads], cont_ref,
            dn.at[heads], ds_out.at[heads],
        )
    kept = HEAD_SIZE + 16
    ds_copies = [
        remote(ds_out.at[:, pl.ds(0, kept)], ds_in.at[at], ds_send.at[at], ds_recv.at[at], chip=to)
        for at, to in enumerate([lax.rem(chip + chips - step, chips) for step in range(1, chips)])
    ]
    for copy in ds_copies:
        copy.start()
    ff_start(1, 1)
    og[...] = t_product(db[...], att_ref[...]).astype(BFLOAT)
    for copy in o_copies:
        copy.start()
    down_rows = t_product(dmid, att_ref[...])[:rank]
    for at in range(kv_heads):
        heads, one, wide = views(at)
        intra_back_kernel(
            group, q_ref.at[:, wide], k_ref.at[one], v_ref.at[one], phi_q_ref.at[heads],
            phi_k_ref.at[heads], dn.at[heads], seg_q_ref, seg_k_ref,
            dq.at[:, wide], dk.at[one], dv.at[one], dphi_q.at[heads], dphi_k.at[heads],
        )
    total = jnp.zeros(ds_in.shape[1:], FLOAT)
    for at, copy in enumerate(ds_copies):
        copy.wait_recv()
        total = total + coef_ref[at] * ds_in[at].astype(FLOAT)
    gstate[:, :kept] = total.astype(BFLOAT)
    gstate[:, kept:] = jnp.zeros((gstate.shape[0], 128 - kept, 128), BFLOAT)
    for at in range(kv_heads):
        heads, one, wide = views(at)
        features_back_kernel(
            group, q_ref.at[:, wide], k_ref.at[one], v_ref.at[one], phi_q_ref.at[heads],
            phi_k_ref.at[heads], dn.at[heads], fq_ref.at[heads], fk_ref.at[heads],
            state_ref.at[heads], gstate.at[heads], cont_ref, carry_ref,
            dq.at[:, wide], dk.at[one], dv.at[one], dphi_q.at[heads], dphi_k.at[heads],
            dq.at[:, wide], dk.at[one], dv.at[one], gq.at[heads], gk.at[heads],
        )

    gap = 128 - SOFTMAX_KEYS

    def joined(rows):
        return jnp.concatenate(
            [dk[head, rows] for head in range(kv_heads)]
            + [dv[head, rows, :HEAD_SIZE] for head in range(kv_heads)],
            axis=1,
        )

    rim_out[...] = joined(slice(gap, 128))
    rim_copy = remote(rim_out, rim_in, rim_sem.at[0], rim_sem.at[1], chip=lax.rem(chip + chips - 1, chips))

    @pl.when(chip > 0)
    def _():
        rim_copy.start()

    tables = []
    for head in range(kv_heads * group):
        pieces = [table[head, :, :FEATURE_HALF] - table[head, :, FEATURE_HALF:] for table in (gq, gk)]
        tables.append(jnp.concatenate(pieces, axis=1))
    small_start(0, jnp.concatenate(tables, axis=0))
    half = HEAD_SIZE // 2
    first_half = lax.rem(lanes((tokens, 128)), HEAD_SIZE) < half

    def unrotated(block):
        turned = jnp.where(first_half, pltpu.roll(block, 128 - half, 1), pltpu.roll(block, half, 1))
        return (block * cos_ref[...] - turned * sin_ref[...]).astype(BFLOAT)

    for at in range(0, q_width, 128):
        gp[:, at : at + 128] = unrotated(dq[:, at : at + 128])

    @pl.when(chip == chips - 1)
    def _():
        rim_in[...] = jnp.zeros(rim_in.shape, FLOAT)

    @pl.when(chip < chips - 1)
    def _():
        rim_copy.wait_recv()

    kv = joined(slice(128, 128 + tokens))
    kv = jnp.concatenate(
        [kv[: tokens - SOFTMAX_KEYS], kv[tokens - SOFTMAX_KEYS :] + rim_in[...]], axis=0
    )
    gp[:, q_width : q_width + 128] = unrotated(kv[:, :128])
    gp[:, q_width + 128 :] = kv[:, 128:].astype(BFLOAT)

    def partial(rows):
        grads = gp[rows]
        return product_t(grads, qkv_ref[...]), product_t(grads, ups_ref[...])

    wide_part, low_part = partial(theirs)
    br_out[:, :model] = wide_part.astype(BFLOAT)
    br_out[:, model:] = low_part.astype(BFLOAT)
    br_copy = remote(br_out, br_in, br_sem.at[0], br_sem.at[1], **sibling)
    br_copy.start()
    wide_part, low_part = partial(mine)
    br_copy.wait()
    tz_out = br_out
    tz_out[:, :model] = (wide_part + br_in[:, :model].astype(FLOAT)).astype(BFLOAT)
    tz_out[:, model:] = (low_part + br_in[:, model:].astype(FLOAT)).astype(BFLOAT)
    tz_copy = remote(tz_out, tz_in, tz_sem.at[0], tz_sem.at[1], tensor=1 - tensor)
    tz_copy.start()
    qg[...] = t_product(normed_ref[...], gp[...]).astype(BFLOAT)
    for copy in q_copies:
        copy.start()
    grads_middle(o_copies, og, o_in, o_dp_out, o_across)
    ff_start(2, 1)
    ff_start(0, 0)
    ff_start(1, 0)
    ff_start(2, 0)
    ups_rows = t_product(low_ref[...], gp[...])[: 3 * rank]
    wide_down = jnp.concatenate(
        [down_rows, jnp.zeros((rank, gp.shape[1] - q_width), FLOAT)], axis=1
    )
    small_start(2, jnp.concatenate([ups_rows, wide_down], axis=0))
    small_middle(1)
    small_middle(0)
    tz_copy.wait_recv()
    low = (tz_out[:, model:].astype(FLOAT) + tz_in[:, model:].astype(FLOAT)).astype(BFLOAT)
    grad_normed = (
        tz_out[:, :model].astype(FLOAT) + tz_in[:, :model].astype(FLOAT)
    ) + product_t(low, downs_ref[...])
    low_rows = t_product(low, normed_ref[mine])[: 3 * rank]
    back_rows, gain_row = norm_back_rows(hid_ref[...].astype(FLOAT), again_ref[...], grad_normed)
    igrad_ref[...] = (dres[...] + back_rows).astype(BFLOAT)
    filler = jnp.zeros((rank - 1, model), FLOAT)
    small_start(3, jnp.concatenate([low_rows, gain_row, filler], axis=0))
    small_end(1)
    small_end(0)
    small_middle(2)
    grads_end(og, o_in, o_dp_in, o_across, o_own, o_core, o_over)

    os_buf = tz_in.at[:, pl.ds(0, model)]
    load = pltpu.make_async_copy(out_ref.at[0], os_buf, o_load.at[0])
    load.start()
    load.wait()
    dres[...] = os_buf[...].astype(FLOAT)
    for at in range(chips - 1):
        os_copies[at].wait_recv()
        load = pltpu.make_async_copy(oin_ref.at[at], os_buf, o_load.at[0])
        load.start()
        load.wait()
        dres[...] += os_buf[...].astype(FLOAT)
    tz_copy.wait_send()
    oz_out, oz_in = (ref.at[:, pl.ds(0, model)] for ref in (br_out, br_in))
    oz_out[...] = dres[...].astype(BFLOAT)
    oz_copy = remote(oz_out, oz_in, oz_sem.at[0], oz_sem.at[1], tensor=1 - tensor)
    oz_copy.start()
    grads_middle(q_copies, qg, q_in, q_dp_out, q_across)
    small_end(2)
    small_middle(3)
    oz_copy.wait()
    block_ref[...] = (
        res_ref[...] + (oz_out[...].astype(FLOAT) + oz_in[...].astype(FLOAT))
    ).astype(BFLOAT)
    grads_end(qg, q_in, q_dp_in, q_across, qkv_own, q_core, q_over)
    small_end(3)

    for copy in [db_copy] + ds_copies + os_copies + q_copies + o_copies:
        copy.wait_send()

    @pl.when(chip > 0)
    def _():
        rim_copy.wait_send()

    for which in range(4):
        small_over(which).wait()
    q_over.wait()
    o_over.wait()
    for which in range(3):
        ff_local(which).wait()
        for side in range(2):
            count = pairs - 1 + side
            group_from = dp if side == 0 else there
            sent = ffg_ref.at[which, pl.ds(0, count * shard)]
            came = ffin_ref.at[which, group_from, :, pl.ds(0, count * units)]
            remote(sent, sent, ff_send.at[which, side], ff_recv.at[which, side], **sibling).wait_send()
            remote(came, came, ff_send.at[which, side], ff_recv.at[which, side], **sibling).wait_recv()


def rear(chips, kv_heads, group, rank, near_args, far_args):
    own, model = near_args[0].shape
    tokens = CORES * own
    heads = kv_heads * group
    q_width = heads * HEAD_SIZE
    qkv_width = q_width + 2 * kv_heads * HEAD_SIZE
    extent = tokens + 128
    pairs = chips * CORES
    shard = model // (2 * pairs)
    units = far_args[1].shape[2]
    near = pl.BlockSpec(memory_space=pltpu.VMEM)
    far = pl.BlockSpec(memory_space=pl.ANY)
    kept = HEAD_SIZE + 16
    smalls = [
        (heads * HEAD_SIZE, 128),
        (16, model),
        (4 * rank, qkv_width),
        (4 * rank, model),
    ]
    near_outs = [
        ((own, model), BFLOAT),
        ((own, model), BFLOAT),
        ((shard, qkv_width), FLOAT),
        ((shard, qkv_width), BFLOAT),
        ((shard, q_width), FLOAT),
        ((shard, q_width), BFLOAT),
    ]
    near_outs += [(shape, FLOAT) for shape in smalls] * 2
    far_outs = [
        ((3, 2, shard, pairs * units), BFLOAT),
        ((chips - 1, own, model), BFLOAT),
    ]
    pair = dma_row(2)
    step_pair = pltpu.SemaphoreType.DMA((2, chips - 1))

    def grads(width):
        return [
            pltpu.VMEM((model, width), BFLOAT),
            pltpu.VMEM((chips - 1, 2, CORES * shard, width), BFLOAT),
            pltpu.VMEM((CORES * shard, width), BFLOAT),
            pltpu.VMEM((CORES * shard, width), BFLOAT),
            pltpu.VMEM((shard, width), BFLOAT),
        ]

    wide = pltpu.VMEM((own, model + 128), BFLOAT)
    return pl.pallas_call(
        functools.partial(rear_kernel, chips, kv_heads, group, rank),
        in_specs=[near] * len(near_args) + [far] * len(far_args),
        out_specs=[near] * len(near_outs) + [far] * len(far_outs),
        out_shape=[jax.ShapeDtypeStruct(*out) for out in near_outs + far_outs],
        scratch_shapes=[
            pltpu.VMEM((tokens, model), BFLOAT),
            pltpu.VMEM((tokens, q_width), FLOAT),
            pltpu.VMEM((heads, tokens, 128), BFLOAT),
            pltpu.VMEM((heads, 128, 128), BFLOAT),
            pltpu.VMEM((chips - 1, heads, kept, 128), BFLOAT),
            pltpu.VMEM((heads, 128, 128), BFLOAT),
            pltpu.VMEM((kv_heads, extent, HEAD_SIZE), FLOAT),
            pltpu.VMEM((kv_heads, extent, 128), FLOAT),
            pltpu.VMEM((heads, tokens, 128), FLOAT),
            pltpu.VMEM((heads, extent, 128), FLOAT),
            pltpu.VMEM((heads, HEAD_SIZE, 128), FLOAT),
            pltpu.VMEM((heads, HEAD_SIZE, 128), FLOAT),
            pltpu.VMEM((own, model), FLOAT),
            pltpu.VMEM((SOFTMAX_KEYS, 256), FLOAT),
            pltpu.VMEM((SOFTMAX_KEYS, 256), FLOAT),
            pltpu.VMEM((tokens, qkv_width), BFLOAT),
            wide,
            wide,
            wide,
        ]
        + grads(qkv_width)
        + grads(q_width)
        + [pltpu.VMEM((chips,) + shape, BFLOAT) for shape in smalls]
        + [pltpu.VMEM((2,) + shape, BFLOAT) for shape in smalls]
        + [
            pair,
            dma_row(chips - 1),
            dma_row(chips - 1),
            pair,
            pair,
            pair,
            pair,
            dma_row(1),
            dma_row(chips - 1),
            dma_row(chips - 1),
            step_pair,
            step_pair,
            pair,
            pair,
            step_pair,
            step_pair,
            pair,
            pair,
            pltpu.SemaphoreType.DMA((4, chips - 1)),
            pltpu.SemaphoreType.DMA((4, chips - 1)),
            pltpu.SemaphoreType.DMA((4, 2)),
            pltpu.SemaphoreType.DMA((4, 2)),
            pltpu.SemaphoreType.DMA((3, 2)),
            pltpu.SemaphoreType.DMA((3, 2)),
            dma_row(3),
        ],
        compiler_params=pltpu.CompilerParams(
            vmem_limit_bytes=63 * 1024 * 1024, collective_id=3, has_side_effects=True
        ),
        cost_estimate=pl.CostEstimate(
            flops=int(4e10), bytes_accessed=int(1e8), transcendentals=0
        ),
    )(*near_args, *far_args)


def carry_coefs(lengths, tokens):
    count = lax.axis_size("chip")
    me = lax.axis_index("chip")
    starts = jnp.arange(count, dtype=jnp.int32) * tokens
    open_chip = locate(starts - 1, lengths)[0] == locate(starts + tokens - 1, lengths)[0]
    source = jnp.arange(count)[:, None]
    between = jnp.arange(count)[None, :]
    after = (between > source) & (between < me)
    before = (between < source) & (between > me)
    forward = jnp.all(open_chip[None, :] | ~after, axis=1) & (source[:, 0] < me)
    backward = jnp.all(open_chip[None, :] | ~before, axis=1) & (source[:, 0] > me)
    return forward.astype(FLOAT), backward.astype(FLOAT)


def on_device(
    hidden_in,
    doc_lengths,
    attention_gain,
    query_weight,
    key_projection,
    value_projection,
    output_weight,
    query_down,
    query_up,
    key_down,
    key_adapter_up,
    value_down,
    value_adapter_up,
    output_down,
    output_up,
    query_feature_maps,
    key_feature_maps,
    feedforward_gain,
    gate_weight,
    up_weight,
    down_weight,
    block_cotangent,
):
    own_rows, model = hidden_in.shape
    tokens = own_rows * CORES
    core = lax.axis_index("core")
    chip = lax.axis_index("chip")
    chips = lax.axis_size("chip")
    heads = query_feature_maps.shape[0] // CORES
    kv_heads = key_projection.shape[1] // HEAD_SIZE // CORES
    group = heads // kv_heads
    q_width = heads * HEAD_SIZE
    kv_width = kv_heads * HEAD_SIZE
    rank = query_down.shape[1]

    def own_cols(value, width, which):
        return lax.dynamic_slice_in_dim(value, which * width, width, 1)

    def own_heads(value, count, which):
        return lax.dynamic_slice_in_dim(value, which * count, count, 0)

    wqkv = jnp.stack(
        [
            jnp.concatenate(
                [
                    own_cols(query_weight, q_width, which),
                    own_cols(key_projection, kv_width, which),
                    own_cols(value_projection, kv_width, which),
                ],
                axis=1,
            )
            for which in range(CORES)
        ]
    )
    wout = output_weight.reshape(CORES, q_width, -1).transpose(0, 2, 1)
    qkv_width = q_width + 2 * kv_width

    first_row = chip * tokens
    lengths = doc_lengths[0]
    seg_rows, pos_rows = locate(first_row + jnp.arange(tokens, dtype=jnp.int32), lengths)
    seg_rim = locate(first_row - SOFTMAX_KEYS + jnp.arange(SOFTMAX_KEYS, dtype=jnp.int32), lengths)[
        0
    ]
    seg_first = locate(jnp.reshape(first_row - 1, (1,)), lengths)[0][0]
    gap = 128 - SOFTMAX_KEYS
    seg_ext = jnp.concatenate([jnp.full((gap,), -2, jnp.int32), seg_rim, seg_rows])
    seg_last = seg_rows[tokens - 1]
    continuing = (seg_rows == seg_first).astype(FLOAT)[:, None]
    carry = ((jnp.arange(tokens + 128) < tokens + gap) & (seg_ext == seg_last)).astype(FLOAT)[:, None]
    seg_column, seg_line = seg_rows[:, None], seg_ext[None, :]
    forward_coefs, backward_coefs = carry_coefs(lengths, tokens)
    cosine_table, sine_table = rotation(pos_rows, HEAD_SIZE)
    query_table = own_heads(query_feature_maps, heads, core)
    key_table = own_heads(key_feature_maps, heads, core)
    query_table = jnp.concatenate([query_table, -query_table], axis=2)
    key_table = jnp.concatenate([key_table, -key_table], axis=2)
    downs = jnp.concatenate([query_down, key_down, value_down], axis=1)
    own_query_up = own_cols(query_up, q_width, core)
    own_key_up = own_cols(key_adapter_up, kv_width, core)
    own_value_up = own_cols(value_adapter_up, kv_width, core)
    own_output_down = own_heads(output_down, q_width, core)
    pad = 128 - 3 * rank
    ups = jnp.concatenate(
        [
            jnp.pad(own_query_up, ((0, 0), (0, 2 * kv_width))),
            jnp.pad(own_key_up, ((0, 0), (q_width, kv_width))),
            jnp.pad(own_value_up, ((0, 0), (q_width + kv_width, 0))),
            jnp.zeros((pad, qkv_width), BFLOAT),
        ],
        axis=0,
    )
    extent = tokens + 128
    behind = [lax.rem(chip + chips - step, chips) for step in range(1, chips)]
    ahead = [lax.rem(chip + step, chips) for step in range(1, chips)]

    def coef_rows(coefs, places):
        rows = jnp.stack([coefs[at] for at in places])
        return jnp.broadcast_to(rows[:, None, None], (chips - 1, 1, 128))

    wide_cosine, wide_sine = spread(cosine_table, 128), spread(sine_table, 128)
    wide_downs = jnp.pad(downs, ((0, 0), (0, pad)))
    wide_output_down = jnp.pad(own_output_down, ((0, 0), (0, 128 - rank)))
    wide_output_up = jnp.pad(output_up, ((0, 128 - rank), (0, 0)))
    (
        full_qkv, full_out, normed, low_rank, low_mid, residual, queries, key_ext, value_ext,
        phi_q, phi_k, attended, denominator, state, full_ff, cotangents, gathered,
    ) = front(
        chips,
        kv_heads,
        group,
        tokens,
        [
            hidden_in,
            attention_gain[None],
            feedforward_gain[None],
            wide_downs,
            ups,
            wide_cosine,
            wide_sine,
            query_table,
            key_table,
            seg_column,
            seg_line,
            continuing,
            carry,
            coef_rows(forward_coefs, behind),
            wide_output_down,
            wide_output_up,
        ],
        [wqkv, wout, gate_weight, up_weight, down_weight.T, block_cotangent],
    )
    grad_normed_ff, out_sums, ff_grads, _ = feed(gathered, cotangents, full_ff)
    rear_outs = rear(
        chips,
        kv_heads,
        group,
        rank,
        [
            grad_normed_ff,
            residual,
            block_cotangent,
            hidden_in,
            attention_gain[None],
            feedforward_gain[None],
            full_out,
            wide_output_down[:, :16],
            wide_output_up[:16],
            low_mid,
            attended,
            denominator,
            queries,
            key_ext,
            value_ext,
            phi_q,
            phi_k,
            query_table,
            key_table,
            state,
            seg_column,
            seg_line,
            continuing,
            carry,
            coef_rows(backward_coefs, ahead),
            wide_cosine,
            wide_sine,
            normed,
            low_rank,
            full_qkv,
            ups,
            wide_downs,
        ],
        [out_sums, ff_grads],
    )
    block_output, input_grad, qkv_keep, qkv_other, out_keep, out_other = rear_outs[:6]
    own_small, sib_small = rear_outs[6:10], rear_outs[10:14]
    qkv_other, out_other = qkv_other.astype(FLOAT), out_other.astype(FLOAT)

    def by_core(dim, mine, other):
        return ordered(core, mine, other, dim)

    at_key, at_value = q_width, q_width + kv_width
    query_shard = by_core(1, qkv_keep[:, :at_key], qkv_other[:, :at_key])
    key_shard = by_core(1, qkv_keep[:, at_key:at_value], qkv_other[:, at_key:at_value])
    value_shard = by_core(1, qkv_keep[:, at_value:], qkv_other[:, at_value:])
    output_shard = by_core(1, out_keep, out_other).T
    ff_shards = rear_outs[14].astype(FLOAT)
    ff_shards = ff_shards[:, 0] + ff_shards[:, 1]

    tables = by_core(0, own_small[0], sib_small[0]).reshape(CORES * heads, HEAD_SIZE, 128)
    early = own_small[1] + sib_small[1]
    late = own_small[3] + sib_small[3]
    ups_mine, ups_other = own_small[2], sib_small[2]

    def ups_part(row, start, stop):
        rows = slice(row * rank, (row + 1) * rank)
        return by_core(1, ups_mine[rows, start:stop], ups_other[rows, start:stop])

    downs_total = late[: 3 * rank].T
    return (
        block_output,
        input_grad,
        late[3 * rank],
        query_shard,
        key_shard,
        value_shard,
        output_shard,
        downs_total[:, :rank],
        ups_part(0, 0, at_key),
        downs_total[:, rank : 2 * rank],
        ups_part(1, at_key, at_value),
        downs_total[:, 2 * rank :],
        ups_part(2, at_value, qkv_width),
        ups_part(3, 0, at_key).T,
        early[:rank],
        tables[:, :, :FEATURE_HALF],
        tables[:, :, FEATURE_HALF:],
        early[rank],
        ff_shards[0],
        ff_shards[1],
        ff_shards[2].T,
    )


def solution(mesh):
    dp, seq, tensor = (mesh.shape[name] for name in ("dp", "seq", "tensor"))
    split = Mesh(
        mesh.devices.reshape(dp, seq // CORES, CORES, tensor), ("dp", "chip", "core", "tensor")
    )
    tok = ("dp", "chip", "core")
    in_specs = (
        P(tok, None),
        P("dp", None),
        P(),
        P(tok, "tensor"),
        P(tok, "tensor"),
        P(tok, "tensor"),
        P("tensor", tok),
        P(),
        P(None, "tensor"),
        P(),
        P(None, "tensor"),
        P(),
        P(None, "tensor"),
        P("tensor", None),
        P(),
        P("tensor", None, None),
        P("tensor", None, None),
        P(),
        P(tok, "tensor"),
        P(tok, "tensor"),
        P("tensor", tok),
        P(tok, None),
    )
    out_specs = (
        P(tok, None),
        P(tok, None),
        P(),
        P(tok, "tensor"),
        P(tok, "tensor"),
        P(tok, "tensor"),
        P("tensor", tok),
        P(),
        P(None, "tensor"),
        P(),
        P(None, "tensor"),
        P(),
        P(None, "tensor"),
        P("tensor", None),
        P(),
        P("tensor", None, None),
        P("tensor", None, None),
        P(),
        P(tok, "tensor"),
        P(tok, "tensor"),
        P("tensor", tok),
    )
    return jax.shard_map(
        on_device, mesh=split, in_specs=in_specs, out_specs=out_specs, check_vma=False
    )
```

```python
import functools

import jax
import jax.numpy as jnp
import numpy as np
from jax import lax
from jax.experimental import pallas as pl
from jax.experimental.pallas import tpu as pltpu
from jax.sharding import Mesh
from jax.sharding import PartitionSpec as P

HEAD_SIZE = 64
FEATURE_HALF = 64
SOFTMAX_KEYS = 64
CORES = 2


EPS = 1e-05
FLOAT = jnp.float32
BFLOAT = jnp.bfloat16


def ordered(which, mine, other, dim):
    return jnp.where(
        which == 0,
        jnp.concatenate([mine, other], axis=dim),
        jnp.concatenate([other, mine], axis=dim),
    )


def frequencies(head_width):
    inverse = 1.0 / 500000.0 ** (np.arange(0, head_width, 2) / head_width)
    wavelen = 2.0 * np.pi / inverse
    smooth = (8192.0 / wavelen - 1.0) / 3.0
    blended = (1.0 - smooth) * inverse / 32.0 + smooth * inverse
    return np.where(wavelen > 8192.0, inverse / 32.0, np.where(wavelen < 2048.0, inverse, blended))


def rotation(positions, head_width):
    table = np.tile(frequencies(head_width), 4)[None].astype(np.float32)
    sign = np.tile(np.repeat([-1.0, 1.0], head_width // 2), 2)[None].astype(np.float32)
    turned = positions.astype(FLOAT)[:, None] * table
    return jnp.cos(turned), jnp.sin(turned) * sign


def locate(places, lengths):
    segment, begin, end = jnp.zeros_like(places), jnp.zeros_like(places), 0
    for at in range(lengths.shape[0]):
        end = end + lengths[at]
        segment = segment + (places >= end).astype(jnp.int32)
        begin = jnp.where(places >= end, end, begin)
    return (jnp.where(places < 0, -1, segment), places - begin)


def product(left, right):
    return jnp.dot(left, right, preferred_element_type=FLOAT)


def product_t(left, right):
    return lax.dot_general(left, right, (((1,), (1,)), ((), ())), preferred_element_type=FLOAT)


def t_product(left, right):
    return lax.dot_general(left, right, (((0,), (0,)), ((), ())), preferred_element_type=FLOAT)


def dot(left, right):
    return lax.dot_general(left, right, (((1,), (0,)), ((), ())), preferred_element_type=FLOAT)


def lanes(shape):
    return lax.broadcasted_iota(jnp.int32, shape, 1)


def half_sums(rows):
    first = lax.broadcasted_iota(jnp.int32, (128, 128), 0) < FEATURE_HALF
    ones = jnp.where(first == (lanes((128, 128)) < FEATURE_HALF), 1.0, 0.0).astype(BFLOAT)
    return dot(rows, ones)


def two_softmax(mixed):
    low = lanes(mixed.shape) < FEATURE_HALF
    top = jnp.max(jnp.where(low, mixed, -jnp.inf), axis=1, keepdims=True)
    top_other = jnp.max(jnp.where(low, -jnp.inf, mixed), axis=1, keepdims=True)
    raised = jnp.exp(mixed - jnp.where(low, top, top_other))
    return (raised / half_sums(raised.astype(BFLOAT))).astype(BFLOAT)


def phi_kernel(group, q_ref, k_ref, vm_ref, fq_ref, fk_ref, phi_q_ref, phi_k_ref, state_ref):
    keys = k_ref[0]
    masked = vm_ref[0]
    for head in range(group):
        rows = q_ref[:, head * HEAD_SIZE : (head + 1) * HEAD_SIZE]
        phi_q_ref[head] = two_softmax(dot(rows, fq_ref[head]))
        phi_k = two_softmax(dot(keys, fk_ref[head]))
        phi_k_ref[head] = phi_k
        state_ref[head] = t_product(masked, phi_k).astype(BFLOAT)


def tile_masks(seg_q, seg_k, at):
    width = at + 256
    same = seg_q == seg_k[:, :width]
    row = lax.broadcasted_iota(jnp.int32, (128, 256), 0)
    col = lanes((128, 256))
    earlier = col <= row + SOFTMAX_KEYS
    window = (col > row + SOFTMAX_KEYS) & (col <= row + 128) & same[:, at:]
    return same[:, :at], window, earlier & same[:, at:]


def tile_weights(rows, phi_rows, k_ref, phi_k, at, masks):
    far, window, earlier = masks
    scale = HEAD_SIZE ** (-0.5)
    raw = product_t(rows, k_ref[0, at : at + 256])
    window_exp = jnp.where(window, jnp.exp(jnp.where(window, scale * raw, 0.0)), 0.0)
    linear = product_t(phi_rows, phi_k[: at + 256])
    near = jnp.where(earlier, linear[:, at:], window_exp)
    if at == 0:
        return window_exp, near.astype(BFLOAT)
    return window_exp, jnp.concatenate(
        [jnp.where(far, linear[:, :at], 0.0), near], axis=1
    ).astype(BFLOAT)


def intra_kernel(group, q_ref, k_ref, v_ref, phi_q_ref, phi_k_ref, seg_q_ref, seg_k_ref, num_ref):
    for at in range(0, q_ref.shape[0], 128):
        masks = tile_masks(seg_q_ref[at : at + 128], seg_k_ref[...], at)
        for head in range(group):
            rows = q_ref[at : at + 128, head * HEAD_SIZE : (head + 1) * HEAD_SIZE]
            weights = tile_weights(
                rows, phi_q_ref[head, at : at + 128], k_ref, phi_k_ref.at[head], at, masks
            )[1]
            num_ref[head, at : at + 128] = dot(weights, v_ref[0, : at + 256])


def finish_kernel(group, num_ref, phi_q_ref, state_ref, cont_ref, att_ref, den_ref):
    cont = cont_ref[...]
    den = jnp.zeros(den_ref.shape[1:], FLOAT)
    for head in range(group):
        total = num_ref[head] + cont * product_t(phi_q_ref[head], state_ref[head])
        below = total[:, HEAD_SIZE : HEAD_SIZE + 1]
        att_ref[:, head * HEAD_SIZE : (head + 1) * HEAD_SIZE] = (
            total[:, :HEAD_SIZE] / below
        ).astype(BFLOAT)
        den = jnp.where(lanes(den.shape) == head, below, den)
    den_ref[0] = den


def grad_numer_kernel(group, da_ref, att_ref, den_ref, phi_q_ref, cont_ref, dn_ref, ds_ref):
    cont = cont_ref[...]
    for head in range(group):
        cols = slice(head * HEAD_SIZE, (head + 1) * HEAD_SIZE)
        numer = da_ref[:, cols] / den_ref[0][:, head : head + 1]
        denom = -jnp.sum(numer * att_ref[:, cols].astype(FLOAT), axis=1, keepdims=True)
        high = denom.astype(BFLOAT).astype(FLOAT)
        wide = jnp.concatenate([numer, jnp.zeros_like(numer)], axis=1)
        lane = lanes(wide.shape)
        wide = jnp.where(lane == HEAD_SIZE, high, wide)
        wide = jnp.where(lane == HEAD_SIZE + 1, denom - high, wide)
        dn_ref[head] = wide.astype(BFLOAT)
        state = t_product((wide * cont).astype(BFLOAT), phi_q_ref[head])
        row = lax.broadcasted_iota(jnp.int32, state.shape, 0)
        both = state[HEAD_SIZE : HEAD_SIZE + 1] + state[HEAD_SIZE + 1 : HEAD_SIZE + 2]
        state = jnp.where(row == HEAD_SIZE, both, jnp.where(row > HEAD_SIZE, 0.0, state))
        ds_ref[head] = state.astype(BFLOAT)


def intra_back_kernel(
    group, q_ref, k_ref, v_ref, phi_q_ref, phi_k_ref, dn_ref, seg_q_ref, seg_k_ref,
    dq_ref, dk_ref, dv_ref, dphi_q_ref, dphi_k_ref,
):
    scale = HEAD_SIZE ** (-0.5)
    dk_ref[...] = jnp.zeros(dk_ref.shape, FLOAT)
    dv_ref[...] = jnp.zeros(dv_ref.shape, FLOAT)
    dphi_k_ref[...] = jnp.zeros(dphi_k_ref.shape, FLOAT)
    for at in range(0, q_ref.shape[0], 128):
        masks = tile_masks(seg_q_ref[at : at + 128], seg_k_ref[...], at)
        tile = slice(at, at + 128)
        width = at + 256
        for head in range(group):
            cols = slice(head * HEAD_SIZE, (head + 1) * HEAD_SIZE)
            rows = q_ref[tile, cols]
            phi_rows = phi_q_ref[head, tile]
            numer = dn_ref[head, tile]
            window_exp, weights = tile_weights(
                rows, phi_rows, k_ref, phi_k_ref.at[head], at, masks
            )
            grad = product_t(numer, v_ref[0, :width])
            near = grad[:, at:]
            grad_raw = (scale * near * window_exp).astype(BFLOAT)
            grad_linear = jnp.where(masks[2], near, 0.0)
            if at > 0:
                grad_linear = jnp.concatenate(
                    [jnp.where(masks[0], grad[:, :at], 0.0), grad_linear], axis=1
                )
            grad_linear = grad_linear.astype(BFLOAT)
            dv_ref[0, :width] += t_product(weights, numer)
            dphi_q_ref[head, tile] = dot(grad_linear, phi_k_ref[head, :width])
            dphi_k_ref[head, :width] += t_product(grad_linear, phi_rows)
            dq_ref[tile, cols] = dot(grad_raw, k_ref[0, at:width])
            dk_ref[0, at:width] += t_product(grad_raw, rows)


def softmax_back(phi, grad):
    wide = phi.astype(FLOAT)
    terms = grad * wide
    high = terms.astype(BFLOAT)
    low = (terms - high.astype(FLOAT)).astype(BFLOAT)
    mean = (half_sums(high) + half_sums(low)) / half_sums(phi)
    return (wide * (grad - mean)).astype(BFLOAT)


def features_back_kernel(
    group, q_ref, k_ref, v_ref, phi_q_ref, phi_k_ref, dn_ref, fq_ref, fk_ref, state_ref, ds_ref,
    cont_ref, carry_ref, dq_in, dk_in, dv_in, dphi_q_ref, dphi_k_ref,
    dq_ref, dk_ref, dv_ref, gq_ref, gk_ref,
):
    cont = cont_ref[...]
    carry = carry_ref[...]
    keys = k_ref[0]
    dk = dk_in[0]
    dv = dv_in[0]
    for head in range(group):
        cols = slice(head * HEAD_SIZE, (head + 1) * HEAD_SIZE)
        grad_state = ds_ref[head]
        phi_k = phi_k_ref[head]
        grad_q = dphi_q_ref[head] + cont * dot(dn_ref[head], state_ref[head])
        grad_k = dphi_k_ref[head] + carry * dot(v_ref[0], grad_state)
        dv = dv + carry * product_t(phi_k, grad_state)
        mixed_q = softmax_back(phi_q_ref[head], grad_q)
        mixed_k = softmax_back(phi_k, grad_k)
        dq_ref[:, cols] = dq_in[:, cols] + product_t(mixed_q, fq_ref[head])
        dk = dk + product_t(mixed_k, fk_ref[head])
        gq_ref[head] = t_product(q_ref[:, cols], mixed_q)
        gk_ref[head] = t_product(keys, mixed_k)
    dk_ref[0] = dk
    dv_ref[0] = dv


def remote(source, target, send_sem, recv_sem, **where):
    return pltpu.make_async_remote_copy(
        src_ref=source,
        dst_ref=target,
        send_sem=send_sem,
        recv_sem=recv_sem,
        device_id=where,
        device_id_type=pl.DeviceIdType.MESH,
    )


def greet(peers):
    barrier = pltpu.get_barrier_semaphore()
    for where in peers:
        pl.semaphore_signal(barrier, inc=1, device_id=where, device_id_type=pl.DeviceIdType.MESH)
    pl.semaphore_wait(barrier, len(peers))


def even_chip(chip):
    return 1 - lax.rem(chip, 2)


def slot_of(chips, chip, step):
    if chips != 4:
        return step
    even = even_chip(chip)
    return lax.rem(even * step + (1 - even) * (chips - step), chips)


def row_copies(chips, chip, source, target, send, recv):
    own = source.shape[0]

    def one(piece, step, rows, at, to):
        return remote(piece, target.at[step, rows], send.at[at], recv.at[at], chip=to)

    every = pl.ds(0, own)
    if chips != 4:
        to = [lax.rem(chip + chips - step, chips) for step in range(1, chips)]
        return [one(source, step + 1, every, step, at) for step, at in enumerate(to)], []
    even = even_chip(chip)
    beside = 3 - 2 * even
    across = chip - 1 + 2 * even
    along = chip + 2 - 4 * (chip // 2)
    upper, lower = pl.ds(0, own // 2), pl.ds(own // 2, own // 2)
    return [
        one(source, chips - beside, every, 0, across),
        one(source, 2, every, 1, along),
    ], [
        one(target.at[beside, upper], chips - beside, upper, 2, along),
        one(target.at[2, lower], beside, lower, 3, across),
    ]


def relay(copies):
    for at, copy in enumerate(copies[1]):
        copies[0][at].wait_recv()
        copy.start()


def forward_copies(chips, chip, core, source, target, send, recv):
    own = source.shape[0]
    copies = []
    for at in range(chips):
        slot = slot_of(chips, chip, at) if at > 0 else 0
        piece = target.at[slot, pl.ds(0, own)] if at > 0 else source
        copies.append(
            remote(piece, target.at[slot, pl.ds(own, own)], send.at[at], recv.at[at], core=1 - core)
        )
    return copies


def hand_over(copies, forwards):
    if copies[1]:
        forwards[1].start()
        forwards[2].start()
        for copy in copies[1]:
            copy.wait_recv()
        forwards[3].start()
    else:
        for copy, forward in zip(copies[0], forwards[1:]):
            copy.wait_recv()
            forward.start()


def feed_kernel(
    chips, x_ref, c_ref, ff_ref,
    grad_ref, out_ref, ffg_ref, got_ref, xall_ref,
    x_buf, c_buf, gg_ref, gu_ref, gd_ref, keep, sib_out, sib_in, part, stage, wide,
    load_sems, stage_sems, sib_send, sib_recv, part_send, part_recv, cross_sems, ffg_sems, free_sem,
    x_send, x_recv, xf_send, xf_recv, x_sem,
):
    core, chip, tensor = (lax.axis_index(name) for name in ("core", "chip", "tensor"))
    rows = keep.shape[2]
    count, model = x_buf.shape[1:]
    units = ff_ref.shape[2]
    gate_ref, up_ref, down_ref = (ff_ref.at[which] for which in range(3))
    sibling = {"core": 1 - core}
    greet(
        [sibling, {"tensor": 1 - tensor}]
        + [{"chip": lax.rem(chip + step, chips)} for step in range(1, chips)]
    )

    def place(step):
        return slot_of(chips, chip, step)

    def load(step, which):
        slot = lax.rem(step, 2)
        ref, buf = ((xall_ref, x_buf), (c_ref, c_buf))[which]
        return pltpu.make_async_copy(ref.at[place(step)], buf.at[slot], load_sems.at[which, slot])

    x_copies = row_copies(chips, chip, x_ref, xall_ref, x_send, x_recv)
    x_forward = forward_copies(chips, chip, core, x_ref, xall_ref, xf_send, xf_recv)
    x_local = pltpu.make_async_copy(x_ref, xall_ref.at[0, pl.ds(0, rows)], x_sem)

    def came(step):
        half = xall_ref.at[place(step), pl.ds(rows, rows)]
        remote(half, half, xf_send.at[step], xf_recv.at[step], **sibling).wait_recv()

    def advance(step):
        if chips == 4:

            @pl.when(step == 0)
            def _():
                relay(x_copies)
                x_forward[1].start()
                x_forward[2].start()

            @pl.when(step == 2)
            def _():
                for copy in x_copies[1]:
                    copy.wait_recv()
                x_forward[3].start()

        else:
            for at, copy in enumerate(x_copies[0]):

                @pl.when(step == at)
                def _(at=at, copy=copy):
                    copy.wait_recv()
                    x_forward[at + 1].start()

    def to_sibling(step):
        slot = lax.rem(step, 2)
        return remote(
            sib_out.at[slot], sib_in.at[slot], sib_send.at[slot], sib_recv.at[slot], **sibling
        )

    def stage_copy(step):
        slot = lax.rem(step, 2)
        return pltpu.make_async_copy(stage.at[slot], out_ref.at[place(step)], stage_sems.at[slot])

    def to_chip(step):
        slot = place(step)
        return remote(
            part.at[step - 1],
            got_ref.at[slot - 1],
            part_send.at[step - 1],
            part_recv.at[slot - 1],
            chip=lax.rem(chip + slot, chips),
        )

    def total(step, which):
        slot = lax.rem(step, 2)
        return keep[slot, which].astype(FLOAT) + sib_in[slot, which].astype(FLOAT)

    x_local.start()
    x_forward[0].start()
    for copy in x_copies[0]:
        copy.start()
    load(0, 1).start()
    gg_ref[...] = jnp.zeros(gg_ref.shape, FLOAT)
    gu_ref[...] = jnp.zeros(gu_ref.shape, FLOAT)
    gd_ref[...] = jnp.zeros(gd_ref.shape, FLOAT)

    def body(step, nothing):
        slot = lax.rem(step, 2)
        came(step)
        load(step, 0).start()
        load(step, 1).wait()

        @pl.when(step < chips - 1)
        def _():
            load(step + 1, 1).start()

        load(step, 0).wait()
        tokens = x_buf[slot]
        cotangent = c_buf[slot]
        gate = dot(tokens, gate_ref[...])
        up = dot(tokens, up_ref[...])
        grad = dot(cotangent, down_ref[...])
        sigmoid = 1.0 / (1.0 + jnp.exp(-gate))
        silu = gate * sigmoid
        hidden = (silu * up).astype(BFLOAT)
        grad_gate = (grad * up * (sigmoid + silu * (1.0 - sigmoid))).astype(BFLOAT)
        grad_up = (grad * silu).astype(BFLOAT)

        @pl.when(step >= 2)
        def _():
            to_sibling(step).wait_send()
            pl.semaphore_wait(free_sem, 1)

        @pl.when(step > 0)
        def _():
            advance(step)

        def back(part_of):
            return (
                product_t(grad_gate[part_of], gate_ref[...])
                + product_t(grad_up[part_of], up_ref[...])
            ).astype(BFLOAT)

        def out(part_of):
            return product_t(hidden[part_of], down_ref[...]).astype(BFLOAT)

        mine, theirs = slice(0, rows), slice(rows, 2 * rows)
        sib_out[slot, 0] = back(theirs)
        sib_out[slot, 1] = out(theirs)
        to_sibling(step).start()
        keep[slot, 0] = back(mine)
        keep[slot, 1] = out(mine)

        @pl.when(step > 0)
        def _():
            before = step - 1
            to_sibling(before).wait_recv()

            @pl.when(before == 0)
            def _():
                grad_ref[...] = total(before, 0)

            @pl.when(before > 0)
            def _():
                part[before - 1] = total(before, 0).astype(BFLOAT)
                to_chip(before).start()

            @pl.when(step > 2)
            def _():
                stage_copy(before).wait()

            stage[lax.rem(before, 2)] = total(before, 1).astype(BFLOAT)
            stage_copy(before).start()
            pl.semaphore_signal(free_sem, inc=1, device_id=sibling, device_id_type=pl.DeviceIdType.MESH)

        gg_ref[...] += t_product(tokens, grad_gate)
        gu_ref[...] += t_product(tokens, grad_up)
        gd_ref[...] += t_product(cotangent, hidden)

        @pl.when(step == 0)
        def _():
            advance(step)

        return nothing

    x_local.wait()
    lax.fori_loop(0, chips, body, 0)
    last = chips - 1
    to_sibling(last).wait_recv()
    part[last - 1] = total(last, 0).astype(BFLOAT)
    to_chip(last).start()
    if chips > 2:
        stage_copy(last).wait()
    stage[last % 2] = total(last, 1).astype(BFLOAT)
    stage_copy(last).start()
    per = model // units
    ffg_copies = []
    for which, ref in enumerate((gg_ref, gu_ref, gd_ref)):
        for at in range(model // count):
            place_at = which * (model // count) + at
            buf = (x_buf, c_buf)[place_at // (2 * per)]
            spot = buf.at[(place_at // per) % 2, :, pl.ds((place_at % per) * units, units)]
            piece = pl.ds(at * count, count)
            spot[...] = ref[piece].astype(BFLOAT)
            copy = pltpu.make_async_copy(spot, ffg_ref.at[which, piece], ffg_sems.at[place_at])
            copy.start()
            ffg_copies.append(copy)

    def finish(step, nothing):
        to_chip(step).wait_recv()
        fetch = pltpu.make_async_copy(got_ref.at[place(step) - 1], wide.at[0], load_sems.at[0, 0])
        fetch.start()
        fetch.wait()
        grad_ref[...] += wide[0].astype(FLOAT)
        return nothing

    lax.fori_loop(1, chips, finish, 0)
    wide[0] = grad_ref[...].astype(BFLOAT)
    across = remote(wide.at[0], wide.at[1], cross_sems.at[0], cross_sems.at[1], tensor=1 - tensor)
    across.start()

    def drain(step, nothing):
        to_chip(step).wait_send()
        return nothing

    lax.fori_loop(1, chips, drain, 0)
    for copy in x_copies[0] + x_copies[1] + x_forward:
        copy.wait_send()
    for copy in ffg_copies:
        copy.wait()
    for step in range(max(0, chips - 2), chips):
        to_sibling(step).wait_send()
        stage_copy(step).wait()
    pl.semaphore_wait(free_sem, min(1, chips - 1))
    across.wait()
    grad_ref[...] = wide[0].astype(FLOAT) + wide[1].astype(FLOAT)


def feed(tokens, cotangent, weights):
    chips, count, model = cotangent.shape
    rows = count // CORES
    units = weights.shape[2]
    near = pl.BlockSpec(memory_space=pltpu.VMEM)
    far = pl.BlockSpec(memory_space=pl.ANY)
    return pl.pallas_call(
        functools.partial(feed_kernel, chips),
        in_specs=[far, far, near],
        out_specs=[near, far, far, far, far],
        out_shape=[
            jax.ShapeDtypeStruct((rows, model), FLOAT),
            jax.ShapeDtypeStruct((chips, rows, model), BFLOAT),
            jax.ShapeDtypeStruct(weights.shape, BFLOAT),
            jax.ShapeDtypeStruct((chips - 1, rows, model), BFLOAT),
            jax.ShapeDtypeStruct((chips, count, model), BFLOAT),
        ],
        scratch_shapes=[
            pltpu.VMEM((2, count, model), BFLOAT),
            pltpu.VMEM((2, count, model), BFLOAT),
            pltpu.VMEM((model, units), FLOAT),
            pltpu.VMEM((model, units), FLOAT),
            pltpu.VMEM((model, units), FLOAT),
            pltpu.VMEM((2, 2, rows, model), BFLOAT),
            pltpu.VMEM((2, 2, rows, model), BFLOAT),
            pltpu.VMEM((2, 2, rows, model), BFLOAT),
            pltpu.VMEM((chips - 1, rows, model), BFLOAT),
            pltpu.VMEM((2, rows, model), BFLOAT),
            pltpu.VMEM((2, rows, model), BFLOAT),
            pltpu.SemaphoreType.DMA((2, 2)),
            dma_row(2),
            dma_row(2),
            dma_row(2),
            dma_row(chips - 1),
            dma_row(chips - 1),
            dma_row(2),
            dma_row(3 * model // count),
            pltpu.SemaphoreType.REGULAR,
            dma_row(chips),
            dma_row(chips),
            dma_row(chips),
            dma_row(chips),
            pltpu.SemaphoreType.DMA,
        ],
        compiler_params=pltpu.CompilerParams(
            vmem_limit_bytes=62 * 1024 * 1024, collective_id=1, has_side_effects=True
        ),
        cost_estimate=pl.CostEstimate(
            flops=18 * chips * count * model * units,
            bytes_accessed=8 * chips * count * model,
            transcendentals=0,
        ),
    )(tokens, cotangent, weights)


def dma_row(count):
    return pltpu.SemaphoreType.DMA((count,))


def front_kernel(
    chips, kv_heads, group,
    hid_ref, again_ref, fgain_ref, downs_ref, ups_ref, cos_ref, sin_ref, fq_ref, fk_ref,
    seg_q_ref, seg_k_ref, cont_ref, carry_ref, coef_ref, odown_ref, oup_ref,
    wqkv_ref, wo_ref, gate_ref, up_ref, down_ref, cot_ref,
    qkv_ref, wof_ref, normed_ref, low_ref, mid_ref, res_ref, q_ref, k_ref, v_ref,
    phi_q_ref, phi_k_ref, att_ref, den_ref, state_ref,
    xn, ff_ref, call_ref,
    hid_sib, vm, rim_out, rim_in, st_out, st_in, num, br_out, br_in, tz_out, tz_in,
    hid_sem, q1_send, q1_recv, q2_send, q2_recv, o1_send, o1_recv, o2_send, o2_recv,
    ff_send, ff_recv, local_sems, c_send, c_recv, cf_send, cf_recv,
    rim_sem, st_send, st_recv, br_sem, tz_sem,
):
    dp, chip, core, tensor = (lax.axis_index(name) for name in ("dp", "chip", "core", "tensor"))
    own = hid_ref.shape[0]
    tokens = CORES * own
    model = hid_ref.shape[1]
    shard = wqkv_ref.shape[1]
    q_width = q_ref.shape[1]
    pairs = CORES * chips
    units = ff_ref.shape[2]
    other = 1 - core
    there = 1 - dp
    sibling = {"core": other}
    at_chip = [lax.rem(chip + step, chips) for step in range(1, chips)]
    behind = [lax.rem(chip + chips - step, chips) for step in range(1, chips)]
    greet(
        [sibling, {"tensor": 1 - tensor}]
        + [{"dp": there, "core": core}, {"dp": there, "core": other}]
        + [{"chip": to, "core": which} for to in at_chip for which in (core, other)]
        + [{"dp": there, "chip": to, "core": which} for to in at_chip for which in (core, other)]
    )

    def first(source, target, send, recv):
        rows = pl.ds(((dp * chips + chip) * CORES + core) * shard, shard)
        return [
            remote(source.at[other], target.at[rows], send.at[0], recv.at[0], core=other),
            remote(source.at[core], target.at[rows], send.at[1], recv.at[1], dp=there),
            remote(source.at[other], target.at[rows], send.at[2], recv.at[2], dp=there, core=other),
        ]

    def local(source, target, at):
        rows = pl.ds(((dp * chips + chip) * CORES + core) * shard, shard)
        return pltpu.make_async_copy(source.at[core], target.at[rows], local_sems.at[at])

    def second(target, send, recv, side):
        group_at = dp if side == 0 else there
        rows = pl.ds((group_at * chips + chip) * CORES * shard, CORES * shard)
        return [
            remote(target.at[rows], target.at[rows], send.at[side, at], recv.at[side, at], chip=to)
            for at, to in enumerate(at_chip)
        ]

    q_first = first(wqkv_ref, qkv_ref, q1_send, q1_recv)
    o_first = first(wo_ref, wof_ref, o1_send, o1_recv)
    q_local, o_local = local(wqkv_ref, qkv_ref, 0), local(wo_ref, wof_ref, 1)
    q_second = [second(qkv_ref, q2_send, q2_recv, side) for side in range(2)]
    o_second = [second(wof_ref, o2_send, o2_recv, side) for side in range(2)]
    hid_copy = remote(hid_ref, hid_sib, hid_sem.at[0], hid_sem.at[1], **sibling)
    q_local.start()
    hid_copy.start()
    for copy in q_first:
        copy.start()
    o_local.start()
    for copy in o_first:
        copy.start()

    ff_rows = pl.ds(((dp * chips + chip) * CORES + core) * shard, shard)
    ff_sources = (gate_ref, up_ref, down_ref)

    def ff_copy(which, step, side):
        to = lax.rem(chip * CORES + core + step, pairs)
        return remote(
            ff_sources[which].at[:, pl.ds(pl.multiple_of(to * units, units), units)],
            ff_ref.at[which, ff_rows],
            ff_send.at[which],
            ff_recv.at[which],
            dp=dp if side == 0 else there,
            chip=to // CORES,
            core=lax.rem(to, CORES),
        )

    def ff_local(which):
        return pltpu.make_async_copy(
            ff_sources[which].at[:, pl.ds(pl.multiple_of((chip * CORES + core) * units, units), units)],
            ff_ref.at[which, ff_rows],
            local_sems.at[2 + which],
        )

    def ff_start(which, side):
        def one(step, nothing):
            ff_copy(which, step, side).start()
            return nothing

        lax.fori_loop(1 - side, pairs, one, 0)

    c_copies = row_copies(chips, chip, cot_ref, call_ref, c_send, c_recv)
    c_forward = forward_copies(chips, chip, core, cot_ref, call_ref, cf_send, cf_recv)
    c_local = pltpu.make_async_copy(cot_ref, call_ref.at[0, pl.ds(0, own)], local_sems.at[5])

    def normalized(rows, gain):
        return (rows * lax.rsqrt(jnp.mean(rows * rows, axis=1, keepdims=True) + EPS) * gain).astype(BFLOAT)

    ff_start(0, 1)
    for which in range(3):
        ff_local(which).start()
    c_local.start()
    hidden = hid_ref[...].astype(FLOAT)
    normed_ref[pl.ds(pl.multiple_of(core * own, own), own)] = normalized(hidden, again_ref[...])
    q_first[0].wait_recv()
    q_local.wait()
    for copy in q_second[0]:
        copy.start()
    hid_copy.wait()
    normed_ref[pl.ds(pl.multiple_of(other * own, own), own)] = normalized(
        hid_sib[...].astype(FLOAT), again_ref[...]
    )
    low_ref[...] = dot(normed_ref[...], downs_ref[...]).astype(BFLOAT)
    q_first[1].wait_recv()
    q_first[2].wait_recv()
    for copy in q_second[1]:
        copy.start()
    o_first[0].wait_recv()
    o_local.wait()
    for copy in o_second[0]:
        copy.start()
    for side in range(2):
        for copy in q_second[side]:
            copy.wait_recv()
    ff_start(0, 0)
    ff_start(1, 1)

    pre = dot(normed_ref[...], qkv_ref[...]) + dot(low_ref[...], ups_ref[...])
    half = HEAD_SIZE // 2
    first_half = lax.rem(lanes((tokens, 128)), HEAD_SIZE) < half

    def rotated(block):
        turned = jnp.where(first_half, pltpu.roll(block, 128 - half, 1), pltpu.roll(block, half, 1))
        return (block * cos_ref[...] + turned * sin_ref[...]).astype(BFLOAT)

    for at in range(0, q_width, 128):
        q_ref[:, at : at + 128] = rotated(pre[:, at : at + 128])
    keys = rotated(pre[:, q_width : q_width + 128])
    values = pre[:, q_width + 128 :].astype(BFLOAT)
    rim_out[:, :128] = keys[tokens - SOFTMAX_KEYS :]
    rim_out[:, 128:] = values[tokens - SOFTMAX_KEYS :]
    rim_copy = remote(rim_out, rim_in, rim_sem.at[0], rim_sem.at[1], chip=lax.rem(chip + 1, chips))

    @pl.when(chip < chips - 1)
    def _():
        rim_copy.start()

    def tailed(rows):
        tail = jnp.where(lanes((rows.shape[0], 128 - HEAD_SIZE)) < 2, 1.0, 0.0).astype(BFLOAT)
        return jnp.concatenate([rows, tail], axis=1)

    gap = 128 - SOFTMAX_KEYS
    for head in range(kv_heads):
        cols = slice(head * HEAD_SIZE, (head + 1) * HEAD_SIZE)
        k_ref[head, 128:] = keys[:, cols]
        v_ref[head, 128:] = tailed(values[:, cols])
        k_ref[head, :gap] = jnp.zeros((gap, HEAD_SIZE), BFLOAT)
        v_ref[head, :gap] = tailed(jnp.zeros((gap, HEAD_SIZE), BFLOAT))

    @pl.when(chip == 0)
    def _():
        rim_in[...] = jnp.zeros(rim_in.shape, BFLOAT)

    @pl.when(chip > 0)
    def _():
        rim_copy.wait_recv()

    carry = carry_ref[...]
    for head in range(kv_heads):
        cols = slice(head * HEAD_SIZE, (head + 1) * HEAD_SIZE)
        k_ref[head, gap:128] = rim_in[:, cols]
        v_ref[head, gap:128] = tailed(rim_in[:, 128 + head * HEAD_SIZE : 128 + (head + 1) * HEAD_SIZE])
        vm[head] = (v_ref[head].astype(FLOAT) * carry).astype(BFLOAT)

    def views(at):
        heads = pl.ds(at * group, group)
        one = pl.ds(at, 1)
        wide = pl.ds(at * group * HEAD_SIZE, group * HEAD_SIZE)
        return heads, one, wide

    for at in range(kv_heads):
        heads, one, wide = views(at)
        phi_kernel(
            group, q_ref.at[:, wide], k_ref.at[one], vm.at[one], fq_ref.at[heads], fk_ref.at[heads],
            phi_q_ref.at[heads], phi_k_ref.at[heads], st_out.at[heads],
        )
    kept = HEAD_SIZE + 16
    st_copies = [
        remote(st_out.at[:, pl.ds(0, kept)], st_in.at[at], st_send.at[at], st_recv.at[at], chip=to)
        for at, to in enumerate(at_chip)
    ]
    for copy in st_copies:
        copy.start()
    o_first[1].wait_recv()
    o_first[2].wait_recv()
    for copy in o_second[1]:
        copy.start()
    ff_start(1, 0)
    c_forward[0].start()
    for copy in c_copies[0]:
        copy.start()
    for at in range(kv_heads):
        heads, one, wide = views(at)
        intra_kernel(
            group, q_ref.at[:, wide], k_ref.at[one], v_ref.at[one], phi_q_ref.at[heads],
            phi_k_ref.at[heads], seg_q_ref, seg_k_ref, num.at[heads],
        )
    total = jnp.zeros(st_in.shape[1:], FLOAT)
    for at, copy in enumerate(st_copies):
        copy.wait_recv()
        total = total + coef_ref[at] * st_in[at].astype(FLOAT)
    state_ref[:, :kept] = total.astype(BFLOAT)
    state_ref[:, kept:] = jnp.zeros((state_ref.shape[0], 128 - kept, 128), BFLOAT)
    for at in range(kv_heads):
        heads, one, wide = views(at)
        finish_kernel(
            group, num.at[heads], phi_q_ref.at[heads], state_ref.at[heads], cont_ref,
            att_ref.at[:, wide], den_ref.at[one],
        )

    for side in range(2):
        for copy in o_second[side]:
            copy.wait_recv()

    def branch(which, target):
        rows = att_ref[pl.ds(pl.multiple_of(which * own, own), own)]
        return product_t(rows, wof_ref[...]), dot(rows, odown_ref[...])

    wide_part, low_part = branch(other, None)
    br_out[:, :model] = wide_part.astype(BFLOAT)
    br_out[:, model:] = low_part.astype(BFLOAT)
    br_copy = remote(br_out, br_in, br_sem.at[0], br_sem.at[1], **sibling)
    br_copy.start()
    wide_part, low_part = branch(core, None)
    br_copy.wait_recv()
    tz_out[:, :model] = (wide_part + br_in[:, :model].astype(FLOAT)).astype(BFLOAT)
    tz_out[:, model:] = (low_part + br_in[:, model:].astype(FLOAT)).astype(BFLOAT)
    tz_copy = remote(tz_out, tz_in, tz_sem.at[0], tz_sem.at[1], tensor=1 - tensor)
    tz_copy.start()
    ff_start(2, 1)
    tz_copy.wait_recv()
    relay(c_copies)
    ff_start(2, 0)
    mid = (tz_out[:, model:].astype(FLOAT) + tz_in[:, model:].astype(FLOAT)).astype(BFLOAT)
    mid_ref[...] = mid
    residual = (
        hid_ref[...].astype(FLOAT)
        + (tz_out[:, :model].astype(FLOAT) + tz_in[:, :model].astype(FLOAT))
        + dot(mid, oup_ref[...])
    )
    res_ref[...] = residual
    xn[...] = normalized(residual, fgain_ref[...])
    hand_over(c_copies, c_forward)

    hid_done = [br_copy, tz_copy] + q_first + o_first + q_second[0] + q_second[1]
    for copy in hid_done + o_second[0] + o_second[1] + st_copies + c_copies[0] + c_copies[1]:
        copy.wait_send()

    @pl.when(chip < chips - 1)
    def _():
        rim_copy.wait_send()

    for copy in c_forward:
        copy.wait()
    c_local.wait()
    moved = (2 * pairs - 1) * shard
    for which in range(3):
        ff_local(which).wait()
        every = ff_ref.at[which, pl.ds(0, moved)]
        remote(every, every, ff_send.at[which], ff_recv.at[which], **sibling).wait()


def front(
    chips, kv_heads, group, tokens, near_args, far_args
):
    own, model = near_args[0].shape
    heads = kv_heads * group
    q_width = heads * HEAD_SIZE
    qkv_width = q_width + 2 * kv_heads * HEAD_SIZE
    extent = tokens + 128
    units = far_args[2].shape[1] // (chips * CORES)
    near = pl.BlockSpec(memory_space=pltpu.VMEM)
    far = pl.BlockSpec(memory_space=pl.ANY)
    kept = HEAD_SIZE + 16
    near_outs = [
        ((model, qkv_width), BFLOAT),
        ((model, q_width), BFLOAT),
        ((tokens, model), BFLOAT),
        ((tokens, 128), BFLOAT),
        ((own, 128), BFLOAT),
        ((own, model), FLOAT),
        ((tokens, q_width), BFLOAT),
        ((kv_heads, extent, HEAD_SIZE), BFLOAT),
        ((kv_heads, extent, 128), BFLOAT),
        ((heads, tokens, 128), BFLOAT),
        ((heads, extent, 128), BFLOAT),
        ((tokens, q_width), BFLOAT),
        ((kv_heads, tokens, 128), FLOAT),
        ((heads, 128, 128), BFLOAT),
        ((own, model), BFLOAT),
    ]
    far_outs = [
        ((3, model, units), BFLOAT),
        ((chips, tokens, model), BFLOAT),
    ]
    pair = dma_row(2)
    return pl.pallas_call(
        functools.partial(front_kernel, chips, kv_heads, group),
        in_specs=[near] * len(near_args) + [far] * len(far_args),
        out_specs=[near] * len(near_outs) + [far] * len(far_outs),
        out_shape=[jax.ShapeDtypeStruct(*out) for out in near_outs + far_outs],
        scratch_shapes=[
            pltpu.VMEM((own, model), BFLOAT),
            pltpu.VMEM((kv_heads, extent, 128), BFLOAT),
            pltpu.VMEM((SOFTMAX_KEYS, 256), BFLOAT),
            pltpu.VMEM((SOFTMAX_KEYS, 256), BFLOAT),
            pltpu.VMEM((heads, 128, 128), BFLOAT),
            pltpu.VMEM((chips - 1, heads, kept, 128), BFLOAT),
            pltpu.VMEM((heads, tokens, 128), FLOAT),
            pltpu.VMEM((own, model + 128), BFLOAT),
            pltpu.VMEM((own, model + 128), BFLOAT),
            pltpu.VMEM((own, model + 128), BFLOAT),
            pltpu.VMEM((own, model + 128), BFLOAT),
            pair,
            dma_row(3),
            dma_row(3),
            pltpu.SemaphoreType.DMA((2, chips - 1)),
            pltpu.SemaphoreType.DMA((2, chips - 1)),
            dma_row(3),
            dma_row(3),
            pltpu.SemaphoreType.DMA((2, chips - 1)),
            pltpu.SemaphoreType.DMA((2, chips - 1)),
            dma_row(3),
            dma_row(3),
            dma_row(7),
            dma_row(chips),
            dma_row(chips),
            dma_row(chips),
            dma_row(chips),
            pair,
            dma_row(chips - 1),
            dma_row(chips - 1),
            pair,
            pair,
        ],
        compiler_params=pltpu.CompilerParams(
            vmem_limit_bytes=60 * 1024 * 1024, collective_id=2, has_side_effects=True
        ),
        cost_estimate=pl.CostEstimate(
            flops=int(1e10), bytes_accessed=int(1e8), transcendentals=0
        ),
    )(*near_args, *far_args)


def rear_kernel(
    chips, kv_heads, group, rank,
    gnf_ref, res_ref, cot_ref, hid_ref, again_ref, fgain_ref, wof_ref, odown_ref, oup_ref, mid_ref,
    att_ref, den_ref, q_ref, k_ref, v_ref, phi_q_ref, phi_k_ref, fq_ref, fk_ref, state_ref,
    seg_q_ref, seg_k_ref, cont_ref, carry_ref, coef_ref, cos_ref, sin_ref,
    normed_ref, low_ref, qkv_ref, ups_ref, downs_ref,
    out_ref, ffg_ref,
    block_ref, igrad_ref, qkv_own, qkv_sib, o_own, o_sib,
    tab_own, early_own, ups_own, late_own, tab_sib, early_sib, ups_sib, late_sib,
    ffin_ref, oin_ref,
    db, dq, dn, ds_out, ds_in, gstate, dk, dv, dphi_q, dphi_k, gq, gk, dres,
    rim_out, rim_in, gp, br_out, br_in, tz_in,
    qg, q_in, q_dp_out, q_dp_in, q_core, og, o_in, o_dp_out, o_dp_in, o_core,
    tab_slots, early_slots, ups_slots, late_slots,
    tab_dp, early_dp, ups_dp, late_dp,
    db_sem, ds_send, ds_recv, rim_sem, br_sem, tz_sem, oz_sem, o_load, os_send, os_recv,
    q_send, q_recv, q_dp_sem, q_core_sem, o_send, o_recv, o_dp_sem, o_core_sem,
    small_send, small_recv, small_dp, small_core,
    ff_send, ff_recv, local_sems,
):
    dp, chip, core, tensor = (lax.axis_index(name) for name in ("dp", "chip", "core", "tensor"))
    own, model = gnf_ref.shape
    tokens = CORES * own
    q_width = q_ref.shape[1]
    pairs = CORES * chips
    shard = model // (2 * pairs)
    units = ffg_ref.shape[2]
    other = 1 - core
    there = 1 - dp
    sibling = {"core": other}
    at_chip = [lax.rem(chip + step, chips) for step in range(1, chips)]
    greet(
        [sibling, {"tensor": 1 - tensor}]
        + [{"dp": there, "core": core}, {"dp": there, "core": other}]
        + [{"chip": to, "core": which} for to in at_chip for which in (core, other)]
        + [{"dp": there, "chip": to, "core": which} for to in at_chip for which in (core, other)]
    )
    mine = pl.ds(pl.multiple_of(core * own, own), own)
    theirs = pl.ds(pl.multiple_of(other * own, own), own)

    def ff_start(which, side):
        def one(step, nothing):
            to = lax.rem(chip * CORES + core + step, pairs)
            group_to = dp if side == 0 else there
            remote(
                ffg_ref.at[which, pl.ds((group_to * pairs + to) * shard, shard)],
                ffin_ref.at[which, dp, :, pl.ds(pl.multiple_of((chip * CORES + core) * units, units), units)],
                ff_send.at[which, side],
                ff_recv.at[which, side],
                dp=group_to,
                chip=to // CORES,
                core=lax.rem(to, CORES),
            ).start()
            return nothing

        lax.fori_loop(1 - side, pairs, one, 0)

    def ff_local(which):
        at = chip * CORES + core
        return pltpu.make_async_copy(
            ffg_ref.at[which, pl.ds((dp * pairs + at) * shard, shard)],
            ffin_ref.at[which, dp, :, pl.ds(pl.multiple_of(at * units, units), units)],
            local_sems.at[which],
        )

    os_copies = [
        remote(out_ref.at[at + 1], oin_ref.at[at], os_send.at[at], os_recv.at[at], chip=to)
        for at, to in enumerate(at_chip)
    ]

    def norm_back_rows(inputs, gain, grad):
        scale = lax.rsqrt(jnp.mean(inputs * inputs, axis=1, keepdims=True) + EPS)
        weighted = grad * gain
        back = scale * weighted - inputs * (
            scale * scale * scale * jnp.mean(weighted * inputs, axis=1, keepdims=True)
        )
        return back, jnp.sum(grad * inputs * scale, axis=0, keepdims=True)

    slots = (tab_slots, early_slots, ups_slots, late_slots)
    dp_bufs = (tab_dp, early_dp, ups_dp, late_dp)
    owns = (tab_own, early_own, ups_own, late_own)
    sibs = (tab_sib, early_sib, ups_sib, late_sib)

    def small_copies(which):
        return [
            remote(
                slots[which].at[chip], slots[which].at[chip],
                small_send.at[which, at], small_recv.at[which, at], chip=to,
            )
            for at, to in enumerate(at_chip)
        ]

    def small_start(which, value):
        slots[which][chip] = value.astype(BFLOAT)
        for copy in small_copies(which):
            copy.start()

    def small_across(which):
        return remote(
            dp_bufs[which].at[0], dp_bufs[which].at[1],
            small_dp.at[which, 0], small_dp.at[which, 1], dp=there,
        )

    def small_over(which):
        return remote(owns[which], sibs[which], small_core.at[which, 0], small_core.at[which, 1], **sibling)

    def small_middle(which):
        for copy in small_copies(which):
            copy.wait()
        total = slots[which][0].astype(FLOAT)
        for at in range(1, chips):
            total = total + slots[which][at].astype(FLOAT)
        dp_bufs[which][0] = total.astype(BFLOAT)
        small_across(which).start()

    def small_end(which):
        small_across(which).wait()
        owns[which][...] = dp_bufs[which][0].astype(FLOAT) + dp_bufs[which][1].astype(FLOAT)
        small_over(which).start()

    def grad_copies(source, target, send, recv):
        return [
            remote(
                source.at[pl.ds(((dp if side == 0 else there) * chips + to) * CORES * shard, CORES * shard)],
                target.at[at, side],
                send.at[side, at],
                recv.at[side, at],
                chip=to,
            )
            for at, to in enumerate(at_chip)
            for side in range(2)
        ]

    q_copies = grad_copies(qg, q_in, q_send, q_recv)
    o_copies = grad_copies(og, o_in, o_send, o_recv)
    q_across = remote(q_dp_out, q_dp_in, q_dp_sem.at[0], q_dp_sem.at[1], dp=there)
    o_across = remote(o_dp_out, o_dp_in, o_dp_sem.at[0], o_dp_sem.at[1], dp=there)
    q_over = remote(q_core, qkv_sib, q_core_sem.at[0], q_core_sem.at[1], **sibling)
    o_over = remote(o_core, o_sib, o_core_sem.at[0], o_core_sem.at[1], **sibling)

    def chip_sum(source, target, side):
        group_at = dp if side == 0 else there
        total = source[pl.ds((group_at * chips + chip) * CORES * shard, CORES * shard)].astype(FLOAT)
        for at in range(chips - 1):
            total = total + target[at, side].astype(FLOAT)
        return total

    def grads_middle(copies, source, target, dp_out, across):
        for copy in copies:
            copy.wait_recv()
        dp_out[...] = chip_sum(source, target, 1).astype(BFLOAT)
        across.start()

    def grads_end(source, target, dp_in, across, result, core_out, over):
        across.wait()
        total = chip_sum(source, target, 0) + dp_in[...].astype(FLOAT)
        upper, lower = total[shard:], total[:shard]
        result[...] = jnp.where(core == 0, lower, upper)
        core_out[...] = jnp.where(core == 0, upper, lower).astype(BFLOAT)
        over.start()

    back_rows, gain_row = norm_back_rows(res_ref[...], fgain_ref[...], gnf_ref[...])
    grad_residual = cot_ref[...].astype(FLOAT) + back_rows
    dres[...] = grad_residual
    db[mine] = grad_residual.astype(BFLOAT)
    db_copy = remote(db.at[mine], db.at[mine], db_sem.at[0], db_sem.at[1], **sibling)
    db_copy.start()
    ff_start(0, 1)
    os_copies[0].start()
    for which in range(3):
        ff_local(which).start()
    up_rows = t_product(mid_ref[...], db[mine])[:rank]
    filler = jnp.zeros((16 - 1 - rank, model), FLOAT)
    early_rows = jnp.concatenate([up_rows, gain_row, filler], axis=0)
    db_copy.wait_recv()
    dmid = product_t(db[...], oup_ref[...]).astype(BFLOAT)
    dq[...] = dot(db[...], wof_ref[...]) + product_t(dmid, odown_ref[...])

    def views(at):
        return (
            pl.ds(at * group, group),
            pl.ds(at, 1),
            pl.ds(at * group * HEAD_SIZE, group * HEAD_SIZE),
        )

    for at in range(kv_heads):
        heads, one, wide = views(at)
        grad_numer_kernel(
            group, dq.at[:, wide], att_ref.at[:, wide], den_ref.at[one], phi_q_ref.at[heads], cont_ref,
            dn.at[heads], ds_out.at[heads],
        )
    kept = HEAD_SIZE + 16
    ds_copies = [
        remote(ds_out.at[:, pl.ds(0, kept)], ds_in.at[at], ds_send.at[at], ds_recv.at[at], chip=to)
        for at, to in enumerate([lax.rem(chip + chips - step, chips) for step in range(1, chips)])
    ]
    for copy in ds_copies:
        copy.start()
    small_start(1, early_rows)
    ff_start(0, 0)
    og[...] = t_product(db[...], att_ref[...]).astype(BFLOAT)
    down_rows = t_product(dmid, att_ref[...])[:rank]
    for at in range(kv_heads):
        heads, one, wide = views(at)
        intra_back_kernel(
            group, q_ref.at[:, wide], k_ref.at[one], v_ref.at[one], phi_q_ref.at[heads],
            phi_k_ref.at[heads], dn.at[heads], seg_q_ref, seg_k_ref,
            dq.at[:, wide], dk.at[one], dv.at[one], dphi_q.at[heads], dphi_k.at[heads],
        )
    total = jnp.zeros(ds_in.shape[1:], FLOAT)
    for at, copy in enumerate(ds_copies):
        copy.wait_recv()
        total = total + coef_ref[at] * ds_in[at].astype(FLOAT)
    gstate[:, :kept] = total.astype(BFLOAT)
    gstate[:, kept:] = jnp.zeros((gstate.shape[0], 128 - kept, 128), BFLOAT)
    for at in range(kv_heads):
        heads, one, wide = views(at)
        features_back_kernel(
            group, q_ref.at[:, wide], k_ref.at[one], v_ref.at[one], phi_q_ref.at[heads],
            phi_k_ref.at[heads], dn.at[heads], fq_ref.at[heads], fk_ref.at[heads],
            state_ref.at[heads], gstate.at[heads], cont_ref, carry_ref,
            dq.at[:, wide], dk.at[one], dv.at[one], dphi_q.at[heads], dphi_k.at[heads],
            dq.at[:, wide], dk.at[one], dv.at[one], gq.at[heads], gk.at[heads],
        )

    gap = 128 - SOFTMAX_KEYS

    def joined(rows):
        return jnp.concatenate(
            [dk[head, rows] for head in range(kv_heads)]
            + [dv[head, rows, :HEAD_SIZE] for head in range(kv_heads)],
            axis=1,
        )

    rim_out[...] = joined(slice(gap, 128))
    rim_copy = remote(rim_out, rim_in, rim_sem.at[0], rim_sem.at[1], chip=lax.rem(chip + chips - 1, chips))

    @pl.when(chip > 0)
    def _():
        rim_copy.start()

    tables = []
    for head in range(kv_heads * group):
        pieces = [table[head, :, :FEATURE_HALF] - table[head, :, FEATURE_HALF:] for table in (gq, gk)]
        tables.append(jnp.concatenate(pieces, axis=1))
    small_start(0, jnp.concatenate(tables, axis=0))
    for copy in o_copies:
        copy.start()
    half = HEAD_SIZE // 2
    first_half = lax.rem(lanes((tokens, 128)), HEAD_SIZE) < half

    def unrotated(block):
        turned = jnp.where(first_half, pltpu.roll(block, 128 - half, 1), pltpu.roll(block, half, 1))
        return (block * cos_ref[...] - turned * sin_ref[...]).astype(BFLOAT)

    for at in range(0, q_width, 128):
        gp[:, at : at + 128] = unrotated(dq[:, at : at + 128])

    @pl.when(chip == chips - 1)
    def _():
        rim_in[...] = jnp.zeros(rim_in.shape, FLOAT)

    @pl.when(chip < chips - 1)
    def _():
        rim_copy.wait_recv()

    kv = joined(slice(128, 128 + tokens))
    kv = jnp.concatenate(
        [kv[: tokens - SOFTMAX_KEYS], kv[tokens - SOFTMAX_KEYS :] + rim_in[...]], axis=0
    )
    gp[:, q_width : q_width + 128] = unrotated(kv[:, :128])
    gp[:, q_width + 128 :] = kv[:, 128:].astype(BFLOAT)

    def partial(rows):
        grads = gp[rows]
        return product_t(grads, qkv_ref[...]), product_t(grads, ups_ref[...])

    wide_part, low_part = partial(theirs)
    br_out[:, :model] = wide_part.astype(BFLOAT)
    br_out[:, model:] = low_part.astype(BFLOAT)
    br_copy = remote(br_out, br_in, br_sem.at[0], br_sem.at[1], **sibling)
    br_copy.start()
    wide_part, low_part = partial(mine)
    br_copy.wait()
    tz_out = br_out
    tz_out[:, :model] = (wide_part + br_in[:, :model].astype(FLOAT)).astype(BFLOAT)
    tz_out[:, model:] = (low_part + br_in[:, model:].astype(FLOAT)).astype(BFLOAT)
    tz_copy = remote(tz_out, tz_in, tz_sem.at[0], tz_sem.at[1], tensor=1 - tensor)
    tz_copy.start()
    ff_start(1, 1)
    qg[...] = t_product(normed_ref[...], gp[...]).astype(BFLOAT)
    for copy in q_copies:
        copy.start()
    ups_rows = t_product(low_ref[...], gp[...])[: 3 * rank]
    wide_down = jnp.concatenate(
        [down_rows, jnp.zeros((rank, gp.shape[1] - q_width), FLOAT)], axis=1
    )
    small_start(2, jnp.concatenate([ups_rows, wide_down], axis=0))
    tz_copy.wait_recv()
    low = (tz_out[:, model:].astype(FLOAT) + tz_in[:, model:].astype(FLOAT)).astype(BFLOAT)
    grad_normed = (
        tz_out[:, :model].astype(FLOAT) + tz_in[:, :model].astype(FLOAT)
    ) + product_t(low, downs_ref[...])
    low_rows = t_product(low, normed_ref[mine])[: 3 * rank]
    back_rows, gain_row = norm_back_rows(hid_ref[...].astype(FLOAT), again_ref[...], grad_normed)
    igrad_ref[...] = (dres[...] + back_rows).astype(BFLOAT)
    filler = jnp.zeros((rank - 1, model), FLOAT)
    small_start(3, jnp.concatenate([low_rows, gain_row, filler], axis=0))
    for copy in os_copies[1:]:
        copy.start()
    ff_start(1, 0)
    ff_start(2, 0)
    grads_middle(o_copies, og, o_in, o_dp_out, o_across)
    ff_start(2, 1)
    small_middle(1)
    small_middle(0)
    small_middle(2)
    grads_middle(q_copies, qg, q_in, q_dp_out, q_across)
    small_middle(3)

    os_buf = tz_in.at[:, pl.ds(0, model)]
    load = pltpu.make_async_copy(out_ref.at[0], os_buf, o_load.at[0])
    load.start()
    load.wait()
    dres[...] = os_buf[...].astype(FLOAT)
    for at in range(chips - 1):
        os_copies[at].wait_recv()
        load = pltpu.make_async_copy(oin_ref.at[at], os_buf, o_load.at[0])
        load.start()
        load.wait()
        dres[...] += os_buf[...].astype(FLOAT)
    tz_copy.wait_send()
    oz_out, oz_in = (ref.at[:, pl.ds(0, model)] for ref in (br_out, br_in))
    oz_out[...] = dres[...].astype(BFLOAT)
    oz_copy = remote(oz_out, oz_in, oz_sem.at[0], oz_sem.at[1], tensor=1 - tensor)
    oz_copy.start()
    grads_end(og, o_in, o_dp_in, o_across, o_own, o_core, o_over)
    for which in range(3):
        small_end(which)
    oz_copy.wait()
    block_ref[...] = (
        res_ref[...] + (oz_out[...].astype(FLOAT) + oz_in[...].astype(FLOAT))
    ).astype(BFLOAT)
    grads_end(qg, q_in, q_dp_in, q_across, qkv_own, q_core, q_over)
    small_end(3)

    for copy in [db_copy] + ds_copies + os_copies + q_copies + o_copies:
        copy.wait_send()

    @pl.when(chip > 0)
    def _():
        rim_copy.wait_send()

    for which in range(4):
        small_over(which).wait()
    q_over.wait()
    o_over.wait()
    for which in range(3):
        ff_local(which).wait()
        for side in range(2):
            count = pairs - 1 + side
            group_from = dp if side == 0 else there
            sent = ffg_ref.at[which, pl.ds(0, count * shard)]
            came = ffin_ref.at[which, group_from, :, pl.ds(0, count * units)]
            remote(sent, sent, ff_send.at[which, side], ff_recv.at[which, side], **sibling).wait_send()
            remote(came, came, ff_send.at[which, side], ff_recv.at[which, side], **sibling).wait_recv()


def rear(chips, kv_heads, group, rank, near_args, far_args):
    own, model = near_args[0].shape
    tokens = CORES * own
    heads = kv_heads * group
    q_width = heads * HEAD_SIZE
    qkv_width = q_width + 2 * kv_heads * HEAD_SIZE
    extent = tokens + 128
    pairs = chips * CORES
    shard = model // (2 * pairs)
    units = far_args[1].shape[2]
    near = pl.BlockSpec(memory_space=pltpu.VMEM)
    far = pl.BlockSpec(memory_space=pl.ANY)
    kept = HEAD_SIZE + 16
    smalls = [
        (heads * HEAD_SIZE, 128),
        (16, model),
        (4 * rank, qkv_width),
        (4 * rank, model),
    ]
    near_outs = [
        ((own, model), BFLOAT),
        ((own, model), BFLOAT),
        ((shard, qkv_width), FLOAT),
        ((shard, qkv_width), BFLOAT),
        ((shard, q_width), FLOAT),
        ((shard, q_width), BFLOAT),
    ]
    near_outs += [(shape, FLOAT) for shape in smalls] * 2
    far_outs = [
        ((3, 2, shard, pairs * units), BFLOAT),
        ((chips - 1, own, model), BFLOAT),
    ]
    pair = dma_row(2)
    step_pair = pltpu.SemaphoreType.DMA((2, chips - 1))

    def grads(width):
        return [
            pltpu.VMEM((model, width), BFLOAT),
            pltpu.VMEM((chips - 1, 2, CORES * shard, width), BFLOAT),
            pltpu.VMEM((CORES * shard, width), BFLOAT),
            pltpu.VMEM((CORES * shard, width), BFLOAT),
            pltpu.VMEM((shard, width), BFLOAT),
        ]

    wide = pltpu.VMEM((own, model + 128), BFLOAT)
    return pl.pallas_call(
        functools.partial(rear_kernel, chips, kv_heads, group, rank),
        in_specs=[near] * len(near_args) + [far] * len(far_args),
        out_specs=[near] * len(near_outs) + [far] * len(far_outs),
        out_shape=[jax.ShapeDtypeStruct(*out) for out in near_outs + far_outs],
        scratch_shapes=[
            pltpu.VMEM((tokens, model), BFLOAT),
            pltpu.VMEM((tokens, q_width), FLOAT),
            pltpu.VMEM((heads, tokens, 128), BFLOAT),
            pltpu.VMEM((heads, 128, 128), BFLOAT),
            pltpu.VMEM((chips - 1, heads, kept, 128), BFLOAT),
            pltpu.VMEM((heads, 128, 128), BFLOAT),
            pltpu.VMEM((kv_heads, extent, HEAD_SIZE), FLOAT),
            pltpu.VMEM((kv_heads, extent, 128), FLOAT),
            pltpu.VMEM((heads, tokens, 128), FLOAT),
            pltpu.VMEM((heads, extent, 128), FLOAT),
            pltpu.VMEM((heads, HEAD_SIZE, 128), FLOAT),
            pltpu.VMEM((heads, HEAD_SIZE, 128), FLOAT),
            pltpu.VMEM((own, model), FLOAT),
            pltpu.VMEM((SOFTMAX_KEYS, 256), FLOAT),
            pltpu.VMEM((SOFTMAX_KEYS, 256), FLOAT),
            pltpu.VMEM((tokens, qkv_width), BFLOAT),
            wide,
            wide,
            wide,
        ]
        + grads(qkv_width)
        + grads(q_width)
        + [pltpu.VMEM((chips,) + shape, BFLOAT) for shape in smalls]
        + [pltpu.VMEM((2,) + shape, BFLOAT) for shape in smalls]
        + [
            pair,
            dma_row(chips - 1),
            dma_row(chips - 1),
            pair,
            pair,
            pair,
            pair,
            dma_row(1),
            dma_row(chips - 1),
            dma_row(chips - 1),
            step_pair,
            step_pair,
            pair,
            pair,
            step_pair,
            step_pair,
            pair,
            pair,
            pltpu.SemaphoreType.DMA((4, chips - 1)),
            pltpu.SemaphoreType.DMA((4, chips - 1)),
            pltpu.SemaphoreType.DMA((4, 2)),
            pltpu.SemaphoreType.DMA((4, 2)),
            pltpu.SemaphoreType.DMA((3, 2)),
            pltpu.SemaphoreType.DMA((3, 2)),
            dma_row(3),
        ],
        compiler_params=pltpu.CompilerParams(
            vmem_limit_bytes=63 * 1024 * 1024, collective_id=3, has_side_effects=True
        ),
        cost_estimate=pl.CostEstimate(
            flops=int(4e10), bytes_accessed=int(1e8), transcendentals=0
        ),
    )(*near_args, *far_args)


def carry_coefs(lengths, tokens):
    chips = lax.axis_size("chip")
    me = lax.axis_index("chip")
    steps = jnp.arange(1, chips, dtype=jnp.int32)
    behind, ahead = lax.rem(me + chips - steps, chips), lax.rem(me + steps, chips)
    places = jnp.stack(
        [behind * tokens + tokens - 1, ahead * tokens - 1, 0 * steps + me * tokens - 1]
        + [0 * steps + me * tokens + tokens - 1]
    )
    segment = locate(places, lengths)[0]
    forward = (behind < me) & (segment[0] == segment[2])
    backward = (ahead > me) & (segment[1] == segment[3])
    return [
        jnp.broadcast_to(row.astype(FLOAT)[:, None, None], (chips - 1, 1, 128))
        for row in (forward, backward)
    ]


def on_device(
    hidden_in,
    doc_lengths,
    attention_gain,
    query_weight,
    key_projection,
    value_projection,
    output_weight,
    query_down,
    query_up,
    key_down,
    key_adapter_up,
    value_down,
    value_adapter_up,
    output_down,
    output_up,
    query_feature_maps,
    key_feature_maps,
    feedforward_gain,
    gate_weight,
    up_weight,
    down_weight,
    block_cotangent,
):
    own_rows, model = hidden_in.shape
    tokens = own_rows * CORES
    core = lax.axis_index("core")
    chip = lax.axis_index("chip")
    chips = lax.axis_size("chip")
    heads = query_feature_maps.shape[0] // CORES
    kv_heads = key_projection.shape[1] // HEAD_SIZE // CORES
    group = heads // kv_heads
    q_width = heads * HEAD_SIZE
    kv_width = kv_heads * HEAD_SIZE
    rank = query_down.shape[1]

    def own_cols(value, width, which):
        return lax.dynamic_slice_in_dim(value, which * width, width, 1)

    def own_heads(value, count, which):
        return lax.dynamic_slice_in_dim(value, which * count, count, 0)

    wqkv = jnp.stack(
        [
            jnp.concatenate(
                [
                    own_cols(query_weight, q_width, which),
                    own_cols(key_projection, kv_width, which),
                    own_cols(value_projection, kv_width, which),
                ],
                axis=1,
            )
            for which in range(CORES)
        ]
    )
    wout = output_weight.reshape(CORES, q_width, -1).transpose(0, 2, 1)
    qkv_width = q_width + 2 * kv_width

    first_row = chip * tokens
    lengths = doc_lengths[0]
    gap = 128 - SOFTMAX_KEYS
    spots = jnp.arange(tokens + 128, dtype=jnp.int32)
    seg_ext, pos_ext = locate(first_row + spots - 128, lengths)
    seg_ext = jnp.where(spots < gap, -2, seg_ext)
    seg_rows, pos_rows = seg_ext[128:], pos_ext[128:]
    seg_first = locate(first_row - 1, lengths)[0]
    seg_last = locate(first_row + tokens - 1, lengths)[0]
    continuing = (seg_rows == seg_first).astype(FLOAT)[:, None]
    carry = ((jnp.arange(tokens + 128) < tokens + gap) & (seg_ext == seg_last)).astype(FLOAT)[:, None]
    seg_column, seg_line = seg_rows[:, None], seg_ext[None, :]
    forward_coefs, backward_coefs = carry_coefs(lengths, tokens)
    wide_cosine, wide_sine = rotation(pos_rows, HEAD_SIZE)
    query_table = own_heads(query_feature_maps, heads, core)
    key_table = own_heads(key_feature_maps, heads, core)
    query_table = jnp.concatenate([query_table, -query_table], axis=2)
    key_table = jnp.concatenate([key_table, -key_table], axis=2)
    downs = jnp.concatenate([query_down, key_down, value_down], axis=1)
    own_query_up = own_cols(query_up, q_width, core)
    own_key_up = own_cols(key_adapter_up, kv_width, core)
    own_value_up = own_cols(value_adapter_up, kv_width, core)
    own_output_down = own_heads(output_down, q_width, core)
    pad = 128 - 3 * rank
    ups = jnp.concatenate(
        [
            jnp.pad(own_query_up, ((0, 0), (0, 2 * kv_width))),
            jnp.pad(own_key_up, ((0, 0), (q_width, kv_width))),
            jnp.pad(own_value_up, ((0, 0), (q_width + kv_width, 0))),
            jnp.zeros((pad, qkv_width), BFLOAT),
        ],
        axis=0,
    )
    extent = tokens + 128
    wide_downs = jnp.pad(downs, ((0, 0), (0, pad)))
    wide_output_down = jnp.pad(own_output_down, ((0, 0), (0, 128 - rank)))
    wide_output_up = jnp.pad(output_up, ((0, 128 - rank), (0, 0)))
    (
        full_qkv, full_out, normed, low_rank, low_mid, residual, queries, key_ext, value_ext,
        phi_q, phi_k, attended, denominator, state, normed_ff, full_ff, cotangents,
    ) = front(
        chips,
        kv_heads,
        group,
        tokens,
        [
            hidden_in,
            attention_gain[None],
            feedforward_gain[None],
            wide_downs,
            ups,
            wide_cosine,
            wide_sine,
            query_table,
            key_table,
            seg_column,
            seg_line,
            continuing,
            carry,
            forward_coefs,
            wide_output_down,
            wide_output_up,
        ],
        [wqkv, wout, gate_weight, up_weight, down_weight.T, block_cotangent],
    )
    grad_normed_ff, out_sums, ff_grads, _, _ = feed(normed_ff, cotangents, full_ff)
    rear_outs = rear(
        chips,
        kv_heads,
        group,
        rank,
        [
            grad_normed_ff,
            residual,
            block_cotangent,
            hidden_in,
            attention_gain[None],
            feedforward_gain[None],
            full_out,
            wide_output_down[:, :16],
            wide_output_up[:16],
            low_mid,
            attended,
            denominator,
            queries,
            key_ext,
            value_ext,
            phi_q,
            phi_k,
            query_table,
            key_table,
            state,
            seg_column,
            seg_line,
            continuing,
            carry,
            backward_coefs,
            wide_cosine,
            wide_sine,
            normed,
            low_rank,
            full_qkv,
            ups,
            wide_downs,
        ],
        [out_sums, ff_grads],
    )
    block_output, input_grad, qkv_keep, qkv_other, out_keep, out_other = rear_outs[:6]
    own_small, sib_small = rear_outs[6:10], rear_outs[10:14]
    qkv_other, out_other = qkv_other.astype(FLOAT), out_other.astype(FLOAT)

    def by_core(dim, mine, other):
        return ordered(core, mine, other, dim)

    at_key, at_value = q_width, q_width + kv_width
    query_shard = by_core(1, qkv_keep[:, :at_key], qkv_other[:, :at_key])
    key_shard = by_core(1, qkv_keep[:, at_key:at_value], qkv_other[:, at_key:at_value])
    value_shard = by_core(1, qkv_keep[:, at_value:], qkv_other[:, at_value:])
    output_shard = by_core(1, out_keep, out_other).T
    ff_both = rear_outs[14]
    ff_shards = [ff_both[at, 0].astype(FLOAT) + ff_both[at, 1].astype(FLOAT) for at in range(3)]

    tables = by_core(0, own_small[0], sib_small[0]).reshape(CORES * heads, HEAD_SIZE, 128)
    early = own_small[1] + sib_small[1]
    late = own_small[3] + sib_small[3]
    ups_mine, ups_other = own_small[2], sib_small[2]

    def ups_part(row, start, stop):
        rows = slice(row * rank, (row + 1) * rank)
        return by_core(1, ups_mine[rows, start:stop], ups_other[rows, start:stop])

    downs_total = late[: 3 * rank].T
    return (
        block_output,
        input_grad,
        late[3 * rank],
        query_shard,
        key_shard,
        value_shard,
        output_shard,
        downs_total[:, :rank],
        ups_part(0, 0, at_key),
        downs_total[:, rank : 2 * rank],
        ups_part(1, at_key, at_value),
        downs_total[:, 2 * rank :],
        ups_part(2, at_value, qkv_width),
        ups_part(3, 0, at_key).T,
        early[:rank],
        tables[:, :, :FEATURE_HALF],
        tables[:, :, FEATURE_HALF:],
        early[rank],
        ff_shards[0],
        ff_shards[1],
        ff_shards[2].T,
    )


def solution(mesh):
    dp, seq, tensor = (mesh.shape[name] for name in ("dp", "seq", "tensor"))
    split = Mesh(
        mesh.devices.reshape(dp, seq // CORES, CORES, tensor), ("dp", "chip", "core", "tensor")
    )
    tok = ("dp", "chip", "core")
    in_specs = (
        P(tok, None),
        P("dp", None),
        P(),
        P(tok, "tensor"),
        P(tok, "tensor"),
        P(tok, "tensor"),
        P("tensor", tok),
        P(),
        P(None, "tensor"),
        P(),
        P(None, "tensor"),
        P(),
        P(None, "tensor"),
        P("tensor", None),
        P(),
        P("tensor", None, None),
        P("tensor", None, None),
        P(),
        P(tok, "tensor"),
        P(tok, "tensor"),
        P("tensor", tok),
        P(tok, None),
    )
    out_specs = (
        P(tok, None),
        P(tok, None),
        P(),
        P(tok, "tensor"),
        P(tok, "tensor"),
        P(tok, "tensor"),
        P("tensor", tok),
        P(),
        P(None, "tensor"),
        P(),
        P(None, "tensor"),
        P(),
        P(None, "tensor"),
        P("tensor", None),
        P(),
        P("tensor", None, None),
        P("tensor", None, None),
        P(),
        P(tok, "tensor"),
        P(tok, "tensor"),
        P("tensor", tok),
    )
    return jax.shard_map(
        on_device, mesh=split, in_specs=in_specs, out_specs=out_specs, check_vma=False
    )
```

```python
import functools

import jax
import jax.numpy as jnp
import numpy as np
from jax import lax
from jax.experimental import pallas as pl
from jax.experimental.pallas import tpu as pltpu
from jax.sharding import Mesh
from jax.sharding import PartitionSpec as P

HEAD_SIZE = 64
FEATURE_HALF = 64
SOFTMAX_KEYS = 64
CORES = 2


EPS = 1e-05
FLOAT = jnp.float32
BFLOAT = jnp.bfloat16


def ordered(which, mine, other, dim):
    return jnp.where(
        which == 0,
        jnp.concatenate([mine, other], axis=dim),
        jnp.concatenate([other, mine], axis=dim),
    )


def frequencies(head_width):
    inverse = 1.0 / 500000.0 ** (np.arange(0, head_width, 2) / head_width)
    wavelen = 2.0 * np.pi / inverse
    smooth = (8192.0 / wavelen - 1.0) / 3.0
    blended = (1.0 - smooth) * inverse / 32.0 + smooth * inverse
    return np.where(wavelen > 8192.0, inverse / 32.0, np.where(wavelen < 2048.0, inverse, blended))


def rotation(positions, head_width):
    table = np.tile(frequencies(head_width), 4)[None].astype(np.float32)
    sign = np.tile(np.repeat([-1.0, 1.0], head_width // 2), 2)[None].astype(np.float32)
    turned = positions.astype(FLOAT)[:, None] * table
    return jnp.cos(turned), jnp.sin(turned) * sign


def locate(places, lengths):
    segment, begin, end = jnp.zeros_like(places), jnp.zeros_like(places), 0
    for at in range(lengths.shape[0]):
        end = end + lengths[at]
        segment = segment + (places >= end).astype(jnp.int32)
        begin = jnp.where(places >= end, end, begin)
    return (jnp.where(places < 0, -1, segment), places - begin)


def product(left, right):
    return jnp.dot(left, right, preferred_element_type=FLOAT)


def product_t(left, right):
    return lax.dot_general(left, right, (((1,), (1,)), ((), ())), preferred_element_type=FLOAT)


def t_product(left, right):
    return lax.dot_general(left, right, (((0,), (0,)), ((), ())), preferred_element_type=FLOAT)


def dot(left, right):
    return lax.dot_general(left, right, (((1,), (0,)), ((), ())), preferred_element_type=FLOAT)


def lanes(shape):
    return lax.broadcasted_iota(jnp.int32, shape, 1)


def half_sums(rows):
    first = lax.broadcasted_iota(jnp.int32, (128, 128), 0) < FEATURE_HALF
    ones = jnp.where(first == (lanes((128, 128)) < FEATURE_HALF), 1.0, 0.0).astype(BFLOAT)
    return dot(rows, ones)


def two_softmax(mixed):
    low = lanes(mixed.shape) < FEATURE_HALF
    top = jnp.max(jnp.where(low, mixed, -jnp.inf), axis=1, keepdims=True)
    top_other = jnp.max(jnp.where(low, -jnp.inf, mixed), axis=1, keepdims=True)
    raised = jnp.exp(mixed - jnp.where(low, top, top_other))
    return (raised / half_sums(raised.astype(BFLOAT))).astype(BFLOAT)


def phi_kernel(group, q_ref, k_ref, vm_ref, fq_ref, fk_ref, phi_q_ref, phi_k_ref, state_ref):
    keys = k_ref[0]
    masked = vm_ref[0]
    for head in range(group):
        rows = q_ref[:, head * HEAD_SIZE : (head + 1) * HEAD_SIZE]
        phi_q_ref[head] = two_softmax(dot(rows, fq_ref[head]))
        phi_k = two_softmax(dot(keys, fk_ref[head]))
        phi_k_ref[head] = phi_k
        state_ref[head] = t_product(masked, phi_k).astype(BFLOAT)


def tile_masks(seg_q, seg_k, at):
    width = at + 256
    same = seg_q == seg_k[:, :width]
    row = lax.broadcasted_iota(jnp.int32, (128, 256), 0)
    col = lanes((128, 256))
    earlier = col <= row + SOFTMAX_KEYS
    window = (col > row + SOFTMAX_KEYS) & (col <= row + 128) & same[:, at:]
    return same[:, :at], window, earlier & same[:, at:]


def tile_weights(rows, phi_rows, k_ref, phi_k, at, masks):
    far, window, earlier = masks
    scale = HEAD_SIZE ** (-0.5)
    raw = product_t(rows, k_ref[0, at : at + 256])
    window_exp = jnp.where(window, jnp.exp(jnp.where(window, scale * raw, 0.0)), 0.0)
    linear = product_t(phi_rows, phi_k[: at + 256])
    near = jnp.where(earlier, linear[:, at:], window_exp)
    if at == 0:
        return window_exp, near.astype(BFLOAT)
    return window_exp, jnp.concatenate(
        [jnp.where(far, linear[:, :at], 0.0), near], axis=1
    ).astype(BFLOAT)


def intra_kernel(group, q_ref, k_ref, v_ref, phi_q_ref, phi_k_ref, seg_q_ref, seg_k_ref, num_ref):
    for at in range(0, q_ref.shape[0], 128):
        masks = tile_masks(seg_q_ref[at : at + 128], seg_k_ref[...], at)
        for head in range(group):
            rows = q_ref[at : at + 128, head * HEAD_SIZE : (head + 1) * HEAD_SIZE]
            weights = tile_weights(
                rows, phi_q_ref[head, at : at + 128], k_ref, phi_k_ref.at[head], at, masks
            )[1]
            num_ref[head, at : at + 128] = dot(weights, v_ref[0, : at + 256])


def finish_kernel(group, num_ref, phi_q_ref, state_ref, cont_ref, att_ref, den_ref):
    cont = cont_ref[...]
    den = jnp.zeros(den_ref.shape[1:], FLOAT)
    for head in range(group):
        total = num_ref[head] + cont * product_t(phi_q_ref[head], state_ref[head])
        below = total[:, HEAD_SIZE : HEAD_SIZE + 1]
        att_ref[:, head * HEAD_SIZE : (head + 1) * HEAD_SIZE] = (
            total[:, :HEAD_SIZE] / below
        ).astype(BFLOAT)
        den = jnp.where(lanes(den.shape) == head, below, den)
    den_ref[0] = den


def grad_numer_kernel(group, da_ref, att_ref, den_ref, phi_q_ref, cont_ref, dn_ref, ds_ref):
    cont = cont_ref[...]
    for head in range(group):
        cols = slice(head * HEAD_SIZE, (head + 1) * HEAD_SIZE)
        numer = da_ref[:, cols] / den_ref[0][:, head : head + 1]
        denom = -jnp.sum(numer * att_ref[:, cols].astype(FLOAT), axis=1, keepdims=True)
        high = denom.astype(BFLOAT).astype(FLOAT)
        wide = jnp.concatenate([numer, jnp.zeros_like(numer)], axis=1)
        lane = lanes(wide.shape)
        wide = jnp.where(lane == HEAD_SIZE, high, wide)
        wide = jnp.where(lane == HEAD_SIZE + 1, denom - high, wide)
        dn_ref[head] = wide.astype(BFLOAT)
        state = t_product((wide * cont).astype(BFLOAT), phi_q_ref[head])
        row = lax.broadcasted_iota(jnp.int32, state.shape, 0)
        both = state[HEAD_SIZE : HEAD_SIZE + 1] + state[HEAD_SIZE + 1 : HEAD_SIZE + 2]
        state = jnp.where(row == HEAD_SIZE, both, jnp.where(row > HEAD_SIZE, 0.0, state))
        ds_ref[head] = state.astype(BFLOAT)


def intra_back_kernel(
    group, q_ref, k_ref, v_ref, phi_q_ref, phi_k_ref, dn_ref, seg_q_ref, seg_k_ref,
    dq_ref, dk_ref, dv_ref, dphi_q_ref, dphi_k_ref,
):
    scale = HEAD_SIZE ** (-0.5)
    dk_ref[...] = jnp.zeros(dk_ref.shape, FLOAT)
    dv_ref[...] = jnp.zeros(dv_ref.shape, FLOAT)
    dphi_k_ref[...] = jnp.zeros(dphi_k_ref.shape, FLOAT)
    for at in range(0, q_ref.shape[0], 128):
        masks = tile_masks(seg_q_ref[at : at + 128], seg_k_ref[...], at)
        tile = slice(at, at + 128)
        width = at + 256
        for head in range(group):
            cols = slice(head * HEAD_SIZE, (head + 1) * HEAD_SIZE)
            rows = q_ref[tile, cols]
            phi_rows = phi_q_ref[head, tile]
            numer = dn_ref[head, tile]
            window_exp, weights = tile_weights(
                rows, phi_rows, k_ref, phi_k_ref.at[head], at, masks
            )
            grad = product_t(numer, v_ref[0, :width])
            near = grad[:, at:]
            grad_raw = (scale * near * window_exp).astype(BFLOAT)
            grad_linear = jnp.where(masks[2], near, 0.0)
            if at > 0:
                grad_linear = jnp.concatenate(
                    [jnp.where(masks[0], grad[:, :at], 0.0), grad_linear], axis=1
                )
            grad_linear = grad_linear.astype(BFLOAT)
            dv_ref[0, :width] += t_product(weights, numer)
            dphi_q_ref[head, tile] = dot(grad_linear, phi_k_ref[head, :width])
            dphi_k_ref[head, :width] += t_product(grad_linear, phi_rows)
            dq_ref[tile, cols] = dot(grad_raw, k_ref[0, at:width])
            dk_ref[0, at:width] += t_product(grad_raw, rows)


def softmax_back(phi, grad):
    wide = phi.astype(FLOAT)
    terms = grad * wide
    high = terms.astype(BFLOAT)
    low = (terms - high.astype(FLOAT)).astype(BFLOAT)
    mean = (half_sums(high) + half_sums(low)) / half_sums(phi)
    return (wide * (grad - mean)).astype(BFLOAT)


def features_back_kernel(
    group, q_ref, k_ref, v_ref, phi_q_ref, phi_k_ref, dn_ref, fq_ref, fk_ref, state_ref, ds_ref,
    cont_ref, carry_ref, dq_in, dk_in, dv_in, dphi_q_ref, dphi_k_ref,
    dq_ref, dk_ref, dv_ref, gq_ref, gk_ref,
):
    cont = cont_ref[...]
    carry = carry_ref[...]
    keys = k_ref[0]
    dk = dk_in[0]
    dv = dv_in[0]
    for head in range(group):
        cols = slice(head * HEAD_SIZE, (head + 1) * HEAD_SIZE)
        grad_state = ds_ref[head]
        phi_k = phi_k_ref[head]
        grad_q = dphi_q_ref[head] + cont * dot(dn_ref[head], state_ref[head])
        grad_k = dphi_k_ref[head] + carry * dot(v_ref[0], grad_state)
        dv = dv + carry * product_t(phi_k, grad_state)
        mixed_q = softmax_back(phi_q_ref[head], grad_q)
        mixed_k = softmax_back(phi_k, grad_k)
        dq_ref[:, cols] = dq_in[:, cols] + product_t(mixed_q, fq_ref[head])
        dk = dk + product_t(mixed_k, fk_ref[head])
        gq_ref[head] = t_product(q_ref[:, cols], mixed_q)
        gk_ref[head] = t_product(keys, mixed_k)
    dk_ref[0] = dk
    dv_ref[0] = dv


def remote(source, target, send_sem, recv_sem, **where):
    return pltpu.make_async_remote_copy(
        src_ref=source,
        dst_ref=target,
        send_sem=send_sem,
        recv_sem=recv_sem,
        device_id=where,
        device_id_type=pl.DeviceIdType.MESH,
    )


def greet(peers):
    barrier = pltpu.get_barrier_semaphore()
    for where in peers:
        pl.semaphore_signal(barrier, inc=1, device_id=where, device_id_type=pl.DeviceIdType.MESH)
    pl.semaphore_wait(barrier, len(peers))


def even_chip(chip):
    return 1 - lax.rem(chip, 2)


def slot_of(chips, chip, step):
    if chips != 4:
        return step
    even = even_chip(chip)
    return lax.rem(even * step + (1 - even) * (chips - step), chips)


def row_copies(chips, chip, source, target, send, recv):
    own = source.shape[0]

    def one(piece, step, rows, at, to):
        return remote(piece, target.at[step, rows], send.at[at], recv.at[at], chip=to)

    every = pl.ds(0, own)
    if chips != 4:
        to = [lax.rem(chip + chips - step, chips) for step in range(1, chips)]
        return [one(source, step + 1, every, step, at) for step, at in enumerate(to)], []
    even = even_chip(chip)
    beside = 3 - 2 * even
    across = chip - 1 + 2 * even
    along = chip + 2 - 4 * (chip // 2)
    upper, lower = pl.ds(0, own // 2), pl.ds(own // 2, own // 2)
    return [
        one(source, chips - beside, every, 0, across),
        one(source, 2, every, 1, along),
    ], [
        one(target.at[beside, upper], chips - beside, upper, 2, along),
        one(target.at[2, lower], beside, lower, 3, across),
    ]


def relay(copies):
    for at, copy in enumerate(copies[1]):
        copies[0][at].wait_recv()
        copy.start()


def forward_copies(chips, chip, core, source, target, send, recv):
    own = source.shape[0]
    copies = []
    for at in range(chips):
        slot = slot_of(chips, chip, at) if at > 0 else 0
        piece = target.at[slot, pl.ds(0, own)] if at > 0 else source
        copies.append(
            remote(piece, target.at[slot, pl.ds(own, own)], send.at[at], recv.at[at], core=1 - core)
        )
    return copies


def hand_over(copies, forwards):
    if copies[1]:
        forwards[1].start()
        forwards[2].start()
        for copy in copies[1]:
            copy.wait_recv()
        forwards[3].start()
    else:
        for copy, forward in zip(copies[0], forwards[1:]):
            copy.wait_recv()
            forward.start()


def feed_kernel(
    chips, x_ref, c_ref, ff_ref,
    grad_ref, out_ref, ffg_ref, got_ref, xall_ref,
    x_buf, c_buf, gg_ref, gu_ref, gd_ref, keep, sib_out, sib_in, part, stage, cross_in,
    load_sems, stage_sems, sib_send, sib_recv, part_send, part_recv, cross_sems, ffg_sems, free_sem,
    x_send, x_recv, xf_send, xf_recv, x_sem,
):
    core, chip, tensor = (lax.axis_index(name) for name in ("core", "chip", "tensor"))
    rows = keep.shape[2]
    count, model = x_buf.shape[1:]
    units = ff_ref.shape[2]
    gate_ref, up_ref, down_ref = (ff_ref.at[which] for which in range(3))
    sibling = {"core": 1 - core}
    greet(
        [sibling, {"tensor": 1 - tensor}]
        + [{"chip": lax.rem(chip + step, chips)} for step in range(1, chips)]
    )

    def place(step):
        return slot_of(chips, chip, step)

    def load(step, which):
        slot = lax.rem(step, 2)
        ref, buf = ((xall_ref, x_buf), (c_ref, c_buf))[which]
        return pltpu.make_async_copy(ref.at[place(step)], buf.at[slot], load_sems.at[which, slot])

    x_copies = row_copies(chips, chip, x_ref, xall_ref, x_send, x_recv)
    x_forward = forward_copies(chips, chip, core, x_ref, xall_ref, xf_send, xf_recv)
    x_local = pltpu.make_async_copy(x_ref, xall_ref.at[0, pl.ds(0, rows)], x_sem)

    def came(step):
        half = xall_ref.at[place(step), pl.ds(rows, rows)]
        remote(half, half, xf_send.at[step], xf_recv.at[step], **sibling).wait_recv()

    def advance(step):
        if chips == 4:

            @pl.when(step == 0)
            def _():
                relay(x_copies)
                x_forward[1].start()
                x_forward[2].start()

            @pl.when(step == 2)
            def _():
                for copy in x_copies[1]:
                    copy.wait_recv()
                x_forward[3].start()

        else:
            for at, copy in enumerate(x_copies[0]):

                @pl.when(step == at)
                def _(at=at, copy=copy):
                    copy.wait_recv()
                    x_forward[at + 1].start()

    def to_sibling(step):
        slot = lax.rem(step, 2)
        return remote(
            sib_out.at[slot], sib_in.at[slot], sib_send.at[slot], sib_recv.at[slot], **sibling
        )

    def stage_copy(step):
        slot = lax.rem(step, 2)
        return pltpu.make_async_copy(stage.at[slot], out_ref.at[place(step)], stage_sems.at[slot])

    halves = [pl.ds(0, rows // 2), pl.ds(rows // 2, rows // 2)]

    def to_chip(step):
        slot = place(step)
        return [
            remote(
                part.at[step - 1, piece],
                got_ref.at[slot - 1, piece],
                part_send.at[step - 1, at],
                part_recv.at[slot - 1, at],
                chip=lax.rem(chip + slot, chips),
            )
            for at, piece in enumerate(halves)
        ]

    def send_part(step):
        for copy in to_chip(step):
            copy.start()

    def total(step, which):
        slot = lax.rem(step, 2)
        return keep[slot, which].astype(FLOAT) + sib_in[slot, which].astype(FLOAT)

    x_local.start()
    x_forward[0].start()
    for copy in x_copies[0]:
        copy.start()
    load(0, 1).start()
    gg_ref[...] = jnp.zeros(gg_ref.shape, FLOAT)
    gu_ref[...] = jnp.zeros(gu_ref.shape, FLOAT)
    gd_ref[...] = jnp.zeros(gd_ref.shape, FLOAT)

    def body(step, nothing):
        slot = lax.rem(step, 2)
        came(step)
        load(step, 0).start()
        load(step, 1).wait()

        @pl.when(step < chips - 1)
        def _():
            load(step + 1, 1).start()

        load(step, 0).wait()
        tokens = x_buf[slot]
        cotangent = c_buf[slot]
        gate = dot(tokens, gate_ref[...])
        up = dot(tokens, up_ref[...])
        grad = dot(cotangent, down_ref[...])
        sigmoid = 1.0 / (1.0 + jnp.exp(-gate))
        silu = gate * sigmoid
        hidden = (silu * up).astype(BFLOAT)
        grad_gate = (grad * up * (sigmoid + silu * (1.0 - sigmoid))).astype(BFLOAT)
        grad_up = (grad * silu).astype(BFLOAT)

        @pl.when(step >= 2)
        def _():
            to_sibling(step).wait_send()
            pl.semaphore_wait(free_sem, 1)

        @pl.when(step > 0)
        def _():
            advance(step)

        def back(part_of):
            return (
                product_t(grad_gate[part_of], gate_ref[...])
                + product_t(grad_up[part_of], up_ref[...])
            ).astype(BFLOAT)

        def out(part_of):
            return product_t(hidden[part_of], down_ref[...]).astype(BFLOAT)

        mine, theirs = slice(0, rows), slice(rows, 2 * rows)
        sib_out[slot, 0] = back(theirs)
        sib_out[slot, 1] = out(theirs)
        to_sibling(step).start()
        keep[slot, 0] = back(mine)
        keep[slot, 1] = out(mine)

        @pl.when(step > 0)
        def _():
            before = step - 1
            to_sibling(before).wait_recv()

            @pl.when(before == 0)
            def _():
                grad_ref[...] = total(before, 0)

            @pl.when(before > 0)
            def _():
                part[before - 1] = total(before, 0).astype(BFLOAT)
                send_part(before)

            @pl.when(step > 2)
            def _():
                stage_copy(before).wait()

            stage[lax.rem(before, 2)] = total(before, 1).astype(BFLOAT)
            stage_copy(before).start()
            pl.semaphore_signal(free_sem, inc=1, device_id=sibling, device_id_type=pl.DeviceIdType.MESH)

        gg_ref[...] += t_product(tokens, grad_gate)
        gu_ref[...] += t_product(tokens, grad_up)
        gd_ref[...] += t_product(cotangent, hidden)

        @pl.when(step == 0)
        def _():
            advance(step)

        return nothing

    x_local.wait()
    lax.fori_loop(0, chips, body, 0)
    last = chips - 1
    to_sibling(last).wait_recv()
    part[last - 1] = total(last, 0).astype(BFLOAT)
    send_part(last)
    if chips > 2:
        stage_copy(last).wait()
    stage[last % 2] = total(last, 1).astype(BFLOAT)
    stage_copy(last).start()
    per = model // units
    ffg_copies = []
    for which, ref in enumerate((gg_ref, gu_ref, gd_ref)):
        for at in range(model // count):
            place_at = which * (model // count) + at
            buf = (x_buf, c_buf)[place_at // (2 * per)]
            spot = buf.at[(place_at // per) % 2, :, pl.ds((place_at % per) * units, units)]
            piece = pl.ds(at * count, count)
            spot[...] = ref[piece].astype(BFLOAT)
            copy = pltpu.make_async_copy(spot, ffg_ref.at[which, piece], ffg_sems.at[place_at])
            copy.start()
            ffg_copies.append(copy)

    wide = keep.at[0, 0]
    across = []
    for at, piece in enumerate(halves):

        def finish(step, nothing, at=at, piece=piece):
            to_chip(step)[at].wait_recv()
            fetch = pltpu.make_async_copy(
                got_ref.at[place(step) - 1, piece], wide.at[piece], load_sems.at[0, 0]
            )
            fetch.start()
            fetch.wait()
            grad_ref[piece] += wide[piece].astype(FLOAT)
            return nothing

        lax.fori_loop(1, chips, finish, 0)
        wide[piece] = grad_ref[piece].astype(BFLOAT)
        across.append(
            remote(
                wide.at[piece], cross_in.at[piece], cross_sems.at[0, at], cross_sems.at[1, at],
                tensor=1 - tensor,
            )
        )
        across[at].start()

    def drain(step, nothing):
        for copy in to_chip(step):
            copy.wait_send()
        return nothing

    lax.fori_loop(1, chips, drain, 0)
    for copy in x_copies[0] + x_copies[1] + x_forward:
        copy.wait_send()
    for copy in ffg_copies:
        copy.wait()
    for step in range(max(0, chips - 2), chips):
        to_sibling(step).wait_send()
        stage_copy(step).wait()
    pl.semaphore_wait(free_sem, min(1, chips - 1))
    for at, piece in enumerate(halves):
        across[at].wait()
        grad_ref[piece] = wide[piece].astype(FLOAT) + cross_in[piece].astype(FLOAT)


def feed(tokens, cotangent, weights):
    chips, count, model = cotangent.shape
    rows = count // CORES
    units = weights.shape[2]
    near = pl.BlockSpec(memory_space=pltpu.VMEM)
    far = pl.BlockSpec(memory_space=pl.ANY)
    return pl.pallas_call(
        functools.partial(feed_kernel, chips),
        in_specs=[near, far, near],
        out_specs=[near, far, far, far, far],
        out_shape=[
            jax.ShapeDtypeStruct((rows, model), FLOAT),
            jax.ShapeDtypeStruct((chips, rows, model), BFLOAT),
            jax.ShapeDtypeStruct(weights.shape, BFLOAT),
            jax.ShapeDtypeStruct((chips - 1, rows, model), BFLOAT),
            jax.ShapeDtypeStruct((chips, count, model), BFLOAT),
        ],
        scratch_shapes=[
            pltpu.VMEM((2, count, model), BFLOAT),
            pltpu.VMEM((2, count, model), BFLOAT),
            pltpu.VMEM((model, units), FLOAT),
            pltpu.VMEM((model, units), FLOAT),
            pltpu.VMEM((model, units), FLOAT),
            pltpu.VMEM((2, 2, rows, model), BFLOAT),
            pltpu.VMEM((2, 2, rows, model), BFLOAT),
            pltpu.VMEM((2, 2, rows, model), BFLOAT),
            pltpu.VMEM((chips - 1, rows, model), BFLOAT),
            pltpu.VMEM((2, rows, model), BFLOAT),
            pltpu.VMEM((rows, model), BFLOAT),
            pltpu.SemaphoreType.DMA((2, 2)),
            dma_row(2),
            dma_row(2),
            dma_row(2),
            pltpu.SemaphoreType.DMA((chips - 1, 2)),
            pltpu.SemaphoreType.DMA((chips - 1, 2)),
            pltpu.SemaphoreType.DMA((2, 2)),
            dma_row(3 * model // count),
            pltpu.SemaphoreType.REGULAR,
            dma_row(chips),
            dma_row(chips),
            dma_row(chips),
            dma_row(chips),
            pltpu.SemaphoreType.DMA,
        ],
        compiler_params=pltpu.CompilerParams(
            vmem_limit_bytes=62 * 1024 * 1024, collective_id=1, has_side_effects=True
        ),
        cost_estimate=pl.CostEstimate(
            flops=18 * chips * count * model * units,
            bytes_accessed=8 * chips * count * model,
            transcendentals=0,
        ),
    )(tokens, cotangent, weights)


def dma_row(count):
    return pltpu.SemaphoreType.DMA((count,))


def front_kernel(
    chips, kv_heads, group,
    hid_ref, again_ref, fgain_ref, downs_ref, ups_ref, cos_ref, sin_ref, fq_ref, fk_ref,
    seg_q_ref, seg_k_ref, cont_ref, carry_ref, coef_ref, odown_ref, oup_ref,
    wqkv_ref, wo_ref, gate_ref, up_ref, down_ref, cot_ref,
    qkv_ref, wof_ref, normed_ref, low_ref, mid_ref, res_ref, q_ref, k_ref, v_ref,
    phi_q_ref, phi_k_ref, att_ref, den_ref, state_ref,
    xn, ff_ref, call_ref,
    hid_sib, vm, rim_out, rim_in, st_out, st_in, num, br_out, br_in, tz_out, tz_in,
    hid_sem, q1_send, q1_recv, q2_send, q2_recv, o1_send, o1_recv, o2_send, o2_recv,
    ff_send, ff_recv, local_sems, c_send, c_recv, cf_send, cf_recv,
    rim_sem, st_send, st_recv, br_sem, tz_sem,
):
    dp, chip, core, tensor = (lax.axis_index(name) for name in ("dp", "chip", "core", "tensor"))
    own = hid_ref.shape[0]
    tokens = CORES * own
    model = hid_ref.shape[1]
    shard = wqkv_ref.shape[1]
    q_width = q_ref.shape[1]
    pairs = CORES * chips
    units = ff_ref.shape[2]
    other = 1 - core
    there = 1 - dp
    sibling = {"core": other}
    at_chip = [lax.rem(chip + step, chips) for step in range(1, chips)]
    behind = [lax.rem(chip + chips - step, chips) for step in range(1, chips)]
    greet(
        [sibling, {"tensor": 1 - tensor}]
        + [{"dp": there, "core": core}, {"dp": there, "core": other}]
        + [{"chip": to, "core": which} for to in at_chip for which in (core, other)]
        + [{"dp": there, "chip": to, "core": which} for to in at_chip for which in (core, other)]
    )

    def first(source, target, send, recv):
        rows = pl.ds(((dp * chips + chip) * CORES + core) * shard, shard)
        return [
            remote(source.at[other], target.at[rows], send.at[0], recv.at[0], core=other),
            remote(source.at[core], target.at[rows], send.at[1], recv.at[1], dp=there),
            remote(source.at[other], target.at[rows], send.at[2], recv.at[2], dp=there, core=other),
        ]

    def local(source, target, at):
        rows = pl.ds(((dp * chips + chip) * CORES + core) * shard, shard)
        return pltpu.make_async_copy(source.at[core], target.at[rows], local_sems.at[at])

    def second(target, send, recv, side):
        group_at = dp if side == 0 else there
        rows = pl.ds((group_at * chips + chip) * CORES * shard, CORES * shard)
        return [
            remote(target.at[rows], target.at[rows], send.at[side, at], recv.at[side, at], chip=to)
            for at, to in enumerate(at_chip)
        ]

    q_first = first(wqkv_ref, qkv_ref, q1_send, q1_recv)
    o_first = first(wo_ref, wof_ref, o1_send, o1_recv)
    q_local, o_local = local(wqkv_ref, qkv_ref, 0), local(wo_ref, wof_ref, 1)
    q_second = [second(qkv_ref, q2_send, q2_recv, side) for side in range(2)]
    o_second = [second(wof_ref, o2_send, o2_recv, side) for side in range(2)]
    hid_copy = remote(hid_ref, hid_sib, hid_sem.at[0], hid_sem.at[1], **sibling)
    q_local.start()
    hid_copy.start()
    for copy in q_first:
        copy.start()
    o_local.start()
    for copy in o_first:
        copy.start()

    ff_rows = pl.ds(((dp * chips + chip) * CORES + core) * shard, shard)
    ff_sources = (gate_ref, up_ref, down_ref)

    def ff_copy(which, step, side):
        to = lax.rem(chip * CORES + core + step, pairs)
        return remote(
            ff_sources[which].at[:, pl.ds(pl.multiple_of(to * units, units), units)],
            ff_ref.at[which, ff_rows],
            ff_send.at[which],
            ff_recv.at[which],
            dp=dp if side == 0 else there,
            chip=to // CORES,
            core=lax.rem(to, CORES),
        )

    def ff_local(which):
        return pltpu.make_async_copy(
            ff_sources[which].at[:, pl.ds(pl.multiple_of((chip * CORES + core) * units, units), units)],
            ff_ref.at[which, ff_rows],
            local_sems.at[2 + which],
        )

    def ff_start(which, side):
        def one(step, nothing):
            ff_copy(which, step, side).start()
            return nothing

        lax.fori_loop(1 - side, pairs, one, 0)

    c_copies = row_copies(chips, chip, cot_ref, call_ref, c_send, c_recv)
    c_forward = forward_copies(chips, chip, core, cot_ref, call_ref, cf_send, cf_recv)
    c_local = pltpu.make_async_copy(cot_ref, call_ref.at[0, pl.ds(0, own)], local_sems.at[5])

    def normalized(rows, gain):
        return (rows * lax.rsqrt(jnp.mean(rows * rows, axis=1, keepdims=True) + EPS) * gain).astype(BFLOAT)

    ff_start(0, 1)
    for which in range(3):
        ff_local(which).start()
    c_local.start()
    hidden = hid_ref[...].astype(FLOAT)
    normed_ref[pl.ds(pl.multiple_of(core * own, own), own)] = normalized(hidden, again_ref[...])
    q_first[0].wait_recv()
    q_local.wait()
    for copy in q_second[0]:
        copy.start()
    hid_copy.wait()
    normed_ref[pl.ds(pl.multiple_of(other * own, own), own)] = normalized(
        hid_sib[...].astype(FLOAT), again_ref[...]
    )
    low_ref[...] = dot(normed_ref[...], downs_ref[...]).astype(BFLOAT)
    q_first[1].wait_recv()
    q_first[2].wait_recv()
    for copy in q_second[1]:
        copy.start()
    o_first[0].wait_recv()
    o_local.wait()
    for copy in o_second[0]:
        copy.start()
    for side in range(2):
        for copy in q_second[side]:
            copy.wait_recv()
    ff_start(0, 0)
    ff_start(1, 1)

    pre = dot(normed_ref[...], qkv_ref[...]) + dot(low_ref[...], ups_ref[...])
    half = HEAD_SIZE // 2
    first_half = lax.rem(lanes((tokens, 128)), HEAD_SIZE) < half

    def rotated(block):
        turned = jnp.where(first_half, pltpu.roll(block, 128 - half, 1), pltpu.roll(block, half, 1))
        return (block * cos_ref[...] + turned * sin_ref[...]).astype(BFLOAT)

    for at in range(0, q_width, 128):
        q_ref[:, at : at + 128] = rotated(pre[:, at : at + 128])
    keys = rotated(pre[:, q_width : q_width + 128])
    values = pre[:, q_width + 128 :].astype(BFLOAT)
    rim_out[:, :128] = keys[tokens - SOFTMAX_KEYS :]
    rim_out[:, 128:] = values[tokens - SOFTMAX_KEYS :]
    rim_copy = remote(rim_out, rim_in, rim_sem.at[0], rim_sem.at[1], chip=lax.rem(chip + 1, chips))

    @pl.when(chip < chips - 1)
    def _():
        rim_copy.start()

    def tailed(rows):
        tail = jnp.where(lanes((rows.shape[0], 128 - HEAD_SIZE)) < 2, 1.0, 0.0).astype(BFLOAT)
        return jnp.concatenate([rows, tail], axis=1)

    gap = 128 - SOFTMAX_KEYS
    for head in range(kv_heads):
        cols = slice(head * HEAD_SIZE, (head + 1) * HEAD_SIZE)
        k_ref[head, 128:] = keys[:, cols]
        v_ref[head, 128:] = tailed(values[:, cols])
        k_ref[head, :gap] = jnp.zeros((gap, HEAD_SIZE), BFLOAT)
        v_ref[head, :gap] = tailed(jnp.zeros((gap, HEAD_SIZE), BFLOAT))

    @pl.when(chip == 0)
    def _():
        rim_in[...] = jnp.zeros(rim_in.shape, BFLOAT)

    @pl.when(chip > 0)
    def _():
        rim_copy.wait_recv()

    carry = carry_ref[...]
    for head in range(kv_heads):
        cols = slice(head * HEAD_SIZE, (head + 1) * HEAD_SIZE)
        k_ref[head, gap:128] = rim_in[:, cols]
        v_ref[head, gap:128] = tailed(rim_in[:, 128 + head * HEAD_SIZE : 128 + (head + 1) * HEAD_SIZE])
        vm[head] = (v_ref[head].astype(FLOAT) * carry).astype(BFLOAT)

    def views(at):
        heads = pl.ds(at * group, group)
        one = pl.ds(at, 1)
        wide = pl.ds(at * group * HEAD_SIZE, group * HEAD_SIZE)
        return heads, one, wide

    for at in range(kv_heads):
        heads, one, wide = views(at)
        phi_kernel(
            group, q_ref.at[:, wide], k_ref.at[one], vm.at[one], fq_ref.at[heads], fk_ref.at[heads],
            phi_q_ref.at[heads], phi_k_ref.at[heads], st_out.at[heads],
        )
    kept = HEAD_SIZE + 16
    st_copies = [
        remote(st_out.at[:, pl.ds(0, kept)], st_in.at[at], st_send.at[at], st_recv.at[at], chip=to)
        for at, to in enumerate(at_chip)
    ]
    for copy in st_copies:
        copy.start()
    o_first[1].wait_recv()
    o_first[2].wait_recv()
    for copy in o_second[1]:
        copy.start()
    ff_start(1, 0)
    c_forward[0].start()
    for copy in c_copies[0]:
        copy.start()
    for at in range(kv_heads):
        heads, one, wide = views(at)
        intra_kernel(
            group, q_ref.at[:, wide], k_ref.at[one], v_ref.at[one], phi_q_ref.at[heads],
            phi_k_ref.at[heads], seg_q_ref, seg_k_ref, num.at[heads],
        )
    total = jnp.zeros(st_in.shape[1:], FLOAT)
    for at, copy in enumerate(st_copies):
        copy.wait_recv()
        total = total + coef_ref[at] * st_in[at].astype(FLOAT)
    state_ref[:, :kept] = total.astype(BFLOAT)
    state_ref[:, kept:] = jnp.zeros((state_ref.shape[0], 128 - kept, 128), BFLOAT)
    for at in range(kv_heads):
        heads, one, wide = views(at)
        finish_kernel(
            group, num.at[heads], phi_q_ref.at[heads], state_ref.at[heads], cont_ref,
            att_ref.at[:, wide], den_ref.at[one],
        )

    for side in range(2):
        for copy in o_second[side]:
            copy.wait_recv()

    def branch(which, target):
        rows = att_ref[pl.ds(pl.multiple_of(which * own, own), own)]
        return product_t(rows, wof_ref[...]), dot(rows, odown_ref[...])

    wide_part, low_part = branch(other, None)
    br_out[:, :model] = wide_part.astype(BFLOAT)
    br_out[:, model:] = low_part.astype(BFLOAT)
    br_copy = remote(br_out, br_in, br_sem.at[0], br_sem.at[1], **sibling)
    br_copy.start()
    wide_part, low_part = branch(core, None)
    br_copy.wait_recv()
    tz_out[:, :model] = (wide_part + br_in[:, :model].astype(FLOAT)).astype(BFLOAT)
    tz_out[:, model:] = (low_part + br_in[:, model:].astype(FLOAT)).astype(BFLOAT)
    tz_copy = remote(tz_out, tz_in, tz_sem.at[0], tz_sem.at[1], tensor=1 - tensor)
    tz_copy.start()
    ff_start(2, 1)
    tz_copy.wait_recv()
    relay(c_copies)
    ff_start(2, 0)
    mid = (tz_out[:, model:].astype(FLOAT) + tz_in[:, model:].astype(FLOAT)).astype(BFLOAT)
    mid_ref[...] = mid
    residual = (
        hid_ref[...].astype(FLOAT)
        + (tz_out[:, :model].astype(FLOAT) + tz_in[:, :model].astype(FLOAT))
        + dot(mid, oup_ref[...])
    )
    res_ref[...] = residual
    xn[...] = normalized(residual, fgain_ref[...])
    hand_over(c_copies, c_forward)

    hid_done = [br_copy, tz_copy] + q_first + o_first + q_second[0] + q_second[1]
    for copy in hid_done + o_second[0] + o_second[1] + st_copies + c_copies[0] + c_copies[1]:
        copy.wait_send()

    @pl.when(chip < chips - 1)
    def _():
        rim_copy.wait_send()

    for copy in c_forward:
        copy.wait()
    c_local.wait()
    moved = (2 * pairs - 1) * shard
    for which in range(3):
        ff_local(which).wait()
        every = ff_ref.at[which, pl.ds(0, moved)]
        remote(every, every, ff_send.at[which], ff_recv.at[which], **sibling).wait()


def front(
    chips, kv_heads, group, tokens, near_args, far_args
):
    own, model = near_args[0].shape
    heads = kv_heads * group
    q_width = heads * HEAD_SIZE
    qkv_width = q_width + 2 * kv_heads * HEAD_SIZE
    extent = tokens + 128
    units = far_args[2].shape[1] // (chips * CORES)
    near = pl.BlockSpec(memory_space=pltpu.VMEM)
    far = pl.BlockSpec(memory_space=pl.ANY)
    kept = HEAD_SIZE + 16
    near_outs = [
        ((model, qkv_width), BFLOAT),
        ((model, q_width), BFLOAT),
        ((tokens, model), BFLOAT),
        ((tokens, 128), BFLOAT),
        ((own, 128), BFLOAT),
        ((own, model), FLOAT),
        ((tokens, q_width), BFLOAT),
        ((kv_heads, extent, HEAD_SIZE), BFLOAT),
        ((kv_heads, extent, 128), BFLOAT),
        ((heads, tokens, 128), BFLOAT),
        ((heads, extent, 128), BFLOAT),
        ((tokens, q_width), BFLOAT),
        ((kv_heads, tokens, 128), FLOAT),
        ((heads, 128, 128), BFLOAT),
        ((own, model), BFLOAT),
    ]
    far_outs = [
        ((3, model, units), BFLOAT),
        ((chips, tokens, model), BFLOAT),
    ]
    pair = dma_row(2)
    return pl.pallas_call(
        functools.partial(front_kernel, chips, kv_heads, group),
        in_specs=[near] * len(near_args) + [far] * len(far_args),
        out_specs=[near] * len(near_outs) + [far] * len(far_outs),
        out_shape=[jax.ShapeDtypeStruct(*out) for out in near_outs + far_outs],
        scratch_shapes=[
            pltpu.VMEM((own, model), BFLOAT),
            pltpu.VMEM((kv_heads, extent, 128), BFLOAT),
            pltpu.VMEM((SOFTMAX_KEYS, 256), BFLOAT),
            pltpu.VMEM((SOFTMAX_KEYS, 256), BFLOAT),
            pltpu.VMEM((heads, 128, 128), BFLOAT),
            pltpu.VMEM((chips - 1, heads, kept, 128), BFLOAT),
            pltpu.VMEM((heads, tokens, 128), FLOAT),
            pltpu.VMEM((own, model + 128), BFLOAT),
            pltpu.VMEM((own, model + 128), BFLOAT),
            pltpu.VMEM((own, model + 128), BFLOAT),
            pltpu.VMEM((own, model + 128), BFLOAT),
            pair,
            dma_row(3),
            dma_row(3),
            pltpu.SemaphoreType.DMA((2, chips - 1)),
            pltpu.SemaphoreType.DMA((2, chips - 1)),
            dma_row(3),
            dma_row(3),
            pltpu.SemaphoreType.DMA((2, chips - 1)),
            pltpu.SemaphoreType.DMA((2, chips - 1)),
            dma_row(3),
            dma_row(3),
            dma_row(7),
            dma_row(chips),
            dma_row(chips),
            dma_row(chips),
            dma_row(chips),
            pair,
            dma_row(chips - 1),
            dma_row(chips - 1),
            pair,
            pair,
        ],
        compiler_params=pltpu.CompilerParams(
            vmem_limit_bytes=60 * 1024 * 1024, collective_id=2, has_side_effects=True
        ),
        cost_estimate=pl.CostEstimate(
            flops=int(1e10), bytes_accessed=int(1e8), transcendentals=0
        ),
    )(*near_args, *far_args)


def rear_kernel(
    chips, kv_heads, group, rank,
    gnf_ref, res_ref, cot_ref, hid_ref, again_ref, fgain_ref, wof_ref, odown_ref, oup_ref, mid_ref,
    att_ref, den_ref, q_ref, k_ref, v_ref, phi_q_ref, phi_k_ref, fq_ref, fk_ref, state_ref,
    seg_q_ref, seg_k_ref, cont_ref, carry_ref, coef_ref, cos_ref, sin_ref,
    normed_ref, low_ref, qkv_ref, ups_ref, downs_ref,
    out_ref, ffg_ref,
    block_ref, igrad_ref, qkv_own, qkv_sib, o_own, o_sib,
    tab_own, early_own, ups_own, late_own, tab_sib, early_sib, ups_sib, late_sib,
    ffin_ref, oin_ref,
    db, dq, dn, ds_out, ds_in, gstate, dk, dv, dphi_q, dphi_k, gq, gk, dres,
    rim_out, rim_in, gp, br_out, br_in, tz_in,
    qg, q_in, q_dp_out, q_dp_in, q_core, og, o_in, o_dp_out, o_dp_in, o_core,
    tab_slots, early_slots, ups_slots, late_slots,
    tab_dp, early_dp, ups_dp, late_dp,
    db_sem, ds_send, ds_recv, rim_sem, br_sem, tz_sem, oz_sem, o_load, os_send, os_recv,
    q_send, q_recv, q_dp_sem, q_core_sem, o_send, o_recv, o_dp_sem, o_core_sem,
    small_send, small_recv, small_dp, small_core,
    ff_send, ff_recv, local_sems,
):
    dp, chip, core, tensor = (lax.axis_index(name) for name in ("dp", "chip", "core", "tensor"))
    own, model = gnf_ref.shape
    tokens = CORES * own
    q_width = q_ref.shape[1]
    pairs = CORES * chips
    shard = model // (2 * pairs)
    units = ffg_ref.shape[2]
    other = 1 - core
    there = 1 - dp
    sibling = {"core": other}
    at_chip = [lax.rem(chip + step, chips) for step in range(1, chips)]
    greet(
        [sibling, {"tensor": 1 - tensor}]
        + [{"dp": there, "core": core}, {"dp": there, "core": other}]
        + [{"chip": to, "core": which} for to in at_chip for which in (core, other)]
        + [{"dp": there, "chip": to, "core": which} for to in at_chip for which in (core, other)]
    )
    mine = pl.ds(pl.multiple_of(core * own, own), own)
    theirs = pl.ds(pl.multiple_of(other * own, own), own)

    def ff_start(which, side):
        def one(step, nothing):
            to = lax.rem(chip * CORES + core + step, pairs)
            group_to = dp if side == 0 else there
            remote(
                ffg_ref.at[which, pl.ds((group_to * pairs + to) * shard, shard)],
                ffin_ref.at[which, dp, :, pl.ds(pl.multiple_of((chip * CORES + core) * units, units), units)],
                ff_send.at[which, side],
                ff_recv.at[which, side],
                dp=group_to,
                chip=to // CORES,
                core=lax.rem(to, CORES),
            ).start()
            return nothing

        lax.fori_loop(1 - side, pairs, one, 0)

    def ff_local(which):
        at = chip * CORES + core
        return pltpu.make_async_copy(
            ffg_ref.at[which, pl.ds((dp * pairs + at) * shard, shard)],
            ffin_ref.at[which, dp, :, pl.ds(pl.multiple_of(at * units, units), units)],
            local_sems.at[which],
        )

    os_copies = [
        remote(out_ref.at[at + 1], oin_ref.at[at], os_send.at[at], os_recv.at[at], chip=to)
        for at, to in enumerate(at_chip)
    ]

    def norm_back_rows(inputs, gain, grad):
        scale = lax.rsqrt(jnp.mean(inputs * inputs, axis=1, keepdims=True) + EPS)
        weighted = grad * gain
        back = scale * weighted - inputs * (
            scale * scale * scale * jnp.mean(weighted * inputs, axis=1, keepdims=True)
        )
        return back, jnp.sum(grad * inputs * scale, axis=0, keepdims=True)

    slots = (tab_slots, early_slots, ups_slots, late_slots)
    dp_bufs = (tab_dp, early_dp, ups_dp, late_dp)
    owns = (tab_own, early_own, ups_own, late_own)
    sibs = (tab_sib, early_sib, ups_sib, late_sib)

    def small_copies(which):
        return [
            remote(
                slots[which].at[chip], slots[which].at[chip],
                small_send.at[which, at], small_recv.at[which, at], chip=to,
            )
            for at, to in enumerate(at_chip)
        ]

    def small_start(which, value):
        slots[which][chip] = value.astype(BFLOAT)
        for copy in small_copies(which):
            copy.start()

    def small_across(which):
        return remote(
            dp_bufs[which].at[0], dp_bufs[which].at[1],
            small_dp.at[which, 0], small_dp.at[which, 1], dp=there,
        )

    def small_over(which):
        return remote(owns[which], sibs[which], small_core.at[which, 0], small_core.at[which, 1], **sibling)

    def small_middle(which):
        for copy in small_copies(which):
            copy.wait()
        total = slots[which][0].astype(FLOAT)
        for at in range(1, chips):
            total = total + slots[which][at].astype(FLOAT)
        dp_bufs[which][0] = total.astype(BFLOAT)
        small_across(which).start()

    def small_end(which):
        small_across(which).wait()
        owns[which][...] = dp_bufs[which][0].astype(FLOAT) + dp_bufs[which][1].astype(FLOAT)
        small_over(which).start()

    def grad_copies(source, target, send, recv):
        return [
            remote(
                source.at[pl.ds(((dp if side == 0 else there) * chips + to) * CORES * shard, CORES * shard)],
                target.at[at, side],
                send.at[side, at],
                recv.at[side, at],
                chip=to,
            )
            for at, to in enumerate(at_chip)
            for side in range(2)
        ]

    q_copies = grad_copies(qg, q_in, q_send, q_recv)
    o_copies = grad_copies(og, o_in, o_send, o_recv)
    q_across = remote(q_dp_out, q_dp_in, q_dp_sem.at[0], q_dp_sem.at[1], dp=there)
    o_across = remote(o_dp_out, o_dp_in, o_dp_sem.at[0], o_dp_sem.at[1], dp=there)
    q_over = remote(q_core, qkv_sib, q_core_sem.at[0], q_core_sem.at[1], **sibling)
    o_over = remote(o_core, o_sib, o_core_sem.at[0], o_core_sem.at[1], **sibling)

    def chip_sum(source, target, side):
        group_at = dp if side == 0 else there
        total = source[pl.ds((group_at * chips + chip) * CORES * shard, CORES * shard)].astype(FLOAT)
        for at in range(chips - 1):
            total = total + target[at, side].astype(FLOAT)
        return total

    def grads_middle(copies, source, target, dp_out, across):
        for copy in copies:
            copy.wait_recv()
        dp_out[...] = chip_sum(source, target, 1).astype(BFLOAT)
        across.start()

    def grads_end(source, target, dp_in, across, result, core_out, over):
        across.wait()
        total = chip_sum(source, target, 0) + dp_in[...].astype(FLOAT)
        upper, lower = total[shard:], total[:shard]
        result[...] = jnp.where(core == 0, lower, upper)
        core_out[...] = jnp.where(core == 0, upper, lower).astype(BFLOAT)
        over.start()

    back_rows, gain_row = norm_back_rows(res_ref[...], fgain_ref[...], gnf_ref[...])
    grad_residual = cot_ref[...].astype(FLOAT) + back_rows
    dres[...] = grad_residual
    db[mine] = grad_residual.astype(BFLOAT)
    db_copy = remote(db.at[mine], db.at[mine], db_sem.at[0], db_sem.at[1], **sibling)
    db_copy.start()
    ff_start(0, 1)
    os_copies[0].start()
    for which in range(3):
        ff_local(which).start()
    up_rows = t_product(mid_ref[...], db[mine])[:rank]
    filler = jnp.zeros((16 - 1 - rank, model), FLOAT)
    early_rows = jnp.concatenate([up_rows, gain_row, filler], axis=0)
    db_copy.wait_recv()
    dmid = product_t(db[...], oup_ref[...]).astype(BFLOAT)
    dq[...] = dot(db[...], wof_ref[...]) + product_t(dmid, odown_ref[...])

    def views(at):
        return (
            pl.ds(at * group, group),
            pl.ds(at, 1),
            pl.ds(at * group * HEAD_SIZE, group * HEAD_SIZE),
        )

    for at in range(kv_heads):
        heads, one, wide = views(at)
        grad_numer_kernel(
            group, dq.at[:, wide], att_ref.at[:, wide], den_ref.at[one], phi_q_ref.at[heads], cont_ref,
            dn.at[heads], ds_out.at[heads],
        )
    kept = HEAD_SIZE + 16
    ds_copies = [
        remote(ds_out.at[:, pl.ds(0, kept)], ds_in.at[at], ds_send.at[at], ds_recv.at[at], chip=to)
        for at, to in enumerate([lax.rem(chip + chips - step, chips) for step in range(1, chips)])
    ]
    for copy in ds_copies:
        copy.start()
    small_start(1, early_rows)
    ff_start(0, 0)
    og[...] = t_product(db[...], att_ref[...]).astype(BFLOAT)
    down_rows = t_product(dmid, att_ref[...])[:rank]
    for at in range(kv_heads):
        heads, one, wide = views(at)
        intra_back_kernel(
            group, q_ref.at[:, wide], k_ref.at[one], v_ref.at[one], phi_q_ref.at[heads],
            phi_k_ref.at[heads], dn.at[heads], seg_q_ref, seg_k_ref,
            dq.at[:, wide], dk.at[one], dv.at[one], dphi_q.at[heads], dphi_k.at[heads],
        )
    total = jnp.zeros(ds_in.shape[1:], FLOAT)
    for at, copy in enumerate(ds_copies):
        copy.wait_recv()
        total = total + coef_ref[at] * ds_in[at].astype(FLOAT)
    gstate[:, :kept] = total.astype(BFLOAT)
    gstate[:, kept:] = jnp.zeros((gstate.shape[0], 128 - kept, 128), BFLOAT)
    for at in range(kv_heads):
        heads, one, wide = views(at)
        features_back_kernel(
            group, q_ref.at[:, wide], k_ref.at[one], v_ref.at[one], phi_q_ref.at[heads],
            phi_k_ref.at[heads], dn.at[heads], fq_ref.at[heads], fk_ref.at[heads],
            state_ref.at[heads], gstate.at[heads], cont_ref, carry_ref,
            dq.at[:, wide], dk.at[one], dv.at[one], dphi_q.at[heads], dphi_k.at[heads],
            dq.at[:, wide], dk.at[one], dv.at[one], gq.at[heads], gk.at[heads],
        )

    gap = 128 - SOFTMAX_KEYS

    def joined(rows):
        return jnp.concatenate(
            [dk[head, rows] for head in range(kv_heads)]
            + [dv[head, rows, :HEAD_SIZE] for head in range(kv_heads)],
            axis=1,
        )

    rim_out[...] = joined(slice(gap, 128))
    rim_copy = remote(rim_out, rim_in, rim_sem.at[0], rim_sem.at[1], chip=lax.rem(chip + chips - 1, chips))

    @pl.when(chip > 0)
    def _():
        rim_copy.start()

    tables = []
    for head in range(kv_heads * group):
        pieces = [table[head, :, :FEATURE_HALF] - table[head, :, FEATURE_HALF:] for table in (gq, gk)]
        tables.append(jnp.concatenate(pieces, axis=1))
    small_start(0, jnp.concatenate(tables, axis=0))
    for copy in o_copies:
        copy.start()
    half = HEAD_SIZE // 2
    first_half = lax.rem(lanes((tokens, 128)), HEAD_SIZE) < half

    def unrotated(block):
        turned = jnp.where(first_half, pltpu.roll(block, 128 - half, 1), pltpu.roll(block, half, 1))
        return (block * cos_ref[...] - turned * sin_ref[...]).astype(BFLOAT)

    for at in range(0, q_width, 128):
        gp[:, at : at + 128] = unrotated(dq[:, at : at + 128])

    @pl.when(chip == chips - 1)
    def _():
        rim_in[...] = jnp.zeros(rim_in.shape, FLOAT)

    @pl.when(chip < chips - 1)
    def _():
        rim_copy.wait_recv()

    kv = joined(slice(128, 128 + tokens))
    kv = jnp.concatenate(
        [kv[: tokens - SOFTMAX_KEYS], kv[tokens - SOFTMAX_KEYS :] + rim_in[...]], axis=0
    )
    gp[:, q_width : q_width + 128] = unrotated(kv[:, :128])
    gp[:, q_width + 128 :] = kv[:, 128:].astype(BFLOAT)

    def partial(rows):
        grads = gp[rows]
        return product_t(grads, qkv_ref[...]), product_t(grads, ups_ref[...])

    wide_part, low_part = partial(theirs)
    br_out[:, :model] = wide_part.astype(BFLOAT)
    br_out[:, model:] = low_part.astype(BFLOAT)
    br_copy = remote(br_out, br_in, br_sem.at[0], br_sem.at[1], **sibling)
    br_copy.start()
    wide_part, low_part = partial(mine)
    br_copy.wait()
    tz_out = br_out
    tz_out[:, :model] = (wide_part + br_in[:, :model].astype(FLOAT)).astype(BFLOAT)
    tz_out[:, model:] = (low_part + br_in[:, model:].astype(FLOAT)).astype(BFLOAT)
    tz_copy = remote(tz_out, tz_in, tz_sem.at[0], tz_sem.at[1], tensor=1 - tensor)
    tz_copy.start()
    ff_start(1, 1)
    qg[...] = t_product(normed_ref[...], gp[...]).astype(BFLOAT)
    for copy in q_copies:
        copy.start()
    ups_rows = t_product(low_ref[...], gp[...])[: 3 * rank]
    wide_down = jnp.concatenate(
        [down_rows, jnp.zeros((rank, gp.shape[1] - q_width), FLOAT)], axis=1
    )
    small_start(2, jnp.concatenate([ups_rows, wide_down], axis=0))
    tz_copy.wait_recv()
    low = (tz_out[:, model:].astype(FLOAT) + tz_in[:, model:].astype(FLOAT)).astype(BFLOAT)
    grad_normed = (
        tz_out[:, :model].astype(FLOAT) + tz_in[:, :model].astype(FLOAT)
    ) + product_t(low, downs_ref[...])
    low_rows = t_product(low, normed_ref[mine])[: 3 * rank]
    back_rows, gain_row = norm_back_rows(hid_ref[...].astype(FLOAT), again_ref[...], grad_normed)
    igrad_ref[...] = (dres[...] + back_rows).astype(BFLOAT)
    filler = jnp.zeros((rank - 1, model), FLOAT)
    small_start(3, jnp.concatenate([low_rows, gain_row, filler], axis=0))
    for copy in os_copies[1:]:
        copy.start()
    ff_start(1, 0)
    ff_start(2, 0)
    grads_middle(o_copies, og, o_in, o_dp_out, o_across)
    ff_start(2, 1)
    small_middle(1)
    small_middle(0)
    small_middle(2)
    grads_middle(q_copies, qg, q_in, q_dp_out, q_across)
    small_middle(3)

    os_buf = tz_in.at[:, pl.ds(0, model)]
    load = pltpu.make_async_copy(out_ref.at[0], os_buf, o_load.at[0])
    load.start()
    load.wait()
    dres[...] = os_buf[...].astype(FLOAT)
    for at in range(chips - 1):
        os_copies[at].wait_recv()
        load = pltpu.make_async_copy(oin_ref.at[at], os_buf, o_load.at[0])
        load.start()
        load.wait()
        dres[...] += os_buf[...].astype(FLOAT)
    tz_copy.wait_send()
    oz_out, oz_in = (ref.at[:, pl.ds(0, model)] for ref in (br_out, br_in))
    oz_out[...] = dres[...].astype(BFLOAT)
    oz_copy = remote(oz_out, oz_in, oz_sem.at[0], oz_sem.at[1], tensor=1 - tensor)
    oz_copy.start()
    grads_end(og, o_in, o_dp_in, o_across, o_own, o_core, o_over)
    for which in range(3):
        small_end(which)
    oz_copy.wait()
    block_ref[...] = (
        res_ref[...] + (oz_out[...].astype(FLOAT) + oz_in[...].astype(FLOAT))
    ).astype(BFLOAT)
    grads_end(qg, q_in, q_dp_in, q_across, qkv_own, q_core, q_over)
    small_end(3)

    for copy in [db_copy] + ds_copies + os_copies + q_copies + o_copies:
        copy.wait_send()

    @pl.when(chip > 0)
    def _():
        rim_copy.wait_send()

    for which in range(4):
        small_over(which).wait()
    q_over.wait()
    o_over.wait()
    for which in range(3):
        ff_local(which).wait()
        for side in range(2):
            count = pairs - 1 + side
            group_from = dp if side == 0 else there
            sent = ffg_ref.at[which, pl.ds(0, count * shard)]
            came = ffin_ref.at[which, group_from, :, pl.ds(0, count * units)]
            remote(sent, sent, ff_send.at[which, side], ff_recv.at[which, side], **sibling).wait_send()
            remote(came, came, ff_send.at[which, side], ff_recv.at[which, side], **sibling).wait_recv()


def rear(chips, kv_heads, group, rank, near_args, far_args):
    own, model = near_args[0].shape
    tokens = CORES * own
    heads = kv_heads * group
    q_width = heads * HEAD_SIZE
    qkv_width = q_width + 2 * kv_heads * HEAD_SIZE
    extent = tokens + 128
    pairs = chips * CORES
    shard = model // (2 * pairs)
    units = far_args[1].shape[2]
    near = pl.BlockSpec(memory_space=pltpu.VMEM)
    far = pl.BlockSpec(memory_space=pl.ANY)
    kept = HEAD_SIZE + 16
    smalls = [
        (heads * HEAD_SIZE, 128),
        (16, model),
        (4 * rank, qkv_width),
        (4 * rank, model),
    ]
    near_outs = [
        ((own, model), BFLOAT),
        ((own, model), BFLOAT),
        ((shard, qkv_width), FLOAT),
        ((shard, qkv_width), BFLOAT),
        ((shard, q_width), FLOAT),
        ((shard, q_width), BFLOAT),
    ]
    near_outs += [(shape, FLOAT) for shape in smalls] * 2
    far_outs = [
        ((3, 2, shard, pairs * units), BFLOAT),
        ((chips - 1, own, model), BFLOAT),
    ]
    pair = dma_row(2)
    step_pair = pltpu.SemaphoreType.DMA((2, chips - 1))

    def grads(width):
        return [
            pltpu.VMEM((model, width), BFLOAT),
            pltpu.VMEM((chips - 1, 2, CORES * shard, width), BFLOAT),
            pltpu.VMEM((CORES * shard, width), BFLOAT),
            pltpu.VMEM((CORES * shard, width), BFLOAT),
            pltpu.VMEM((shard, width), BFLOAT),
        ]

    wide = pltpu.VMEM((own, model + 128), BFLOAT)
    return pl.pallas_call(
        functools.partial(rear_kernel, chips, kv_heads, group, rank),
        in_specs=[near] * len(near_args) + [far] * len(far_args),
        out_specs=[near] * len(near_outs) + [far] * len(far_outs),
        out_shape=[jax.ShapeDtypeStruct(*out) for out in near_outs + far_outs],
        scratch_shapes=[
            pltpu.VMEM((tokens, model), BFLOAT),
            pltpu.VMEM((tokens, q_width), FLOAT),
            pltpu.VMEM((heads, tokens, 128), BFLOAT),
            pltpu.VMEM((heads, 128, 128), BFLOAT),
            pltpu.VMEM((chips - 1, heads, kept, 128), BFLOAT),
            pltpu.VMEM((heads, 128, 128), BFLOAT),
            pltpu.VMEM((kv_heads, extent, HEAD_SIZE), FLOAT),
            pltpu.VMEM((kv_heads, extent, 128), FLOAT),
            pltpu.VMEM((heads, tokens, 128), FLOAT),
            pltpu.VMEM((heads, extent, 128), FLOAT),
            pltpu.VMEM((heads, HEAD_SIZE, 128), FLOAT),
            pltpu.VMEM((heads, HEAD_SIZE, 128), FLOAT),
            pltpu.VMEM((own, model), FLOAT),
            pltpu.VMEM((SOFTMAX_KEYS, 256), FLOAT),
            pltpu.VMEM((SOFTMAX_KEYS, 256), FLOAT),
            pltpu.VMEM((tokens, qkv_width), BFLOAT),
            wide,
            wide,
            wide,
        ]
        + grads(qkv_width)
        + grads(q_width)
        + [pltpu.VMEM((chips,) + shape, BFLOAT) for shape in smalls]
        + [pltpu.VMEM((2,) + shape, BFLOAT) for shape in smalls]
        + [
            pair,
            dma_row(chips - 1),
            dma_row(chips - 1),
            pair,
            pair,
            pair,
            pair,
            dma_row(1),
            dma_row(chips - 1),
            dma_row(chips - 1),
            step_pair,
            step_pair,
            pair,
            pair,
            step_pair,
            step_pair,
            pair,
            pair,
            pltpu.SemaphoreType.DMA((4, chips - 1)),
            pltpu.SemaphoreType.DMA((4, chips - 1)),
            pltpu.SemaphoreType.DMA((4, 2)),
            pltpu.SemaphoreType.DMA((4, 2)),
            pltpu.SemaphoreType.DMA((3, 2)),
            pltpu.SemaphoreType.DMA((3, 2)),
            dma_row(3),
        ],
        compiler_params=pltpu.CompilerParams(
            vmem_limit_bytes=63 * 1024 * 1024, collective_id=3, has_side_effects=True
        ),
        cost_estimate=pl.CostEstimate(
            flops=int(4e10), bytes_accessed=int(1e8), transcendentals=0
        ),
    )(*near_args, *far_args)


def carry_coefs(lengths, tokens):
    chips = lax.axis_size("chip")
    me = lax.axis_index("chip")
    steps = jnp.arange(1, chips, dtype=jnp.int32)
    behind, ahead = lax.rem(me + chips - steps, chips), lax.rem(me + steps, chips)
    places = jnp.stack(
        [behind * tokens + tokens - 1, ahead * tokens - 1, 0 * steps + me * tokens - 1]
        + [0 * steps + me * tokens + tokens - 1]
    )
    segment = locate(places, lengths)[0]
    forward = (behind < me) & (segment[0] == segment[2])
    backward = (ahead > me) & (segment[1] == segment[3])
    return [
        jnp.broadcast_to(row.astype(FLOAT)[:, None, None], (chips - 1, 1, 128))
        for row in (forward, backward)
    ]


def on_device(
    hidden_in,
    doc_lengths,
    attention_gain,
    query_weight,
    key_projection,
    value_projection,
    output_weight,
    query_down,
    query_up,
    key_down,
    key_adapter_up,
    value_down,
    value_adapter_up,
    output_down,
    output_up,
    query_feature_maps,
    key_feature_maps,
    feedforward_gain,
    gate_weight,
    up_weight,
    down_weight,
    block_cotangent,
):
    own_rows, model = hidden_in.shape
    tokens = own_rows * CORES
    core = lax.axis_index("core")
    chip = lax.axis_index("chip")
    chips = lax.axis_size("chip")
    heads = query_feature_maps.shape[0] // CORES
    kv_heads = key_projection.shape[1] // HEAD_SIZE // CORES
    group = heads // kv_heads
    q_width = heads * HEAD_SIZE
    kv_width = kv_heads * HEAD_SIZE
    rank = query_down.shape[1]

    def own_cols(value, width, which):
        return lax.dynamic_slice_in_dim(value, which * width, width, 1)

    def own_heads(value, count, which):
        return lax.dynamic_slice_in_dim(value, which * count, count, 0)

    wqkv = jnp.stack(
        [
            jnp.concatenate(
                [
                    own_cols(query_weight, q_width, which),
                    own_cols(key_projection, kv_width, which),
                    own_cols(value_projection, kv_width, which),
                ],
                axis=1,
            )
            for which in range(CORES)
        ]
    )
    wout = output_weight.reshape(CORES, q_width, -1).transpose(0, 2, 1)
    qkv_width = q_width + 2 * kv_width

    first_row = chip * tokens
    lengths = doc_lengths[0]
    gap = 128 - SOFTMAX_KEYS
    spots = jnp.arange(tokens + 128, dtype=jnp.int32)
    seg_ext, pos_ext = locate(first_row + spots - 128, lengths)
    seg_ext = jnp.where(spots < gap, -2, seg_ext)
    seg_rows, pos_rows = seg_ext[128:], pos_ext[128:]
    seg_first = locate(first_row - 1, lengths)[0]
    seg_last = locate(first_row + tokens - 1, lengths)[0]
    continuing = (seg_rows == seg_first).astype(FLOAT)[:, None]
    carry = ((jnp.arange(tokens + 128) < tokens + gap) & (seg_ext == seg_last)).astype(FLOAT)[:, None]
    seg_column, seg_line = seg_rows[:, None], seg_ext[None, :]
    forward_coefs, backward_coefs = carry_coefs(lengths, tokens)
    wide_cosine, wide_sine = rotation(pos_rows, HEAD_SIZE)
    query_table = own_heads(query_feature_maps, heads, core)
    key_table = own_heads(key_feature_maps, heads, core)
    query_table = jnp.concatenate([query_table, -query_table], axis=2)
    key_table = jnp.concatenate([key_table, -key_table], axis=2)
    downs = jnp.concatenate([query_down, key_down, value_down], axis=1)
    own_query_up = own_cols(query_up, q_width, core)
    own_key_up = own_cols(key_adapter_up, kv_width, core)
    own_value_up = own_cols(value_adapter_up, kv_width, core)
    own_output_down = own_heads(output_down, q_width, core)
    pad = 128 - 3 * rank
    ups = jnp.concatenate(
        [
            jnp.pad(own_query_up, ((0, 0), (0, 2 * kv_width))),
            jnp.pad(own_key_up, ((0, 0), (q_width, kv_width))),
            jnp.pad(own_value_up, ((0, 0), (q_width + kv_width, 0))),
            jnp.zeros((pad, qkv_width), BFLOAT),
        ],
        axis=0,
    )
    extent = tokens + 128
    wide_downs = jnp.pad(downs, ((0, 0), (0, pad)))
    wide_output_down = jnp.pad(own_output_down, ((0, 0), (0, 128 - rank)))
    wide_output_up = jnp.pad(output_up, ((0, 128 - rank), (0, 0)))
    (
        full_qkv, full_out, normed, low_rank, low_mid, residual, queries, key_ext, value_ext,
        phi_q, phi_k, attended, denominator, state, normed_ff, full_ff, cotangents,
    ) = front(
        chips,
        kv_heads,
        group,
        tokens,
        [
            hidden_in,
            attention_gain[None],
            feedforward_gain[None],
            wide_downs,
            ups,
            wide_cosine,
            wide_sine,
            query_table,
            key_table,
            seg_column,
            seg_line,
            continuing,
            carry,
            forward_coefs,
            wide_output_down,
            wide_output_up,
        ],
        [wqkv, wout, gate_weight, up_weight, down_weight.T, block_cotangent],
    )
    grad_normed_ff, out_sums, ff_grads, _, _ = feed(normed_ff, cotangents, full_ff)
    rear_outs = rear(
        chips,
        kv_heads,
        group,
        rank,
        [
            grad_normed_ff,
            residual,
            block_cotangent,
            hidden_in,
            attention_gain[None],
            feedforward_gain[None],
            full_out,
            wide_output_down[:, :16],
            wide_output_up[:16],
            low_mid,
            attended,
            denominator,
            queries,
            key_ext,
            value_ext,
            phi_q,
            phi_k,
            query_table,
            key_table,
            state,
            seg_column,
            seg_line,
            continuing,
            carry,
            backward_coefs,
            wide_cosine,
            wide_sine,
            normed,
            low_rank,
            full_qkv,
            ups,
            wide_downs,
        ],
        [out_sums, ff_grads],
    )
    block_output, input_grad, qkv_keep, qkv_other, out_keep, out_other = rear_outs[:6]
    own_small, sib_small = rear_outs[6:10], rear_outs[10:14]
    qkv_other, out_other = qkv_other.astype(FLOAT), out_other.astype(FLOAT)

    def by_core(dim, mine, other):
        return ordered(core, mine, other, dim)

    at_key, at_value = q_width, q_width + kv_width
    query_shard = by_core(1, qkv_keep[:, :at_key], qkv_other[:, :at_key])
    key_shard = by_core(1, qkv_keep[:, at_key:at_value], qkv_other[:, at_key:at_value])
    value_shard = by_core(1, qkv_keep[:, at_value:], qkv_other[:, at_value:])
    output_shard = by_core(1, out_keep, out_other).T
    ff_both = rear_outs[14]
    ff_shards = [ff_both[at, 0].astype(FLOAT) + ff_both[at, 1].astype(FLOAT) for at in range(3)]

    tables = by_core(0, own_small[0], sib_small[0]).reshape(CORES * heads, HEAD_SIZE, 128)
    early = own_small[1] + sib_small[1]
    late = own_small[3] + sib_small[3]
    ups_mine, ups_other = own_small[2], sib_small[2]

    def ups_part(row, start, stop):
        rows = slice(row * rank, (row + 1) * rank)
        return by_core(1, ups_mine[rows, start:stop], ups_other[rows, start:stop])

    downs_total = late[: 3 * rank].T
    return (
        block_output,
        input_grad,
        late[3 * rank],
        query_shard,
        key_shard,
        value_shard,
        output_shard,
        downs_total[:, :rank],
        ups_part(0, 0, at_key),
        downs_total[:, rank : 2 * rank],
        ups_part(1, at_key, at_value),
        downs_total[:, 2 * rank :],
        ups_part(2, at_value, qkv_width),
        ups_part(3, 0, at_key).T,
        early[:rank],
        tables[:, :, :FEATURE_HALF],
        tables[:, :, FEATURE_HALF:],
        early[rank],
        ff_shards[0],
        ff_shards[1],
        ff_shards[2].T,
    )


def solution(mesh):
    dp, seq, tensor = (mesh.shape[name] for name in ("dp", "seq", "tensor"))
    split = Mesh(
        mesh.devices.reshape(dp, seq // CORES, CORES, tensor), ("dp", "chip", "core", "tensor")
    )
    tok = ("dp", "chip", "core")
    in_specs = (
        P(tok, None),
        P("dp", None),
        P(),
        P(tok, "tensor"),
        P(tok, "tensor"),
        P(tok, "tensor"),
        P("tensor", tok),
        P(),
        P(None, "tensor"),
        P(),
        P(None, "tensor"),
        P(),
        P(None, "tensor"),
        P("tensor", None),
        P(),
        P("tensor", None, None),
        P("tensor", None, None),
        P(),
        P(tok, "tensor"),
        P(tok, "tensor"),
        P("tensor", tok),
        P(tok, None),
    )
    out_specs = (
        P(tok, None),
        P(tok, None),
        P(),
        P(tok, "tensor"),
        P(tok, "tensor"),
        P(tok, "tensor"),
        P("tensor", tok),
        P(),
        P(None, "tensor"),
        P(),
        P(None, "tensor"),
        P(),
        P(None, "tensor"),
        P("tensor", None),
        P(),
        P("tensor", None, None),
        P("tensor", None, None),
        P(),
        P(tok, "tensor"),
        P(tok, "tensor"),
        P("tensor", tok),
    )
    return jax.shard_map(
        on_device, mesh=split, in_specs=in_specs, out_specs=out_specs, check_vma=False
    )
```

```python
import functools

import jax
import jax.numpy as jnp
import numpy as np
from jax import lax
from jax.experimental import pallas as pl
from jax.experimental.pallas import tpu as pltpu
from jax.sharding import Mesh
from jax.sharding import PartitionSpec as P

HEAD_SIZE = 64
FEATURE_HALF = 64
SOFTMAX_KEYS = 64
CORES = 2


EPS = 1e-05
FLOAT = jnp.float32
BFLOAT = jnp.bfloat16


def ordered(which, mine, other, dim):
    return jnp.where(
        which == 0,
        jnp.concatenate([mine, other], axis=dim),
        jnp.concatenate([other, mine], axis=dim),
    )


def frequencies(head_width):
    inverse = 1.0 / 500000.0 ** (np.arange(0, head_width, 2) / head_width)
    wavelen = 2.0 * np.pi / inverse
    smooth = (8192.0 / wavelen - 1.0) / 3.0
    blended = (1.0 - smooth) * inverse / 32.0 + smooth * inverse
    return np.where(wavelen > 8192.0, inverse / 32.0, np.where(wavelen < 2048.0, inverse, blended))


def rotation(positions, head_width):
    table = np.tile(frequencies(head_width), 4)[None].astype(np.float32)
    sign = np.tile(np.repeat([-1.0, 1.0], head_width // 2), 2)[None].astype(np.float32)
    turned = positions.astype(FLOAT)[:, None] * table
    return jnp.cos(turned), jnp.sin(turned) * sign


def locate(places, lengths):
    segment, begin, end = jnp.zeros_like(places), jnp.zeros_like(places), 0
    for at in range(lengths.shape[0]):
        end = end + lengths[at]
        segment = segment + (places >= end).astype(jnp.int32)
        begin = jnp.where(places >= end, end, begin)
    return (jnp.where(places < 0, -1, segment), places - begin)


def product(left, right):
    return jnp.dot(left, right, preferred_element_type=FLOAT)


def product_t(left, right):
    return lax.dot_general(left, right, (((1,), (1,)), ((), ())), preferred_element_type=FLOAT)


def t_product(left, right):
    return lax.dot_general(left, right, (((0,), (0,)), ((), ())), preferred_element_type=FLOAT)


def dot(left, right):
    return lax.dot_general(left, right, (((1,), (0,)), ((), ())), preferred_element_type=FLOAT)


def lanes(shape):
    return lax.broadcasted_iota(jnp.int32, shape, 1)


def half_sums(rows):
    first = lax.broadcasted_iota(jnp.int32, (128, 128), 0) < FEATURE_HALF
    ones = jnp.where(first == (lanes((128, 128)) < FEATURE_HALF), 1.0, 0.0).astype(BFLOAT)
    return dot(rows, ones)


def two_softmax(mixed):
    low = lanes(mixed.shape) < FEATURE_HALF
    top = jnp.max(jnp.where(low, mixed, -jnp.inf), axis=1, keepdims=True)
    top_other = jnp.max(jnp.where(low, -jnp.inf, mixed), axis=1, keepdims=True)
    raised = jnp.exp(mixed - jnp.where(low, top, top_other))
    return (raised / half_sums(raised.astype(BFLOAT))).astype(BFLOAT)


def phi_kernel(group, q_ref, k_ref, vm_ref, fq_ref, fk_ref, phi_q_ref, phi_k_ref, state_ref):
    keys = k_ref[0]
    masked = vm_ref[0]
    for head in range(group):
        rows = q_ref[:, head * HEAD_SIZE : (head + 1) * HEAD_SIZE]
        phi_q_ref[head] = two_softmax(dot(rows, fq_ref[head]))
        phi_k = two_softmax(dot(keys, fk_ref[head]))
        phi_k_ref[head] = phi_k
        state_ref[head] = t_product(masked, phi_k).astype(BFLOAT)


def tile_masks(seg_q, seg_k, at):
    width = at + 256
    same = seg_q == seg_k[:, :width]
    row = lax.broadcasted_iota(jnp.int32, (128, 256), 0)
    col = lanes((128, 256))
    earlier = col <= row + SOFTMAX_KEYS
    window = (col > row + SOFTMAX_KEYS) & (col <= row + 128) & same[:, at:]
    return same[:, :at], window, earlier & same[:, at:]


def tile_weights(rows, phi_rows, k_ref, phi_k, at, masks):
    far, window, earlier = masks
    scale = HEAD_SIZE ** (-0.5)
    raw = product_t(rows, k_ref[0, at : at + 256])
    window_exp = jnp.where(window, jnp.exp(jnp.where(window, scale * raw, 0.0)), 0.0)
    linear = product_t(phi_rows, phi_k[: at + 256])
    near = jnp.where(earlier, linear[:, at:], window_exp)
    if at == 0:
        return window_exp, near.astype(BFLOAT)
    return window_exp, jnp.concatenate(
        [jnp.where(far, linear[:, :at], 0.0), near], axis=1
    ).astype(BFLOAT)


def intra_kernel(group, q_ref, k_ref, v_ref, phi_q_ref, phi_k_ref, seg_q_ref, seg_k_ref, num_ref):
    for at in range(0, q_ref.shape[0], 128):
        masks = tile_masks(seg_q_ref[at : at + 128], seg_k_ref[...], at)
        for head in range(group):
            rows = q_ref[at : at + 128, head * HEAD_SIZE : (head + 1) * HEAD_SIZE]
            weights = tile_weights(
                rows, phi_q_ref[head, at : at + 128], k_ref, phi_k_ref.at[head], at, masks
            )[1]
            num_ref[head, at : at + 128] = dot(weights, v_ref[0, : at + 256])


def finish_kernel(group, num_ref, phi_q_ref, state_ref, cont_ref, att_ref, den_ref):
    cont = cont_ref[...]
    den = jnp.zeros(den_ref.shape[1:], FLOAT)
    for head in range(group):
        total = num_ref[head] + cont * product_t(phi_q_ref[head], state_ref[head])
        below = total[:, HEAD_SIZE : HEAD_SIZE + 1]
        att_ref[:, head * HEAD_SIZE : (head + 1) * HEAD_SIZE] = (
            total[:, :HEAD_SIZE] / below
        ).astype(BFLOAT)
        den = jnp.where(lanes(den.shape) == head, below, den)
    den_ref[0] = den


def grad_numer_kernel(group, da_ref, att_ref, den_ref, phi_q_ref, cont_ref, dn_ref, ds_ref):
    cont = cont_ref[...]
    for head in range(group):
        cols = slice(head * HEAD_SIZE, (head + 1) * HEAD_SIZE)
        numer = da_ref[:, cols] / den_ref[0][:, head : head + 1]
        denom = -jnp.sum(numer * att_ref[:, cols].astype(FLOAT), axis=1, keepdims=True)
        high = denom.astype(BFLOAT).astype(FLOAT)
        wide = jnp.concatenate([numer, jnp.zeros_like(numer)], axis=1)
        lane = lanes(wide.shape)
        wide = jnp.where(lane == HEAD_SIZE, high, wide)
        wide = jnp.where(lane == HEAD_SIZE + 1, denom - high, wide)
        dn_ref[head] = wide.astype(BFLOAT)
        state = t_product((wide * cont).astype(BFLOAT), phi_q_ref[head])
        row = lax.broadcasted_iota(jnp.int32, state.shape, 0)
        both = state[HEAD_SIZE : HEAD_SIZE + 1] + state[HEAD_SIZE + 1 : HEAD_SIZE + 2]
        state = jnp.where(row == HEAD_SIZE, both, jnp.where(row > HEAD_SIZE, 0.0, state))
        ds_ref[head] = state.astype(BFLOAT)


def intra_back_kernel(
    group, q_ref, k_ref, v_ref, phi_q_ref, phi_k_ref, dn_ref, seg_q_ref, seg_k_ref,
    dq_ref, dk_ref, dv_ref, dphi_q_ref, dphi_k_ref,
):
    scale = HEAD_SIZE ** (-0.5)
    dk_ref[...] = jnp.zeros(dk_ref.shape, FLOAT)
    dv_ref[...] = jnp.zeros(dv_ref.shape, FLOAT)
    dphi_k_ref[...] = jnp.zeros(dphi_k_ref.shape, FLOAT)
    for at in range(0, q_ref.shape[0], 128):
        masks = tile_masks(seg_q_ref[at : at + 128], seg_k_ref[...], at)
        tile = slice(at, at + 128)
        width = at + 256
        for head in range(group):
            cols = slice(head * HEAD_SIZE, (head + 1) * HEAD_SIZE)
            rows = q_ref[tile, cols]
            phi_rows = phi_q_ref[head, tile]
            numer = dn_ref[head, tile]
            window_exp, weights = tile_weights(
                rows, phi_rows, k_ref, phi_k_ref.at[head], at, masks
            )
            grad = product_t(numer, v_ref[0, :width])
            near = grad[:, at:]
            grad_raw = (scale * near * window_exp).astype(BFLOAT)
            grad_linear = jnp.where(masks[2], near, 0.0)
            if at > 0:
                grad_linear = jnp.concatenate(
                    [jnp.where(masks[0], grad[:, :at], 0.0), grad_linear], axis=1
                )
            grad_linear = grad_linear.astype(BFLOAT)
            dv_ref[0, :width] += t_product(weights, numer)
            dphi_q_ref[head, tile] = dot(grad_linear, phi_k_ref[head, :width])
            dphi_k_ref[head, :width] += t_product(grad_linear, phi_rows)
            dq_ref[tile, cols] = dot(grad_raw, k_ref[0, at:width])
            dk_ref[0, at:width] += t_product(grad_raw, rows)


def softmax_back(phi, grad):
    wide = phi.astype(FLOAT)
    terms = grad * wide
    high = terms.astype(BFLOAT)
    low = (terms - high.astype(FLOAT)).astype(BFLOAT)
    mean = (half_sums(high) + half_sums(low)) / half_sums(phi)
    return (wide * (grad - mean)).astype(BFLOAT)


def features_back_kernel(
    group, q_ref, k_ref, v_ref, phi_q_ref, phi_k_ref, dn_ref, fq_ref, fk_ref, state_ref, ds_ref,
    cont_ref, carry_ref, dq_in, dk_in, dv_in, dphi_q_ref, dphi_k_ref,
    dq_ref, dk_ref, dv_ref, gq_ref, gk_ref,
):
    cont = cont_ref[...]
    carry = carry_ref[...]
    keys = k_ref[0]
    dk = dk_in[0]
    dv = dv_in[0]
    for head in range(group):
        cols = slice(head * HEAD_SIZE, (head + 1) * HEAD_SIZE)
        grad_state = ds_ref[head]
        phi_k = phi_k_ref[head]
        grad_q = dphi_q_ref[head] + cont * dot(dn_ref[head], state_ref[head])
        grad_k = dphi_k_ref[head] + carry * dot(v_ref[0], grad_state)
        dv = dv + carry * product_t(phi_k, grad_state)
        mixed_q = softmax_back(phi_q_ref[head], grad_q)
        mixed_k = softmax_back(phi_k, grad_k)
        dq_ref[:, cols] = dq_in[:, cols] + product_t(mixed_q, fq_ref[head])
        dk = dk + product_t(mixed_k, fk_ref[head])
        gq_ref[head] = t_product(q_ref[:, cols], mixed_q)
        gk_ref[head] = t_product(keys, mixed_k)
    dk_ref[0] = dk
    dv_ref[0] = dv


def remote(source, target, send_sem, recv_sem, **where):
    return pltpu.make_async_remote_copy(
        src_ref=source,
        dst_ref=target,
        send_sem=send_sem,
        recv_sem=recv_sem,
        device_id=where,
        device_id_type=pl.DeviceIdType.MESH,
    )


def greet(peers):
    barrier = pltpu.get_barrier_semaphore()
    for where in peers:
        pl.semaphore_signal(barrier, inc=1, device_id=where, device_id_type=pl.DeviceIdType.MESH)
    pl.semaphore_wait(barrier, len(peers))


def even_chip(chip):
    return 1 - lax.rem(chip, 2)


def slot_of(chips, chip, step):
    if chips != 4:
        return step
    even = even_chip(chip)
    return lax.rem(even * step + (1 - even) * (chips - step), chips)


def row_copies(chips, chip, source, target, send, recv):
    own = source.shape[0]

    def one(piece, step, rows, at, to):
        return remote(piece, target.at[step, rows], send.at[at], recv.at[at], chip=to)

    every = pl.ds(0, own)
    if chips != 4:
        to = [lax.rem(chip + chips - step, chips) for step in range(1, chips)]
        return [one(source, step + 1, every, step, at) for step, at in enumerate(to)], []
    even = even_chip(chip)
    beside = 3 - 2 * even
    across = chip - 1 + 2 * even
    along = chip + 2 - 4 * (chip // 2)
    upper, lower = pl.ds(0, own // 2), pl.ds(own // 2, own // 2)
    return [
        one(source, chips - beside, every, 0, across),
        one(source, 2, every, 1, along),
    ], [
        one(target.at[beside, upper], chips - beside, upper, 2, along),
        one(target.at[2, lower], beside, lower, 3, across),
    ]


def relay(copies):
    for at, copy in enumerate(copies[1]):
        copies[0][at].wait_recv()
        copy.start()


def forward_copies(chips, chip, core, source, target, send, recv):
    own = source.shape[0]
    copies = []
    for at in range(chips):
        slot = slot_of(chips, chip, at) if at > 0 else 0
        piece = target.at[slot, pl.ds(0, own)] if at > 0 else source
        copies.append(
            remote(piece, target.at[slot, pl.ds(own, own)], send.at[at], recv.at[at], core=1 - core)
        )
    return copies


def hand_over(copies, forwards):
    if copies[1]:
        forwards[1].start()
        forwards[2].start()
        for copy in copies[1]:
            copy.wait_recv()
        forwards[3].start()
    else:
        for copy, forward in zip(copies[0], forwards[1:]):
            copy.wait_recv()
            forward.start()


def feed_kernel(
    chips, x_ref, c_ref, ff_ref,
    grad_ref, out_ref, ffg_ref, got_ref, xall_ref,
    x_buf, c_buf, gg_ref, gu_ref, gd_ref, keep, sib_out, sib_in, part, stage, cross_in,
    load_sems, stage_sems, sib_send, sib_recv, part_send, part_recv, cross_sems, ffg_sems, free_sem,
    x_send, x_recv, xf_send, xf_recv, x_sem,
):
    core, chip, tensor = (lax.axis_index(name) for name in ("core", "chip", "tensor"))
    rows = keep.shape[2]
    count, model = x_buf.shape[1:]
    units = ff_ref.shape[2]
    gate_ref, up_ref, down_ref = (ff_ref.at[which] for which in range(3))
    sibling = {"core": 1 - core}
    greet(
        [sibling, {"tensor": 1 - tensor}]
        + [{"chip": lax.rem(chip + step, chips)} for step in range(1, chips)]
    )

    def place(step):
        return slot_of(chips, chip, step)

    def load(step, which):
        slot = lax.rem(step, 2)
        ref, buf = ((xall_ref, x_buf), (c_ref, c_buf))[which]
        return pltpu.make_async_copy(ref.at[place(step)], buf.at[slot], load_sems.at[which, slot])

    x_copies = row_copies(chips, chip, x_ref, xall_ref, x_send, x_recv)
    x_forward = forward_copies(chips, chip, core, x_ref, xall_ref, xf_send, xf_recv)
    x_local = pltpu.make_async_copy(x_ref, xall_ref.at[0, pl.ds(0, rows)], x_sem)

    def came(step):
        half = xall_ref.at[place(step), pl.ds(rows, rows)]
        remote(half, half, xf_send.at[step], xf_recv.at[step], **sibling).wait_recv()

    def advance(step):
        if chips == 4:

            @pl.when(step == 0)
            def _():
                relay(x_copies)
                x_forward[1].start()
                x_forward[2].start()

            @pl.when(step == 2)
            def _():
                for copy in x_copies[1]:
                    copy.wait_recv()
                x_forward[3].start()

        else:
            for at, copy in enumerate(x_copies[0]):

                @pl.when(step == at)
                def _(at=at, copy=copy):
                    copy.wait_recv()
                    x_forward[at + 1].start()

    def to_sibling(step):
        slot = lax.rem(step, 2)
        return remote(
            sib_out.at[slot], sib_in.at[slot], sib_send.at[slot], sib_recv.at[slot], **sibling
        )

    def stage_copy(step):
        slot = lax.rem(step, 2)
        return pltpu.make_async_copy(stage.at[slot], out_ref.at[place(step)], stage_sems.at[slot])

    halves = [pl.ds(0, rows // 2), pl.ds(rows // 2, rows // 2)]

    def to_chip(step):
        slot = place(step)
        return [
            remote(
                part.at[step - 1, piece],
                got_ref.at[slot - 1, piece],
                part_send.at[step - 1, at],
                part_recv.at[slot - 1, at],
                chip=lax.rem(chip + slot, chips),
            )
            for at, piece in enumerate(halves)
        ]

    def send_part(step):
        for copy in to_chip(step):
            copy.start()

    def total(step, which):
        slot = lax.rem(step, 2)
        return keep[slot, which].astype(FLOAT) + sib_in[slot, which].astype(FLOAT)

    x_local.start()
    x_forward[0].start()
    for copy in x_copies[0]:
        copy.start()
    load(0, 1).start()
    gg_ref[...] = jnp.zeros(gg_ref.shape, FLOAT)
    gu_ref[...] = jnp.zeros(gu_ref.shape, FLOAT)
    gd_ref[...] = jnp.zeros(gd_ref.shape, FLOAT)

    def body(step, nothing):
        slot = lax.rem(step, 2)
        came(step)
        load(step, 0).start()
        load(step, 1).wait()

        @pl.when(step < chips - 1)
        def _():
            load(step + 1, 1).start()

        load(step, 0).wait()
        tokens = x_buf[slot]
        cotangent = c_buf[slot]
        gate = dot(tokens, gate_ref[...])
        up = dot(tokens, up_ref[...])
        grad = dot(cotangent, down_ref[...])
        sigmoid = 1.0 / (1.0 + jnp.exp(-gate))
        silu = gate * sigmoid
        hidden = (silu * up).astype(BFLOAT)
        grad_gate = (grad * up * (sigmoid + silu * (1.0 - sigmoid))).astype(BFLOAT)
        grad_up = (grad * silu).astype(BFLOAT)

        @pl.when(step >= 2)
        def _():
            to_sibling(step).wait_send()
            pl.semaphore_wait(free_sem, 1)

        @pl.when(step > 0)
        def _():
            advance(step)

        def back(part_of):
            return (
                product_t(grad_gate[part_of], gate_ref[...])
                + product_t(grad_up[part_of], up_ref[...])
            ).astype(BFLOAT)

        def out(part_of):
            return product_t(hidden[part_of], down_ref[...]).astype(BFLOAT)

        mine, theirs = slice(0, rows), slice(rows, 2 * rows)
        sib_out[slot, 0] = back(theirs)
        sib_out[slot, 1] = out(theirs)
        to_sibling(step).start()
        keep[slot, 0] = back(mine)
        keep[slot, 1] = out(mine)

        @pl.when(step > 0)
        def _():
            before = step - 1
            to_sibling(before).wait_recv()

            @pl.when(before == 0)
            def _():
                grad_ref[...] = total(before, 0)

            @pl.when(before > 0)
            def _():
                part[before - 1] = total(before, 0).astype(BFLOAT)
                send_part(before)

            @pl.when(step > 2)
            def _():
                stage_copy(before).wait()

            stage[lax.rem(before, 2)] = total(before, 1).astype(BFLOAT)
            stage_copy(before).start()
            pl.semaphore_signal(free_sem, inc=1, device_id=sibling, device_id_type=pl.DeviceIdType.MESH)

        gg_ref[...] += t_product(tokens, grad_gate)
        gu_ref[...] += t_product(tokens, grad_up)
        gd_ref[...] += t_product(cotangent, hidden)

        @pl.when(step == 0)
        def _():
            advance(step)

        return nothing

    x_local.wait()
    lax.fori_loop(0, chips, body, 0)
    last = chips - 1
    to_sibling(last).wait_recv()
    part[last - 1] = total(last, 0).astype(BFLOAT)
    send_part(last)
    if chips > 2:
        stage_copy(last).wait()
    stage[last % 2] = total(last, 1).astype(BFLOAT)
    stage_copy(last).start()
    per = model // units
    ffg_copies = []
    for which, ref in enumerate((gg_ref, gu_ref, gd_ref)):
        for at in range(model // count):
            place_at = which * (model // count) + at
            buf = (x_buf, c_buf)[place_at // (2 * per)]
            spot = buf.at[(place_at // per) % 2, :, pl.ds((place_at % per) * units, units)]
            piece = pl.ds(at * count, count)
            spot[...] = ref[piece].astype(BFLOAT)
            copy = pltpu.make_async_copy(spot, ffg_ref.at[which, piece], ffg_sems.at[place_at])
            copy.start()
            ffg_copies.append(copy)

    wide = keep.at[0, 0]
    across = []
    for at, piece in enumerate(halves):

        def finish(step, nothing, at=at, piece=piece):
            to_chip(step)[at].wait_recv()
            fetch = pltpu.make_async_copy(
                got_ref.at[place(step) - 1, piece], wide.at[piece], load_sems.at[0, 0]
            )
            fetch.start()
            fetch.wait()
            grad_ref[piece] += wide[piece].astype(FLOAT)
            return nothing

        lax.fori_loop(1, chips, finish, 0)
        wide[piece] = grad_ref[piece].astype(BFLOAT)
        across.append(
            remote(
                wide.at[piece], cross_in.at[piece], cross_sems.at[0, at], cross_sems.at[1, at],
                tensor=1 - tensor,
            )
        )
        across[at].start()

    def drain(step, nothing):
        for copy in to_chip(step):
            copy.wait_send()
        return nothing

    lax.fori_loop(1, chips, drain, 0)
    for copy in x_copies[0] + x_copies[1] + x_forward:
        copy.wait_send()
    for copy in ffg_copies:
        copy.wait()
    for step in range(max(0, chips - 2), chips):
        to_sibling(step).wait_send()
        stage_copy(step).wait()
    pl.semaphore_wait(free_sem, min(1, chips - 1))
    for at, piece in enumerate(halves):
        across[at].wait()
        grad_ref[piece] = wide[piece].astype(FLOAT) + cross_in[piece].astype(FLOAT)


def feed(tokens, cotangent, weights):
    chips, count, model = cotangent.shape
    rows = count // CORES
    units = weights.shape[2]
    near = pl.BlockSpec(memory_space=pltpu.VMEM)
    far = pl.BlockSpec(memory_space=pl.ANY)
    return pl.pallas_call(
        functools.partial(feed_kernel, chips),
        in_specs=[near, far, near],
        out_specs=[near, far, far, far, far],
        out_shape=[
            jax.ShapeDtypeStruct((rows, model), FLOAT),
            jax.ShapeDtypeStruct((chips, rows, model), BFLOAT),
            jax.ShapeDtypeStruct(weights.shape, BFLOAT),
            jax.ShapeDtypeStruct((chips - 1, rows, model), BFLOAT),
            jax.ShapeDtypeStruct((chips, count, model), BFLOAT),
        ],
        scratch_shapes=[
            pltpu.VMEM((2, count, model), BFLOAT),
            pltpu.VMEM((2, count, model), BFLOAT),
            pltpu.VMEM((model, units), FLOAT),
            pltpu.VMEM((model, units), FLOAT),
            pltpu.VMEM((model, units), FLOAT),
            pltpu.VMEM((2, 2, rows, model), BFLOAT),
            pltpu.VMEM((2, 2, rows, model), BFLOAT),
            pltpu.VMEM((2, 2, rows, model), BFLOAT),
            pltpu.VMEM((chips - 1, rows, model), BFLOAT),
            pltpu.VMEM((2, rows, model), BFLOAT),
            pltpu.VMEM((rows, model), BFLOAT),
            pltpu.SemaphoreType.DMA((2, 2)),
            dma_row(2),
            dma_row(2),
            dma_row(2),
            pltpu.SemaphoreType.DMA((chips - 1, 2)),
            pltpu.SemaphoreType.DMA((chips - 1, 2)),
            pltpu.SemaphoreType.DMA((2, 2)),
            dma_row(3 * model // count),
            pltpu.SemaphoreType.REGULAR,
            dma_row(chips),
            dma_row(chips),
            dma_row(chips),
            dma_row(chips),
            pltpu.SemaphoreType.DMA,
        ],
        compiler_params=pltpu.CompilerParams(
            vmem_limit_bytes=62 * 1024 * 1024, collective_id=1, has_side_effects=True
        ),
        cost_estimate=pl.CostEstimate(
            flops=18 * chips * count * model * units,
            bytes_accessed=8 * chips * count * model,
            transcendentals=0,
        ),
    )(tokens, cotangent, weights)


def dma_row(count):
    return pltpu.SemaphoreType.DMA((count,))


def front_kernel(
    chips, kv_heads, group,
    hid_ref, again_ref, fgain_ref, downs_ref, ups_ref, cos_ref, sin_ref, fq_ref, fk_ref,
    seg_q_ref, seg_k_ref, cont_ref, carry_ref, coef_ref, odown_ref, oup_ref,
    wqkv_ref, wo_ref, gate_ref, up_ref, down_ref, cot_ref,
    qkv_ref, wof_ref, normed_ref, low_ref, mid_ref, res_ref, q_ref, k_ref, v_ref,
    phi_q_ref, phi_k_ref, att_ref, den_ref, state_ref,
    xn, ff_ref, call_ref,
    hid_sib, vm, rim_out, rim_in, st_out, st_in, num, br_out, br_in, tz_out, tz_in,
    hid_sem, q1_send, q1_recv, q2_send, q2_recv, o1_send, o1_recv, o2_send, o2_recv,
    ff_send, ff_recv, local_sems, c_send, c_recv, cf_send, cf_recv,
    rim_sem, st_send, st_recv, br_sem, tz_sem,
):
    dp, chip, core, tensor = (lax.axis_index(name) for name in ("dp", "chip", "core", "tensor"))
    own = hid_ref.shape[0]
    tokens = CORES * own
    model = hid_ref.shape[1]
    shard = wqkv_ref.shape[1]
    q_width = q_ref.shape[1]
    pairs = CORES * chips
    units = ff_ref.shape[2]
    other = 1 - core
    there = 1 - dp
    sibling = {"core": other}
    at_chip = [lax.rem(chip + step, chips) for step in range(1, chips)]
    behind = [lax.rem(chip + chips - step, chips) for step in range(1, chips)]
    greet(
        [sibling, {"tensor": 1 - tensor}]
        + [{"dp": there, "core": core}, {"dp": there, "core": other}]
        + [{"chip": to, "core": which} for to in at_chip for which in (core, other)]
        + [{"dp": there, "chip": to, "core": which} for to in at_chip for which in (core, other)]
    )

    def first(source, target, send, recv):
        rows = pl.ds(((dp * chips + chip) * CORES + core) * shard, shard)
        return [
            remote(source.at[other], target.at[rows], send.at[0], recv.at[0], core=other),
            remote(source.at[core], target.at[rows], send.at[1], recv.at[1], dp=there),
            remote(source.at[other], target.at[rows], send.at[2], recv.at[2], dp=there, core=other),
        ]

    def local(source, target, at):
        rows = pl.ds(((dp * chips + chip) * CORES + core) * shard, shard)
        return pltpu.make_async_copy(source.at[core], target.at[rows], local_sems.at[at])

    def second(target, send, recv, side):
        group_at = dp if side == 0 else there
        rows = pl.ds((group_at * chips + chip) * CORES * shard, CORES * shard)
        return [
            remote(target.at[rows], target.at[rows], send.at[side, at], recv.at[side, at], chip=to)
            for at, to in enumerate(at_chip)
        ]

    q_first = first(wqkv_ref, qkv_ref, q1_send, q1_recv)
    o_first = first(wo_ref, wof_ref, o1_send, o1_recv)
    q_local, o_local = local(wqkv_ref, qkv_ref, 0), local(wo_ref, wof_ref, 1)
    q_second = [second(qkv_ref, q2_send, q2_recv, side) for side in range(2)]
    o_second = [second(wof_ref, o2_send, o2_recv, side) for side in range(2)]
    hid_copy = remote(hid_ref, hid_sib, hid_sem.at[0], hid_sem.at[1], **sibling)
    q_local.start()
    hid_copy.start()
    for copy in q_first:
        copy.start()
    o_local.start()
    for copy in o_first:
        copy.start()

    ff_rows = pl.ds(((dp * chips + chip) * CORES + core) * shard, shard)
    ff_sources = (gate_ref, up_ref, down_ref)

    def ff_copy(which, step, side):
        to = lax.rem(chip * CORES + core + step, pairs)
        return remote(
            ff_sources[which].at[:, pl.ds(pl.multiple_of(to * units, units), units)],
            ff_ref.at[which, ff_rows],
            ff_send.at[which],
            ff_recv.at[which],
            dp=dp if side == 0 else there,
            chip=to // CORES,
            core=lax.rem(to, CORES),
        )

    def ff_local(which):
        return pltpu.make_async_copy(
            ff_sources[which].at[:, pl.ds(pl.multiple_of((chip * CORES + core) * units, units), units)],
            ff_ref.at[which, ff_rows],
            local_sems.at[2 + which],
        )

    def ff_start(which, side):
        def one(step, nothing):
            ff_copy(which, step, side).start()
            return nothing

        lax.fori_loop(1 - side, pairs, one, 0)

    c_copies = row_copies(chips, chip, cot_ref, call_ref, c_send, c_recv)
    c_forward = forward_copies(chips, chip, core, cot_ref, call_ref, cf_send, cf_recv)
    c_local = pltpu.make_async_copy(cot_ref, call_ref.at[0, pl.ds(0, own)], local_sems.at[5])

    def normalized(rows, gain):
        return (rows * lax.rsqrt(jnp.mean(rows * rows, axis=1, keepdims=True) + EPS) * gain).astype(BFLOAT)

    ff_start(0, 1)
    for which in range(3):
        ff_local(which).start()
    c_local.start()
    hidden = hid_ref[...].astype(FLOAT)
    normed_ref[pl.ds(pl.multiple_of(core * own, own), own)] = normalized(hidden, again_ref[...])
    q_first[0].wait_recv()
    q_local.wait()
    for copy in q_second[0]:
        copy.start()
    hid_copy.wait()
    normed_ref[pl.ds(pl.multiple_of(other * own, own), own)] = normalized(
        hid_sib[...].astype(FLOAT), again_ref[...]
    )
    low_ref[...] = dot(normed_ref[...], downs_ref[...]).astype(BFLOAT)
    q_first[1].wait_recv()
    q_first[2].wait_recv()
    for copy in q_second[1]:
        copy.start()
    o_first[0].wait_recv()
    o_local.wait()
    for copy in o_second[0]:
        copy.start()
    for side in range(2):
        for copy in q_second[side]:
            copy.wait_recv()
    ff_start(0, 0)
    ff_start(1, 1)

    pre = dot(normed_ref[...], qkv_ref[...]) + dot(low_ref[...], ups_ref[...])
    half = HEAD_SIZE // 2
    first_half = lax.rem(lanes((tokens, 128)), HEAD_SIZE) < half

    def rotated(block):
        turned = jnp.where(first_half, pltpu.roll(block, 128 - half, 1), pltpu.roll(block, half, 1))
        return (block * cos_ref[...] + turned * sin_ref[...]).astype(BFLOAT)

    for at in range(0, q_width, 128):
        q_ref[:, at : at + 128] = rotated(pre[:, at : at + 128])
    keys = rotated(pre[:, q_width : q_width + 128])
    values = pre[:, q_width + 128 :].astype(BFLOAT)
    rim_out[:, :128] = keys[tokens - SOFTMAX_KEYS :]
    rim_out[:, 128:] = values[tokens - SOFTMAX_KEYS :]
    rim_copy = remote(rim_out, rim_in, rim_sem.at[0], rim_sem.at[1], chip=lax.rem(chip + 1, chips))

    @pl.when(chip < chips - 1)
    def _():
        rim_copy.start()

    def tailed(rows):
        tail = jnp.where(lanes((rows.shape[0], 128 - HEAD_SIZE)) < 2, 1.0, 0.0).astype(BFLOAT)
        return jnp.concatenate([rows, tail], axis=1)

    gap = 128 - SOFTMAX_KEYS
    for head in range(kv_heads):
        cols = slice(head * HEAD_SIZE, (head + 1) * HEAD_SIZE)
        k_ref[head, 128:] = keys[:, cols]
        v_ref[head, 128:] = tailed(values[:, cols])
        k_ref[head, :gap] = jnp.zeros((gap, HEAD_SIZE), BFLOAT)
        v_ref[head, :gap] = tailed(jnp.zeros((gap, HEAD_SIZE), BFLOAT))

    @pl.when(chip == 0)
    def _():
        rim_in[...] = jnp.zeros(rim_in.shape, BFLOAT)

    @pl.when(chip > 0)
    def _():
        rim_copy.wait_recv()

    carry = carry_ref[...]
    for head in range(kv_heads):
        cols = slice(head * HEAD_SIZE, (head + 1) * HEAD_SIZE)
        k_ref[head, gap:128] = rim_in[:, cols]
        v_ref[head, gap:128] = tailed(rim_in[:, 128 + head * HEAD_SIZE : 128 + (head + 1) * HEAD_SIZE])
        vm[head] = (v_ref[head].astype(FLOAT) * carry).astype(BFLOAT)

    def views(at):
        heads = pl.ds(at * group, group)
        one = pl.ds(at, 1)
        wide = pl.ds(at * group * HEAD_SIZE, group * HEAD_SIZE)
        return heads, one, wide

    for at in range(kv_heads):
        heads, one, wide = views(at)
        phi_kernel(
            group, q_ref.at[:, wide], k_ref.at[one], vm.at[one], fq_ref.at[heads], fk_ref.at[heads],
            phi_q_ref.at[heads], phi_k_ref.at[heads], st_out.at[heads],
        )
    kept = HEAD_SIZE + 16
    st_copies = [
        remote(st_out.at[:, pl.ds(0, kept)], st_in.at[at], st_send.at[at], st_recv.at[at], chip=to)
        for at, to in enumerate(at_chip)
    ]
    for copy in st_copies:
        copy.start()
    o_first[1].wait_recv()
    o_first[2].wait_recv()
    for copy in o_second[1]:
        copy.start()
    c_forward[0].start()
    for copy in c_copies[0]:
        copy.start()
    ff_start(1, 0)
    for at in range(kv_heads):
        heads, one, wide = views(at)
        intra_kernel(
            group, q_ref.at[:, wide], k_ref.at[one], v_ref.at[one], phi_q_ref.at[heads],
            phi_k_ref.at[heads], seg_q_ref, seg_k_ref, num.at[heads],
        )
    total = jnp.zeros(st_in.shape[1:], FLOAT)
    for at, copy in enumerate(st_copies):
        copy.wait_recv()
        total = total + coef_ref[at] * st_in[at].astype(FLOAT)
    state_ref[:, :kept] = total.astype(BFLOAT)
    state_ref[:, kept:] = jnp.zeros((state_ref.shape[0], 128 - kept, 128), BFLOAT)
    for at in range(kv_heads):
        heads, one, wide = views(at)
        finish_kernel(
            group, num.at[heads], phi_q_ref.at[heads], state_ref.at[heads], cont_ref,
            att_ref.at[:, wide], den_ref.at[one],
        )

    for side in range(2):
        for copy in o_second[side]:
            copy.wait_recv()

    def branch(which, target):
        rows = att_ref[pl.ds(pl.multiple_of(which * own, own), own)]
        return product_t(rows, wof_ref[...]), dot(rows, odown_ref[...])

    wide_part, low_part = branch(other, None)
    br_out[:, :model] = wide_part.astype(BFLOAT)
    br_out[:, model:] = low_part.astype(BFLOAT)
    br_copy = remote(br_out, br_in, br_sem.at[0], br_sem.at[1], **sibling)
    br_copy.start()
    wide_part, low_part = branch(core, None)
    br_copy.wait_recv()
    tz_out[:, :model] = (wide_part + br_in[:, :model].astype(FLOAT)).astype(BFLOAT)
    tz_out[:, model:] = (low_part + br_in[:, model:].astype(FLOAT)).astype(BFLOAT)
    tz_copy = remote(tz_out, tz_in, tz_sem.at[0], tz_sem.at[1], tensor=1 - tensor)
    tz_copy.start()
    ff_start(2, 1)
    tz_copy.wait_recv()
    relay(c_copies)
    ff_start(2, 0)
    mid = (tz_out[:, model:].astype(FLOAT) + tz_in[:, model:].astype(FLOAT)).astype(BFLOAT)
    mid_ref[...] = mid
    residual = (
        hid_ref[...].astype(FLOAT)
        + (tz_out[:, :model].astype(FLOAT) + tz_in[:, :model].astype(FLOAT))
        + dot(mid, oup_ref[...])
    )
    res_ref[...] = residual
    xn[...] = normalized(residual, fgain_ref[...])
    hand_over(c_copies, c_forward)

    hid_done = [br_copy, tz_copy] + q_first + o_first + q_second[0] + q_second[1]
    for copy in hid_done + o_second[0] + o_second[1] + st_copies + c_copies[0] + c_copies[1]:
        copy.wait_send()

    @pl.when(chip < chips - 1)
    def _():
        rim_copy.wait_send()

    for copy in c_forward:
        copy.wait()
    c_local.wait()
    moved = (2 * pairs - 1) * shard
    for which in range(3):
        ff_local(which).wait()
        every = ff_ref.at[which, pl.ds(0, moved)]
        remote(every, every, ff_send.at[which], ff_recv.at[which], **sibling).wait()


def front(
    chips, kv_heads, group, tokens, near_args, far_args
):
    own, model = near_args[0].shape
    heads = kv_heads * group
    q_width = heads * HEAD_SIZE
    qkv_width = q_width + 2 * kv_heads * HEAD_SIZE
    extent = tokens + 128
    units = far_args[2].shape[1] // (chips * CORES)
    near = pl.BlockSpec(memory_space=pltpu.VMEM)
    far = pl.BlockSpec(memory_space=pl.ANY)
    kept = HEAD_SIZE + 16
    near_outs = [
        ((model, qkv_width), BFLOAT),
        ((model, q_width), BFLOAT),
        ((tokens, model), BFLOAT),
        ((tokens, 128), BFLOAT),
        ((own, 128), BFLOAT),
        ((own, model), FLOAT),
        ((tokens, q_width), BFLOAT),
        ((kv_heads, extent, HEAD_SIZE), BFLOAT),
        ((kv_heads, extent, 128), BFLOAT),
        ((heads, tokens, 128), BFLOAT),
        ((heads, extent, 128), BFLOAT),
        ((tokens, q_width), BFLOAT),
        ((kv_heads, tokens, 128), FLOAT),
        ((heads, 128, 128), BFLOAT),
        ((own, model), BFLOAT),
    ]
    far_outs = [
        ((3, model, units), BFLOAT),
        ((chips, tokens, model), BFLOAT),
    ]
    pair = dma_row(2)
    return pl.pallas_call(
        functools.partial(front_kernel, chips, kv_heads, group),
        in_specs=[near] * len(near_args) + [far] * len(far_args),
        out_specs=[near] * len(near_outs) + [far] * len(far_outs),
        out_shape=[jax.ShapeDtypeStruct(*out) for out in near_outs + far_outs],
        scratch_shapes=[
            pltpu.VMEM((own, model), BFLOAT),
            pltpu.VMEM((kv_heads, extent, 128), BFLOAT),
            pltpu.VMEM((SOFTMAX_KEYS, 256), BFLOAT),
            pltpu.VMEM((SOFTMAX_KEYS, 256), BFLOAT),
            pltpu.VMEM((heads, 128, 128), BFLOAT),
            pltpu.VMEM((chips - 1, heads, kept, 128), BFLOAT),
            pltpu.VMEM((heads, tokens, 128), FLOAT),
            pltpu.VMEM((own, model + 128), BFLOAT),
            pltpu.VMEM((own, model + 128), BFLOAT),
            pltpu.VMEM((own, model + 128), BFLOAT),
            pltpu.VMEM((own, model + 128), BFLOAT),
            pair,
            dma_row(3),
            dma_row(3),
            pltpu.SemaphoreType.DMA((2, chips - 1)),
            pltpu.SemaphoreType.DMA((2, chips - 1)),
            dma_row(3),
            dma_row(3),
            pltpu.SemaphoreType.DMA((2, chips - 1)),
            pltpu.SemaphoreType.DMA((2, chips - 1)),
            dma_row(3),
            dma_row(3),
            dma_row(7),
            dma_row(chips),
            dma_row(chips),
            dma_row(chips),
            dma_row(chips),
            pair,
            dma_row(chips - 1),
            dma_row(chips - 1),
            pair,
            pair,
        ],
        compiler_params=pltpu.CompilerParams(
            vmem_limit_bytes=60 * 1024 * 1024, collective_id=2, has_side_effects=True
        ),
        cost_estimate=pl.CostEstimate(
            flops=int(1e10), bytes_accessed=int(1e8), transcendentals=0
        ),
    )(*near_args, *far_args)


def rear_kernel(
    chips, kv_heads, group, rank,
    gnf_ref, res_ref, cot_ref, hid_ref, again_ref, fgain_ref, wof_ref, odown_ref, oup_ref, mid_ref,
    att_ref, den_ref, q_ref, k_ref, v_ref, phi_q_ref, phi_k_ref, fq_ref, fk_ref, state_ref,
    seg_q_ref, seg_k_ref, cont_ref, carry_ref, coef_ref, cos_ref, sin_ref,
    normed_ref, low_ref, qkv_ref, ups_ref, downs_ref,
    out_ref, ffg_ref,
    block_ref, igrad_ref, qkv_own, qkv_sib, o_own, o_sib,
    tab_own, early_own, ups_own, late_own, tab_sib, early_sib, ups_sib, late_sib,
    ffin_ref, oin_ref,
    db, dq, dn, ds_out, ds_in, gstate, dk, dv, dphi_q, dphi_k, gq, gk, dres,
    rim_out, rim_in, gp, br_out, br_in, tz_in,
    qg, q_in, q_dp_out, q_dp_in, q_core, og, o_in, o_dp_out, o_dp_in, o_core,
    tab_slots, early_slots, ups_slots, late_slots,
    tab_dp, early_dp, ups_dp, late_dp,
    db_sem, ds_send, ds_recv, rim_sem, br_sem, tz_sem, oz_sem, o_load, os_send, os_recv,
    q_send, q_recv, q_dp_sem, q_core_sem, o_send, o_recv, o_dp_sem, o_core_sem,
    small_send, small_recv, small_dp, small_core,
    ff_send, ff_recv, local_sems,
):
    dp, chip, core, tensor = (lax.axis_index(name) for name in ("dp", "chip", "core", "tensor"))
    own, model = gnf_ref.shape
    tokens = CORES * own
    q_width = q_ref.shape[1]
    pairs = CORES * chips
    shard = model // (2 * pairs)
    units = ffg_ref.shape[2]
    other = 1 - core
    there = 1 - dp
    sibling = {"core": other}
    at_chip = [lax.rem(chip + step, chips) for step in range(1, chips)]
    greet(
        [sibling, {"tensor": 1 - tensor}]
        + [{"dp": there, "core": core}, {"dp": there, "core": other}]
        + [{"chip": to, "core": which} for to in at_chip for which in (core, other)]
        + [{"dp": there, "chip": to, "core": which} for to in at_chip for which in (core, other)]
    )
    mine = pl.ds(pl.multiple_of(core * own, own), own)
    theirs = pl.ds(pl.multiple_of(other * own, own), own)

    def ff_start(which, side):
        def one(step, nothing):
            to = lax.rem(chip * CORES + core + step, pairs)
            group_to = dp if side == 0 else there
            remote(
                ffg_ref.at[which, pl.ds((group_to * pairs + to) * shard, shard)],
                ffin_ref.at[which, dp, :, pl.ds(pl.multiple_of((chip * CORES + core) * units, units), units)],
                ff_send.at[which, side],
                ff_recv.at[which, side],
                dp=group_to,
                chip=to // CORES,
                core=lax.rem(to, CORES),
            ).start()
            return nothing

        lax.fori_loop(1 - side, pairs, one, 0)

    def ff_local(which):
        at = chip * CORES + core
        return pltpu.make_async_copy(
            ffg_ref.at[which, pl.ds((dp * pairs + at) * shard, shard)],
            ffin_ref.at[which, dp, :, pl.ds(pl.multiple_of(at * units, units), units)],
            local_sems.at[which],
        )

    os_copies = [
        remote(out_ref.at[at + 1], oin_ref.at[at], os_send.at[at], os_recv.at[at], chip=to)
        for at, to in enumerate(at_chip)
    ]

    def norm_back_rows(inputs, gain, grad):
        scale = lax.rsqrt(jnp.mean(inputs * inputs, axis=1, keepdims=True) + EPS)
        weighted = grad * gain
        back = scale * weighted - inputs * (
            scale * scale * scale * jnp.mean(weighted * inputs, axis=1, keepdims=True)
        )
        return back, jnp.sum(grad * inputs * scale, axis=0, keepdims=True)

    slots = (tab_slots, early_slots, ups_slots, late_slots)
    dp_bufs = (tab_dp, early_dp, ups_dp, late_dp)
    owns = (tab_own, early_own, ups_own, late_own)
    sibs = (tab_sib, early_sib, ups_sib, late_sib)

    def small_copies(which):
        return [
            remote(
                slots[which].at[chip], slots[which].at[chip],
                small_send.at[which, at], small_recv.at[which, at], chip=to,
            )
            for at, to in enumerate(at_chip)
        ]

    def small_start(which, value):
        slots[which][chip] = value.astype(BFLOAT)
        for copy in small_copies(which):
            copy.start()

    def small_across(which):
        return remote(
            dp_bufs[which].at[0], dp_bufs[which].at[1],
            small_dp.at[which, 0], small_dp.at[which, 1], dp=there,
        )

    def small_over(which):
        return remote(owns[which], sibs[which], small_core.at[which, 0], small_core.at[which, 1], **sibling)

    def small_middle(which):
        for copy in small_copies(which):
            copy.wait()
        total = slots[which][0].astype(FLOAT)
        for at in range(1, chips):
            total = total + slots[which][at].astype(FLOAT)
        dp_bufs[which][0] = total.astype(BFLOAT)
        small_across(which).start()

    def small_end(which):
        small_across(which).wait()
        owns[which][...] = dp_bufs[which][0].astype(FLOAT) + dp_bufs[which][1].astype(FLOAT)
        small_over(which).start()

    def grad_copies(source, target, send, recv):
        return [
            remote(
                source.at[pl.ds(((dp if side == 0 else there) * chips + to) * CORES * shard, CORES * shard)],
                target.at[at, side],
                send.at[side, at],
                recv.at[side, at],
                chip=to,
            )
            for at, to in enumerate(at_chip)
            for side in range(2)
        ]

    q_copies = grad_copies(qg, q_in, q_send, q_recv)
    o_copies = grad_copies(og, o_in, o_send, o_recv)
    q_across = remote(q_dp_out, q_dp_in, q_dp_sem.at[0], q_dp_sem.at[1], dp=there)
    o_across = remote(o_dp_out, o_dp_in, o_dp_sem.at[0], o_dp_sem.at[1], dp=there)
    q_over = remote(q_core, qkv_sib, q_core_sem.at[0], q_core_sem.at[1], **sibling)
    o_over = remote(o_core, o_sib, o_core_sem.at[0], o_core_sem.at[1], **sibling)

    def chip_sum(source, target, side):
        group_at = dp if side == 0 else there
        total = source[pl.ds((group_at * chips + chip) * CORES * shard, CORES * shard)].astype(FLOAT)
        for at in range(chips - 1):
            total = total + target[at, side].astype(FLOAT)
        return total

    def grads_middle(copies, source, target, dp_out, across):
        for copy in copies:
            copy.wait_recv()
        dp_out[...] = chip_sum(source, target, 1).astype(BFLOAT)
        across.start()

    def grads_end(source, target, dp_in, across, result, core_out, over):
        across.wait()
        total = chip_sum(source, target, 0) + dp_in[...].astype(FLOAT)
        upper, lower = total[shard:], total[:shard]
        result[...] = jnp.where(core == 0, lower, upper)
        core_out[...] = jnp.where(core == 0, upper, lower).astype(BFLOAT)
        over.start()

    back_rows, gain_row = norm_back_rows(res_ref[...], fgain_ref[...], gnf_ref[...])
    grad_residual = cot_ref[...].astype(FLOAT) + back_rows
    dres[...] = grad_residual
    db[mine] = grad_residual.astype(BFLOAT)
    db_copy = remote(db.at[mine], db.at[mine], db_sem.at[0], db_sem.at[1], **sibling)
    db_copy.start()
    ff_start(0, 1)
    os_copies[0].start()
    for which in range(3):
        ff_local(which).start()
    up_rows = t_product(mid_ref[...], db[mine])[:rank]
    filler = jnp.zeros((16 - 1 - rank, model), FLOAT)
    early_rows = jnp.concatenate([up_rows, gain_row, filler], axis=0)
    db_copy.wait_recv()
    dmid = product_t(db[...], oup_ref[...]).astype(BFLOAT)
    dq[...] = dot(db[...], wof_ref[...]) + product_t(dmid, odown_ref[...])

    def views(at):
        return (
            pl.ds(at * group, group),
            pl.ds(at, 1),
            pl.ds(at * group * HEAD_SIZE, group * HEAD_SIZE),
        )

    for at in range(kv_heads):
        heads, one, wide = views(at)
        grad_numer_kernel(
            group, dq.at[:, wide], att_ref.at[:, wide], den_ref.at[one], phi_q_ref.at[heads], cont_ref,
            dn.at[heads], ds_out.at[heads],
        )
    kept = HEAD_SIZE + 16
    ds_copies = [
        remote(ds_out.at[:, pl.ds(0, kept)], ds_in.at[at], ds_send.at[at], ds_recv.at[at], chip=to)
        for at, to in enumerate([lax.rem(chip + chips - step, chips) for step in range(1, chips)])
    ]
    for copy in ds_copies:
        copy.start()
    small_start(1, early_rows)
    ff_start(0, 0)
    og[...] = t_product(db[...], att_ref[...]).astype(BFLOAT)
    down_rows = t_product(dmid, att_ref[...])[:rank]
    for at in range(kv_heads):
        heads, one, wide = views(at)
        intra_back_kernel(
            group, q_ref.at[:, wide], k_ref.at[one], v_ref.at[one], phi_q_ref.at[heads],
            phi_k_ref.at[heads], dn.at[heads], seg_q_ref, seg_k_ref,
            dq.at[:, wide], dk.at[one], dv.at[one], dphi_q.at[heads], dphi_k.at[heads],
        )
    total = jnp.zeros(ds_in.shape[1:], FLOAT)
    for at, copy in enumerate(ds_copies):
        copy.wait_recv()
        total = total + coef_ref[at] * ds_in[at].astype(FLOAT)
    gstate[:, :kept] = total.astype(BFLOAT)
    gstate[:, kept:] = jnp.zeros((gstate.shape[0], 128 - kept, 128), BFLOAT)
    for at in range(kv_heads):
        heads, one, wide = views(at)
        features_back_kernel(
            group, q_ref.at[:, wide], k_ref.at[one], v_ref.at[one], phi_q_ref.at[heads],
            phi_k_ref.at[heads], dn.at[heads], fq_ref.at[heads], fk_ref.at[heads],
            state_ref.at[heads], gstate.at[heads], cont_ref, carry_ref,
            dq.at[:, wide], dk.at[one], dv.at[one], dphi_q.at[heads], dphi_k.at[heads],
            dq.at[:, wide], dk.at[one], dv.at[one], gq.at[heads], gk.at[heads],
        )

    gap = 128 - SOFTMAX_KEYS

    def joined(rows):
        return jnp.concatenate(
            [dk[head, rows] for head in range(kv_heads)]
            + [dv[head, rows, :HEAD_SIZE] for head in range(kv_heads)],
            axis=1,
        )

    rim_out[...] = joined(slice(gap, 128))
    rim_copy = remote(rim_out, rim_in, rim_sem.at[0], rim_sem.at[1], chip=lax.rem(chip + chips - 1, chips))

    @pl.when(chip > 0)
    def _():
        rim_copy.start()

    tables = []
    for head in range(kv_heads * group):
        pieces = [table[head, :, :FEATURE_HALF] - table[head, :, FEATURE_HALF:] for table in (gq, gk)]
        tables.append(jnp.concatenate(pieces, axis=1))
    small_start(0, jnp.concatenate(tables, axis=0))
    for copy in o_copies:
        copy.start()
    half = HEAD_SIZE // 2
    first_half = lax.rem(lanes((tokens, 128)), HEAD_SIZE) < half

    def unrotated(block):
        turned = jnp.where(first_half, pltpu.roll(block, 128 - half, 1), pltpu.roll(block, half, 1))
        return (block * cos_ref[...] - turned * sin_ref[...]).astype(BFLOAT)

    for at in range(0, q_width, 128):
        gp[:, at : at + 128] = unrotated(dq[:, at : at + 128])

    @pl.when(chip == chips - 1)
    def _():
        rim_in[...] = jnp.zeros(rim_in.shape, FLOAT)

    @pl.when(chip < chips - 1)
    def _():
        rim_copy.wait_recv()

    kv = joined(slice(128, 128 + tokens))
    kv = jnp.concatenate(
        [kv[: tokens - SOFTMAX_KEYS], kv[tokens - SOFTMAX_KEYS :] + rim_in[...]], axis=0
    )
    gp[:, q_width : q_width + 128] = unrotated(kv[:, :128])
    gp[:, q_width + 128 :] = kv[:, 128:].astype(BFLOAT)

    def partial(rows):
        grads = gp[rows]
        return product_t(grads, qkv_ref[...]), product_t(grads, ups_ref[...])

    wide_part, low_part = partial(theirs)
    br_out[:, :model] = wide_part.astype(BFLOAT)
    br_out[:, model:] = low_part.astype(BFLOAT)
    br_copy = remote(br_out, br_in, br_sem.at[0], br_sem.at[1], **sibling)
    br_copy.start()
    wide_part, low_part = partial(mine)
    br_copy.wait()
    tz_out = br_out
    tz_out[:, :model] = (wide_part + br_in[:, :model].astype(FLOAT)).astype(BFLOAT)
    tz_out[:, model:] = (low_part + br_in[:, model:].astype(FLOAT)).astype(BFLOAT)
    tz_copy = remote(tz_out, tz_in, tz_sem.at[0], tz_sem.at[1], tensor=1 - tensor)
    tz_copy.start()
    ff_start(1, 1)
    qg[...] = t_product(normed_ref[...], gp[...]).astype(BFLOAT)
    for copy in q_copies:
        copy.start()
    ups_rows = t_product(low_ref[...], gp[...])[: 3 * rank]
    wide_down = jnp.concatenate(
        [down_rows, jnp.zeros((rank, gp.shape[1] - q_width), FLOAT)], axis=1
    )
    small_start(2, jnp.concatenate([ups_rows, wide_down], axis=0))
    tz_copy.wait_recv()
    low = (tz_out[:, model:].astype(FLOAT) + tz_in[:, model:].astype(FLOAT)).astype(BFLOAT)
    grad_normed = (
        tz_out[:, :model].astype(FLOAT) + tz_in[:, :model].astype(FLOAT)
    ) + product_t(low, downs_ref[...])
    low_rows = t_product(low, normed_ref[mine])[: 3 * rank]
    back_rows, gain_row = norm_back_rows(hid_ref[...].astype(FLOAT), again_ref[...], grad_normed)
    igrad_ref[...] = (dres[...] + back_rows).astype(BFLOAT)
    filler = jnp.zeros((rank - 1, model), FLOAT)
    small_start(3, jnp.concatenate([low_rows, gain_row, filler], axis=0))
    for copy in os_copies[1:]:
        copy.start()
    ff_start(1, 0)
    ff_start(2, 0)
    grads_middle(o_copies, og, o_in, o_dp_out, o_across)
    ff_start(2, 1)
    small_middle(1)
    small_middle(0)
    small_middle(2)
    grads_middle(q_copies, qg, q_in, q_dp_out, q_across)
    small_middle(3)

    os_buf = tz_in.at[:, pl.ds(0, model)]
    load = pltpu.make_async_copy(out_ref.at[0], os_buf, o_load.at[0])
    load.start()
    load.wait()
    dres[...] = os_buf[...].astype(FLOAT)
    for at in range(chips - 1):
        os_copies[at].wait_recv()
        load = pltpu.make_async_copy(oin_ref.at[at], os_buf, o_load.at[0])
        load.start()
        load.wait()
        dres[...] += os_buf[...].astype(FLOAT)
    tz_copy.wait_send()
    oz_out, oz_in = (ref.at[:, pl.ds(0, model)] for ref in (br_out, br_in))
    oz_out[...] = dres[...].astype(BFLOAT)
    oz_copy = remote(oz_out, oz_in, oz_sem.at[0], oz_sem.at[1], tensor=1 - tensor)
    oz_copy.start()
    grads_end(og, o_in, o_dp_in, o_across, o_own, o_core, o_over)
    for which in range(3):
        small_end(which)
    oz_copy.wait()
    block_ref[...] = (
        res_ref[...] + (oz_out[...].astype(FLOAT) + oz_in[...].astype(FLOAT))
    ).astype(BFLOAT)
    grads_end(qg, q_in, q_dp_in, q_across, qkv_own, q_core, q_over)
    small_end(3)

    for copy in [db_copy] + ds_copies + os_copies + q_copies + o_copies:
        copy.wait_send()

    @pl.when(chip > 0)
    def _():
        rim_copy.wait_send()

    for which in range(4):
        small_over(which).wait()
    q_over.wait()
    o_over.wait()
    for which in range(3):
        ff_local(which).wait()
        for side in range(2):
            count = pairs - 1 + side
            group_from = dp if side == 0 else there
            sent = ffg_ref.at[which, pl.ds(0, count * shard)]
            came = ffin_ref.at[which, group_from, :, pl.ds(0, count * units)]
            remote(sent, sent, ff_send.at[which, side], ff_recv.at[which, side], **sibling).wait_send()
            remote(came, came, ff_send.at[which, side], ff_recv.at[which, side], **sibling).wait_recv()


def rear(chips, kv_heads, group, rank, near_args, far_args):
    own, model = near_args[0].shape
    tokens = CORES * own
    heads = kv_heads * group
    q_width = heads * HEAD_SIZE
    qkv_width = q_width + 2 * kv_heads * HEAD_SIZE
    extent = tokens + 128
    pairs = chips * CORES
    shard = model // (2 * pairs)
    units = far_args[1].shape[2]
    near = pl.BlockSpec(memory_space=pltpu.VMEM)
    far = pl.BlockSpec(memory_space=pl.ANY)
    kept = HEAD_SIZE + 16
    smalls = [
        (heads * HEAD_SIZE, 128),
        (16, model),
        (4 * rank, qkv_width),
        (4 * rank, model),
    ]
    near_outs = [
        ((own, model), BFLOAT),
        ((own, model), BFLOAT),
        ((shard, qkv_width), FLOAT),
        ((shard, qkv_width), BFLOAT),
        ((shard, q_width), FLOAT),
        ((shard, q_width), BFLOAT),
    ]
    near_outs += [(shape, FLOAT) for shape in smalls] * 2
    far_outs = [
        ((3, 2, shard, pairs * units), BFLOAT),
        ((chips - 1, own, model), BFLOAT),
    ]
    pair = dma_row(2)
    step_pair = pltpu.SemaphoreType.DMA((2, chips - 1))

    def grads(width):
        return [
            pltpu.VMEM((model, width), BFLOAT),
            pltpu.VMEM((chips - 1, 2, CORES * shard, width), BFLOAT),
            pltpu.VMEM((CORES * shard, width), BFLOAT),
            pltpu.VMEM((CORES * shard, width), BFLOAT),
            pltpu.VMEM((shard, width), BFLOAT),
        ]

    wide = pltpu.VMEM((own, model + 128), BFLOAT)
    return pl.pallas_call(
        functools.partial(rear_kernel, chips, kv_heads, group, rank),
        in_specs=[near] * len(near_args) + [far] * len(far_args),
        out_specs=[near] * len(near_outs) + [far] * len(far_outs),
        out_shape=[jax.ShapeDtypeStruct(*out) for out in near_outs + far_outs],
        scratch_shapes=[
            pltpu.VMEM((tokens, model), BFLOAT),
            pltpu.VMEM((tokens, q_width), FLOAT),
            pltpu.VMEM((heads, tokens, 128), BFLOAT),
            pltpu.VMEM((heads, 128, 128), BFLOAT),
            pltpu.VMEM((chips - 1, heads, kept, 128), BFLOAT),
            pltpu.VMEM((heads, 128, 128), BFLOAT),
            pltpu.VMEM((kv_heads, extent, HEAD_SIZE), FLOAT),
            pltpu.VMEM((kv_heads, extent, 128), FLOAT),
            pltpu.VMEM((heads, tokens, 128), FLOAT),
            pltpu.VMEM((heads, extent, 128), FLOAT),
            pltpu.VMEM((heads, HEAD_SIZE, 128), FLOAT),
            pltpu.VMEM((heads, HEAD_SIZE, 128), FLOAT),
            pltpu.VMEM((own, model), FLOAT),
            pltpu.VMEM((SOFTMAX_KEYS, 256), FLOAT),
            pltpu.VMEM((SOFTMAX_KEYS, 256), FLOAT),
            pltpu.VMEM((tokens, qkv_width), BFLOAT),
            wide,
            wide,
            wide,
        ]
        + grads(qkv_width)
        + grads(q_width)
        + [pltpu.VMEM((chips,) + shape, BFLOAT) for shape in smalls]
        + [pltpu.VMEM((2,) + shape, BFLOAT) for shape in smalls]
        + [
            pair,
            dma_row(chips - 1),
            dma_row(chips - 1),
            pair,
            pair,
            pair,
            pair,
            dma_row(1),
            dma_row(chips - 1),
            dma_row(chips - 1),
            step_pair,
            step_pair,
            pair,
            pair,
            step_pair,
            step_pair,
            pair,
            pair,
            pltpu.SemaphoreType.DMA((4, chips - 1)),
            pltpu.SemaphoreType.DMA((4, chips - 1)),
            pltpu.SemaphoreType.DMA((4, 2)),
            pltpu.SemaphoreType.DMA((4, 2)),
            pltpu.SemaphoreType.DMA((3, 2)),
            pltpu.SemaphoreType.DMA((3, 2)),
            dma_row(3),
        ],
        compiler_params=pltpu.CompilerParams(
            vmem_limit_bytes=63 * 1024 * 1024, collective_id=3, has_side_effects=True
        ),
        cost_estimate=pl.CostEstimate(
            flops=int(4e10), bytes_accessed=int(1e8), transcendentals=0
        ),
    )(*near_args, *far_args)


def carry_coefs(lengths, tokens):
    chips = lax.axis_size("chip")
    me = lax.axis_index("chip")
    steps = jnp.arange(1, chips, dtype=jnp.int32)
    behind, ahead = lax.rem(me + chips - steps, chips), lax.rem(me + steps, chips)
    places = jnp.stack(
        [behind * tokens + tokens - 1, ahead * tokens - 1, 0 * steps + me * tokens - 1]
        + [0 * steps + me * tokens + tokens - 1]
    )
    segment = locate(places, lengths)[0]
    forward = (behind < me) & (segment[0] == segment[2])
    backward = (ahead > me) & (segment[1] == segment[3])
    return [
        jnp.broadcast_to(row.astype(FLOAT)[:, None, None], (chips - 1, 1, 128))
        for row in (forward, backward)
    ]


def on_device(
    hidden_in,
    doc_lengths,
    attention_gain,
    query_weight,
    key_projection,
    value_projection,
    output_weight,
    query_down,
    query_up,
    key_down,
    key_adapter_up,
    value_down,
    value_adapter_up,
    output_down,
    output_up,
    query_feature_maps,
    key_feature_maps,
    feedforward_gain,
    gate_weight,
    up_weight,
    down_weight,
    block_cotangent,
):
    own_rows, model = hidden_in.shape
    tokens = own_rows * CORES
    core = lax.axis_index("core")
    chip = lax.axis_index("chip")
    chips = lax.axis_size("chip")
    heads = query_feature_maps.shape[0] // CORES
    kv_heads = key_projection.shape[1] // HEAD_SIZE // CORES
    group = heads // kv_heads
    q_width = heads * HEAD_SIZE
    kv_width = kv_heads * HEAD_SIZE
    rank = query_down.shape[1]

    def own_cols(value, width, which):
        return lax.dynamic_slice_in_dim(value, which * width, width, 1)

    def own_heads(value, count, which):
        return lax.dynamic_slice_in_dim(value, which * count, count, 0)

    wqkv = jnp.stack(
        [
            jnp.concatenate(
                [
                    own_cols(query_weight, q_width, which),
                    own_cols(key_projection, kv_width, which),
                    own_cols(value_projection, kv_width, which),
                ],
                axis=1,
            )
            for which in range(CORES)
        ]
    )
    wout = output_weight.reshape(CORES, q_width, -1).transpose(0, 2, 1)
    qkv_width = q_width + 2 * kv_width

    first_row = chip * tokens
    lengths = doc_lengths[0]
    gap = 128 - SOFTMAX_KEYS
    spots = jnp.arange(tokens + 128, dtype=jnp.int32)
    seg_ext, pos_ext = locate(first_row + spots - 128, lengths)
    seg_ext = jnp.where(spots < gap, -2, seg_ext)
    seg_rows, pos_rows = seg_ext[128:], pos_ext[128:]
    seg_first = locate(first_row - 1, lengths)[0]
    seg_last = locate(first_row + tokens - 1, lengths)[0]
    continuing = (seg_rows == seg_first).astype(FLOAT)[:, None]
    carry = ((jnp.arange(tokens + 128) < tokens + gap) & (seg_ext == seg_last)).astype(FLOAT)[:, None]
    seg_column, seg_line = seg_rows[:, None], seg_ext[None, :]
    forward_coefs, backward_coefs = carry_coefs(lengths, tokens)
    wide_cosine, wide_sine = rotation(pos_rows, HEAD_SIZE)
    query_table = own_heads(query_feature_maps, heads, core)
    key_table = own_heads(key_feature_maps, heads, core)
    query_table = jnp.concatenate([query_table, -query_table], axis=2)
    key_table = jnp.concatenate([key_table, -key_table], axis=2)
    downs = jnp.concatenate([query_down, key_down, value_down], axis=1)
    own_query_up = own_cols(query_up, q_width, core)
    own_key_up = own_cols(key_adapter_up, kv_width, core)
    own_value_up = own_cols(value_adapter_up, kv_width, core)
    own_output_down = own_heads(output_down, q_width, core)
    pad = 128 - 3 * rank
    ups = jnp.concatenate(
        [
            jnp.pad(own_query_up, ((0, 0), (0, 2 * kv_width))),
            jnp.pad(own_key_up, ((0, 0), (q_width, kv_width))),
            jnp.pad(own_value_up, ((0, 0), (q_width + kv_width, 0))),
            jnp.zeros((pad, qkv_width), BFLOAT),
        ],
        axis=0,
    )
    extent = tokens + 128
    wide_downs = jnp.pad(downs, ((0, 0), (0, pad)))
    wide_output_down = jnp.pad(own_output_down, ((0, 0), (0, 128 - rank)))
    wide_output_up = jnp.pad(output_up, ((0, 128 - rank), (0, 0)))
    (
        full_qkv, full_out, normed, low_rank, low_mid, residual, queries, key_ext, value_ext,
        phi_q, phi_k, attended, denominator, state, normed_ff, full_ff, cotangents,
    ) = front(
        chips,
        kv_heads,
        group,
        tokens,
        [
            hidden_in,
            attention_gain[None],
            feedforward_gain[None],
            wide_downs,
            ups,
            wide_cosine,
            wide_sine,
            query_table,
            key_table,
            seg_column,
            seg_line,
            continuing,
            carry,
            forward_coefs,
            wide_output_down,
            wide_output_up,
        ],
        [wqkv, wout, gate_weight, up_weight, down_weight.T, block_cotangent],
    )
    grad_normed_ff, out_sums, ff_grads, _, _ = feed(normed_ff, cotangents, full_ff)
    rear_outs = rear(
        chips,
        kv_heads,
        group,
        rank,
        [
            grad_normed_ff,
            residual,
            block_cotangent,
            hidden_in,
            attention_gain[None],
            feedforward_gain[None],
            full_out,
            wide_output_down[:, :16],
            wide_output_up[:16],
            low_mid,
            attended,
            denominator,
            queries,
            key_ext,
            value_ext,
            phi_q,
            phi_k,
            query_table,
            key_table,
            state,
            seg_column,
            seg_line,
            continuing,
            carry,
            backward_coefs,
            wide_cosine,
            wide_sine,
            normed,
            low_rank,
            full_qkv,
            ups,
            wide_downs,
        ],
        [out_sums, ff_grads],
    )
    block_output, input_grad, qkv_keep, qkv_other, out_keep, out_other = rear_outs[:6]
    own_small, sib_small = rear_outs[6:10], rear_outs[10:14]
    qkv_other, out_other = qkv_other.astype(FLOAT), out_other.astype(FLOAT)

    def by_core(dim, mine, other):
        return ordered(core, mine, other, dim)

    at_key, at_value = q_width, q_width + kv_width
    query_shard = by_core(1, qkv_keep[:, :at_key], qkv_other[:, :at_key])
    key_shard = by_core(1, qkv_keep[:, at_key:at_value], qkv_other[:, at_key:at_value])
    value_shard = by_core(1, qkv_keep[:, at_value:], qkv_other[:, at_value:])
    output_shard = by_core(1, out_keep, out_other).T
    ff_both = rear_outs[14]
    ff_shards = [ff_both[at, 0].astype(FLOAT) + ff_both[at, 1].astype(FLOAT) for at in range(3)]

    tables = by_core(0, own_small[0], sib_small[0]).reshape(CORES * heads, HEAD_SIZE, 128)
    early = own_small[1] + sib_small[1]
    late = own_small[3] + sib_small[3]
    ups_mine, ups_other = own_small[2], sib_small[2]

    def ups_part(row, start, stop):
        rows = slice(row * rank, (row + 1) * rank)
        return by_core(1, ups_mine[rows, start:stop], ups_other[rows, start:stop])

    downs_total = late[: 3 * rank].T
    return (
        block_output,
        input_grad,
        late[3 * rank],
        query_shard,
        key_shard,
        value_shard,
        output_shard,
        downs_total[:, :rank],
        ups_part(0, 0, at_key),
        downs_total[:, rank : 2 * rank],
        ups_part(1, at_key, at_value),
        downs_total[:, 2 * rank :],
        ups_part(2, at_value, qkv_width),
        ups_part(3, 0, at_key).T,
        early[:rank],
        tables[:, :, :FEATURE_HALF],
        tables[:, :, FEATURE_HALF:],
        early[rank],
        ff_shards[0],
        ff_shards[1],
        ff_shards[2].T,
    )


def solution(mesh):
    dp, seq, tensor = (mesh.shape[name] for name in ("dp", "seq", "tensor"))
    split = Mesh(
        mesh.devices.reshape(dp, seq // CORES, CORES, tensor), ("dp", "chip", "core", "tensor")
    )
    tok = ("dp", "chip", "core")
    in_specs = (
        P(tok, None),
        P("dp", None),
        P(),
        P(tok, "tensor"),
        P(tok, "tensor"),
        P(tok, "tensor"),
        P("tensor", tok),
        P(),
        P(None, "tensor"),
        P(),
        P(None, "tensor"),
        P(),
        P(None, "tensor"),
        P("tensor", None),
        P(),
        P("tensor", None, None),
        P("tensor", None, None),
        P(),
        P(tok, "tensor"),
        P(tok, "tensor"),
        P("tensor", tok),
        P(tok, None),
    )
    out_specs = (
        P(tok, None),
        P(tok, None),
        P(),
        P(tok, "tensor"),
        P(tok, "tensor"),
        P(tok, "tensor"),
        P("tensor", tok),
        P(),
        P(None, "tensor"),
        P(),
        P(None, "tensor"),
        P(),
        P(None, "tensor"),
        P("tensor", None),
        P(),
        P("tensor", None, None),
        P("tensor", None, None),
        P(),
        P(tok, "tensor"),
        P(tok, "tensor"),
        P("tensor", tok),
    )
    return jax.shard_map(
        on_device, mesh=split, in_specs=in_specs, out_specs=out_specs, check_vma=False
    )
```
